32 devices in a mesh: batch: 4 (over y, x), wide: 8 (over z, core).
Axes of the slice: x: 2, y: 2, z: 4, core: 2. Of those that a mesh axis runs over, the one named last changes fastest.
Arguments:
- block_in: bfloat16 [16, 512, 384], P('batch', 'wide'), may hold values from -6 to 6
- lead_embed: bfloat16 [16, 384], P('batch'), may hold values from -6 to 6
- lengths: int32 [16], P('batch'), may hold values from 128 to 512, as said below
- w_ada: bfloat16 [384, 2304], replicated, may hold values from -0.3125 to 0.3125
- b_ada: bfloat16 [2304], replicated, may hold values from -3 to 3
- w_qkv: bfloat16 [384, 1152], replicated, may hold values from -0.3125 to 0.3125
- w_proj: bfloat16 [384, 384], replicated, may hold values from -1.25 to 1.25
- w_fc1: bfloat16 [384, 1536], replicated, may hold values from -0.3125 to 0.3125
- w_fc2: bfloat16 [1536, 384], replicated, may hold values from -0.15625 to 0.15625
- cotangent: bfloat16 [16, 512, 384], P('batch', 'wide'), may hold values from -6 to 6
Outputs:
- block_out: float32 [16, 512, 384], P('batch', 'wide')
- input_grad: float32 [16, 512, 384], P('batch', 'wide')
- ada_grad: float32 [384, 2304], replicated
- bias_grad: float32 [2304], replicated
- qkv_grad: float32 [384, 1152], replicated
- proj_grad: float32 [384, 384], replicated
- fc1_grad: float32 [384, 1536], replicated
- fc2_grad: float32 [1536, 384], replicated
The draws below stay inside these ranges and needn't reach their ends.
Inputs may be any that keep to these rules, and one draw needn't show every extreme that they name: `lengths`: each batch group of 4 items has max(1, 0) items of exactly 512 patches, which ones drawn at random; the others have 512 // 4 to 384.
All inputs are finite; a program needn't handle non-finite values.
Results may differ from the reference program's by a relative error of at most 0.012.
The reference program's roundings to bfloat16 on the way count: a program that leaves them out, or rounds other values in their place, can miss the bound.
Values may be sent and summed in bfloat16 or wider, within the bound.
A program may use at most 512 MiB of HBM per device.

```python
import jax
import jax.numpy as jnp
from jax import lax

HEADS = 6
HEAD_DIM = 64
FF = 1536
D = 384
SLOT = 512
ITEMS = 4
ALL_ITEMS = 16


def draw_lengths(key, part):
    key = jax.random.fold_in(key, 11)
    groups = ALL_ITEMS // ITEMS
    long_count = max(1, 3 * ITEMS // 16)
    order_key = jax.random.fold_in(key, 1)
    short_key = jax.random.fold_in(key, 2)
    ranks = jax.vmap(lambda sub_key: jax.random.permutation(sub_key, ITEMS))(jax.random.split(order_key, groups))
    shorter = jax.random.randint(short_key, (groups, ITEMS), SLOT // 4, 3 * SLOT // 4 + 1)
    result = jnp.where(ranks < long_count, SLOT, shorter)
    return result.reshape(ALL_ITEMS).astype(jnp.int32)


def block_levels(rng, dims, cuts, low, top_value):
    def one(position, parts):
        heights = jax.random.uniform(jax.random.fold_in(jax.random.fold_in(rng, 6), position), (parts,), jnp.float32, low / len(cuts), top_value / len(cuts))
        return jnp.repeat(jnp.exp(heights), dims[position] // parts).reshape((-1,) + (1,) * (len(dims) - position - 1))

    loudness = one(*cuts[0])
    for cut in cuts[1:]:
        loudness = loudness * one(*cut)
    return loudness


def gaussian(own_key, extent, scale, reach, shards=(), kind=jnp.bfloat16):
    entries = scale * jax.random.normal(own_key, extent, jnp.float32)
    if shards:
        entries = entries * block_levels(own_key, extent, shards, -0.22, 0.18)
    return jnp.clip(entries, -reach, reach).astype(kind)


def setup_inputs(seed: int = 0) -> dict:
    keys = jax.random.split(jax.random.key(seed), 11)
    return {
        "block_in": gaussian(keys[0], (ALL_ITEMS, SLOT, D), 1.0, 6.0, ((0, 4), (1, 8))),
        "lead_embed": gaussian(keys[1], (ALL_ITEMS, D), 1.0, 6.0, ((0, 4),)),
        "lengths": draw_lengths(jax.random.fold_in(keys[10], 71), 0),
        "w_ada": gaussian(keys[3], (D, 6 * D), D ** -0.5, 0.3125),
        "b_ada": gaussian(keys[4], (6 * D,), 0.5, 3.0),
        "w_qkv": gaussian(keys[5], (D, 3 * D), D ** -0.5, 0.3125),
        "w_proj": gaussian(keys[6], (D, D), (D // 16) ** -0.5, 1.25),
        "w_fc1": gaussian(keys[7], (D, FF), D ** -0.5, 0.3125),
        "w_fc2": gaussian(keys[8], (FF, D), FF ** -0.5, 0.15625),
        "cotangent": gaussian(keys[9], (ALL_ITEMS, SLOT, D), 1.0, 6.0, ((0, 4), (1, 8))),
    }


EPS = 1e-06

@jax.custom_vjp
def low(v):
    return lax.optimization_barrier(v.astype(jnp.bfloat16)).astype(jnp.float32)

@jax.custom_vjp
def low_back(v):
    return v

def low_keep(v):
    return (low(v), None)

def low_pass(kept, grad):
    return (grad,)

def back_keep(v):
    return (v, None)

def back_low(kept, grad):
    return (low(grad),)
low.defvjp(low_keep, low_pass)
low_back.defvjp(back_keep, back_low)

def layer_norm(values):
    center = values - lax.optimization_barrier(jnp.mean(values, axis=-1, keepdims=True))
    return center * lax.rsqrt(lax.optimization_barrier(jnp.mean(center * center, axis=-1, keepdims=True)) + EPS)

def matmul(left, right):
    return jnp.dot(left, right, precision=lax.Precision.HIGHEST)

def attend(queries, keys_all, values, key_valid):
    block_rows = min(512, SLOT)
    inv_root = HEAD_DIM ** (-0.5)
    query_blocks = queries.reshape(HEADS, SLOT // block_rows, block_rows, HEAD_DIM).transpose(1, 0, 2, 3)

    def one_block(query_block):
        scores = jnp.einsum('hqd,hkd->hqk', query_block, keys_all, precision=lax.Precision.HIGHEST) * inv_root
        scores = low_back(scores)
        scores = jnp.where(key_valid[None, None, :], scores, -1e+30)
        row_peak = lax.optimization_barrier(jnp.max(scores, axis=-1, keepdims=True))
        exp_scores = jnp.exp(scores - row_peak)
        weights = low(exp_scores / lax.optimization_barrier(jnp.sum(exp_scores, axis=-1, keepdims=True)))
        return jnp.einsum('hqk,hkd->hqd', weights, values, precision=lax.Precision.HIGHEST)
    outputs = lax.map(jax.checkpoint(one_block), query_blocks)
    return outputs.transpose(1, 0, 2, 3).reshape(HEADS, SLOT, HEAD_DIM)

def one_item(inputs, embedding, length, weight_ada, bias_ada, weight_qkv, weight_proj, weight_one, weight_two):
    modulation = matmul(low(jax.nn.silu(embedding))[None, :], weight_ada)[0] + bias_ada
    shift_att, scale_att, gate_att, shift_mlp, scale_mlp, gate_mlp = jnp.split(modulation, 6)
    entry = low(layer_norm(inputs) * (1.0 + scale_att) + shift_att)
    triple = low_back(low(matmul(entry, weight_qkv)))
    triple = triple.reshape(SLOT, 3, HEADS, HEAD_DIM).transpose(1, 2, 0, 3)
    key_valid = jnp.arange(SLOT, dtype=jnp.int32) < length
    mixed_out = attend(triple[0], triple[1], triple[2], key_valid)
    mixed_out = low_back(low(mixed_out.transpose(1, 0, 2).reshape(SLOT, D)))
    branch = low_back(matmul(mixed_out, weight_proj))
    middle = inputs + gate_att * branch
    second = low(layer_norm(middle) * (1.0 + scale_mlp) + shift_mlp)
    hidden = low_back(matmul(second, weight_one))
    active = low(jax.nn.gelu(hidden, approximate=False))
    return middle + gate_mlp * low_back(matmul(active, weight_two))

def reference(block_in, lead_embed, lengths, w_ada, b_ada, w_qkv, w_proj, w_fc1, w_fc2, cotangent):
    inputs = block_in.astype(jnp.float32)
    embeds = lead_embed.astype(jnp.float32)

    def forward(inputs, weight_ada, bias_ada, weight_qkv, weight_proj, weight_one, weight_two):

        def per_item(packed):
            return one_item(packed[0], packed[1], packed[2], weight_ada, bias_ada, weight_qkv, weight_proj, weight_one, weight_two)
        return lax.map(jax.checkpoint(per_item), (inputs, embeds, lengths))
    result, pullback = jax.vjp(forward, inputs, w_ada.astype(jnp.float32), b_ada.astype(jnp.float32), w_qkv.astype(jnp.float32), w_proj.astype(jnp.float32), w_fc1.astype(jnp.float32), w_fc2.astype(jnp.float32))
    grads = pullback(cotangent.astype(jnp.float32))
    return (result, grads[0], grads[1], grads[2], grads[3], grads[4], grads[5], grads[6])
```

```python
import math
from functools import partial

import jax
import jax.numpy as jnp
from jax import lax
from jax.experimental import pallas as pl
from jax.experimental.pallas import tpu as pltpu
from jax.sharding import PartitionSpec as P

HEADS = 6
HEAD_DIM = 64


EPS = 1e-06


def norm_rows(values):
    center = values - jnp.mean(values, axis=-1, keepdims=True)
    inverse = lax.rsqrt(jnp.mean(center * center, axis=-1, keepdims=True) + EPS)
    return (center * inverse, inverse)


def norm_back(normed, inverse, gradient):
    return inverse * (
        gradient
        - jnp.mean(gradient, axis=-1, keepdims=True)
        - normed * jnp.mean(gradient * normed, axis=-1, keepdims=True)
    )


def to_heads(tokens, part_count, head_count, head_size):
    item_count, span_len, _ = tokens.shape
    shaped = tokens.reshape(item_count, span_len, part_count, head_count, head_size)
    return shaped.transpose(2, 0, 3, 1, 4).reshape(
        part_count, item_count * head_count, span_len * head_size
    )


def from_heads(blocks, item_count, head_count, head_size):
    part_count = blocks.shape[0]
    span_len = blocks.shape[2] // head_size
    shaped = blocks.reshape(part_count, item_count, head_count, span_len, head_size)
    return shaped.transpose(1, 3, 0, 2, 4).reshape(
        item_count, span_len, part_count * head_count * head_size
    )


def split_rows(values, block_rows):
    pair_count, slot_len = (values.shape[0], values.shape[1])
    rest = values.shape[2:]
    shaped = values.reshape((pair_count, slot_len // block_rows, block_rows) + rest)
    return jnp.moveaxis(shaped, 1, 0)


def join_rows(values):
    merged = jnp.moveaxis(values, 0, 1)
    return merged.reshape((merged.shape[0], merged.shape[1] * merged.shape[2]) + merged.shape[3:])


def masked_scores(query_block, keys_all, key_valid, inv_root):
    scores = (
        jnp.einsum("pqd,pkd->pqk", query_block, keys_all, preferred_element_type=jnp.float32)
        * inv_root
    )
    return jnp.where(key_valid[:, None, :], scores, -1e30)


def attend_forward(queries, keys_all, values, key_valid, inv_root):
    block_rows = min(512, queries.shape[1])

    def one_block(query_block):
        scores = masked_scores(query_block, keys_all, key_valid, inv_root)
        row_peak = jnp.max(scores, axis=-1, keepdims=True)
        exp_scores = jnp.exp(scores - row_peak)
        row_total = jnp.sum(exp_scores, axis=-1, keepdims=True)
        weights = (exp_scores / row_total).astype(jnp.bfloat16)
        outcome = jnp.einsum("pqk,pkd->pqd", weights, values, preferred_element_type=jnp.float32)
        return (outcome.astype(jnp.bfloat16), (row_peak + jnp.log(row_total))[..., 0])

    outputs, logsum = lax.map(one_block, split_rows(queries, block_rows))
    return (join_rows(outputs), join_rows(logsum))


def attend_backward(queries, keys_all, values, out_grad, logsum, key_valid, inv_root):
    block_rows = min(512, queries.shape[1])
    zeros = jnp.zeros(keys_all.shape, jnp.float32)

    def one_block(carried, packed):
        key_grad, value_grad = carried
        query_block, grad_block, logsum_block = packed
        scores = masked_scores(query_block, keys_all, key_valid, inv_root)
        weights = jnp.exp(scores - logsum_block[..., None])
        weight_grad = jnp.einsum(
            "pqd,pkd->pqk", grad_block, values, preferred_element_type=jnp.float32
        )
        score_grad = weights * (
            weight_grad - jnp.sum(weights * weight_grad, axis=-1, keepdims=True)
        )
        score_grad = score_grad.astype(jnp.bfloat16)
        query_grad = (
            jnp.einsum("pqk,pkd->pqd", score_grad, keys_all, preferred_element_type=jnp.float32)
            * inv_root
        )
        key_grad = (
            key_grad
            + jnp.einsum(
                "pqk,pqd->pkd", score_grad, query_block, preferred_element_type=jnp.float32
            )
            * inv_root
        )
        value_grad = value_grad + jnp.einsum(
            "pqk,pqd->pkd",
            weights.astype(jnp.bfloat16),
            grad_block,
            preferred_element_type=jnp.float32,
        )
        return ((key_grad, value_grad), query_grad)

    packed = (
        split_rows(queries, block_rows),
        split_rows(out_grad, block_rows),
        split_rows(logsum, block_rows),
    )
    (key_grad, value_grad), query_grads = lax.scan(one_block, (zeros, zeros), packed)
    return jnp.stack([join_rows(query_grads), key_grad, value_grad]).astype(jnp.bfloat16)


def on_device(block_in, lead_embed, lengths, w_ada, b_ada, w_qkv, w_proj, w_fc1, w_fc2, cotangent):
    item_count, span_len, width = block_in.shape
    head_count = HEADS
    head_size = HEAD_DIM
    shards = lax.axis_size("wide")
    pair_count = item_count * head_count // shards
    slot_len = span_len * shards
    inv_root = HEAD_DIM ** (-0.5)
    inputs = block_in.astype(jnp.float32)
    condition = jax.nn.silu(lead_embed.astype(jnp.float32)).astype(jnp.bfloat16)
    modulation = jnp.dot(condition, w_ada, preferred_element_type=jnp.float32) + b_ada.astype(
        jnp.float32
    )
    pieces = [modulation[:, None, column * width : (column + 1) * width] for column in range(6)]
    shift_att, scale_att, gate_att, shift_mlp, scale_mlp, gate_mlp = pieces
    normed, norm_inverse = norm_rows(inputs)
    entry = (normed * (1.0 + scale_att) + shift_att).astype(jnp.bfloat16)
    triple = jnp.dot(entry, w_qkv, preferred_element_type=jnp.float32).astype(jnp.bfloat16)
    arrived = lax.all_to_all(
        to_heads(triple, 3, head_count, head_size), "wide", split_axis=1, concat_axis=2, tiled=True
    )
    heads_in = arrived.reshape(3, pair_count, slot_len, head_size)
    pair_ids = lax.axis_index("wide") * pair_count + jnp.arange(pair_count, dtype=jnp.int32)
    item_ids = pair_ids // head_count
    pair_length = jnp.sum(
        jnp.where(
            jnp.arange(item_count, dtype=jnp.int32)[None, :] == item_ids[:, None],
            lengths[None, :],
            0,
        ),
        axis=1,
    )
    key_valid = jnp.arange(slot_len, dtype=jnp.int32)[None, :] < pair_length[:, None]
    mixed_heads, logsum = attend_forward(heads_in[0], heads_in[1], heads_in[2], key_valid, inv_root)
    returned = lax.all_to_all(
        mixed_heads.reshape(pair_count, slot_len * head_size),
        "wide",
        split_axis=1,
        concat_axis=0,
        tiled=True,
    )
    mixed_tok = from_heads(returned[None], item_count, head_count, head_size)
    branch = jnp.dot(mixed_tok, w_proj, preferred_element_type=jnp.float32)
    middle = inputs + gate_att * branch
    second_normed, second_inverse = norm_rows(middle)
    second = (second_normed * (1.0 + scale_mlp) + shift_mlp).astype(jnp.bfloat16)
    hidden = jnp.dot(second, w_fc1, preferred_element_type=jnp.float32)
    active = jax.nn.gelu(hidden, approximate=False).astype(jnp.bfloat16)
    mlp_out = jnp.dot(active, w_fc2, preferred_element_type=jnp.float32)
    block_out = middle + gate_mlp * mlp_out
    gradient = cotangent.astype(jnp.float32)
    mlp_grad = (gate_mlp * gradient).astype(jnp.bfloat16)
    gate_mlp_grad = jnp.sum(gradient * mlp_out, axis=1)
    fc2_grad = jnp.einsum("isf,isd->fd", active, mlp_grad, preferred_element_type=jnp.float32)
    active_grad = jnp.dot(mlp_grad, w_fc2.T, preferred_element_type=jnp.float32)
    hidden_grad = jax.vjp(partial(jax.nn.gelu, approximate=False), hidden)[1](active_grad)[0]
    hidden_grad = hidden_grad.astype(jnp.bfloat16)
    fc1_grad = jnp.einsum("isd,isf->df", second, hidden_grad, preferred_element_type=jnp.float32)
    second_grad = jnp.dot(hidden_grad, w_fc1.T, preferred_element_type=jnp.float32)
    scale_mlp_grad = jnp.sum(second_grad * second_normed, axis=1)
    shift_mlp_grad = jnp.sum(second_grad, axis=1)
    middle_grad = gradient + norm_back(
        second_normed, second_inverse, second_grad * (1.0 + scale_mlp)
    )
    branch_grad = (gate_att * middle_grad).astype(jnp.bfloat16)
    gate_att_grad = jnp.sum(middle_grad * branch, axis=1)
    proj_grad = jnp.einsum(
        "isd,ise->de", mixed_tok, branch_grad, preferred_element_type=jnp.float32
    )
    mixed_grad = jnp.dot(branch_grad, w_proj.T, preferred_element_type=jnp.float32).astype(
        jnp.bfloat16
    )
    heads_grad = lax.all_to_all(
        to_heads(mixed_grad, 1, head_count, head_size)[0],
        "wide",
        split_axis=0,
        concat_axis=1,
        tiled=True,
    )
    heads_grad = heads_grad.reshape(pair_count, slot_len, head_size)
    again_in, _ = lax.optimization_barrier((inputs, heads_grad))
    again_normed, _ = norm_rows(again_in)
    again_entry = (again_normed * (1.0 + scale_att) + shift_att).astype(jnp.bfloat16)
    again_triple = jnp.dot(again_entry, w_qkv, preferred_element_type=jnp.float32).astype(
        jnp.bfloat16
    )
    again_heads = lax.all_to_all(
        to_heads(again_triple, 3, head_count, head_size),
        "wide",
        split_axis=1,
        concat_axis=2,
        tiled=True,
    )
    used_heads = again_heads.reshape(3, pair_count, slot_len, head_size)
    triple_grad = attend_backward(
        used_heads[0], used_heads[1], used_heads[2], heads_grad, logsum, key_valid, inv_root
    )
    sent_back = lax.all_to_all(
        triple_grad.reshape(3, pair_count, slot_len * head_size),
        "wide",
        split_axis=2,
        concat_axis=1,
        tiled=True,
    )
    token_grad = from_heads(sent_back, item_count, head_count, head_size)
    qkv_grad = jnp.einsum("isd,ise->de", entry, token_grad, preferred_element_type=jnp.float32)
    entry_grad = jnp.dot(token_grad, w_qkv.T, preferred_element_type=jnp.float32)
    scale_att_grad = jnp.sum(entry_grad * normed, axis=1)
    shift_att_grad = jnp.sum(entry_grad, axis=1)
    input_grad = middle_grad + norm_back(normed, norm_inverse, entry_grad * (1.0 + scale_att))
    modulation_grad = jnp.concatenate(
        [
            shift_att_grad,
            scale_att_grad,
            gate_att_grad,
            shift_mlp_grad,
            scale_mlp_grad,
            gate_mlp_grad,
        ],
        axis=-1,
    )
    ada_grad = jnp.dot(
        condition.astype(jnp.float32).T, modulation_grad, precision=lax.Precision.HIGHEST
    )
    bias_grad = jnp.sum(modulation_grad, axis=0)
    totals = lax.psum(
        (ada_grad, bias_grad, qkv_grad, proj_grad, fc1_grad, fc2_grad), ("batch", "wide")
    )
    return (block_out, input_grad, totals[0], totals[1], totals[2], totals[3], totals[4], totals[5])


MESH = pl.DeviceIdType.MESH
MM = (((1,), (0,)), ((), ()))
NT = (((1,), (1,)), ((), ()))
TN = (((0,), (0,)), ((), ()))
B16 = jnp.bfloat16
F32 = jnp.float32


def dot(left, right, dims):
    return lax.dot_general(left, right, dims, preferred_element_type=F32)


def col_sum(values):
    return jnp.sum(values, axis=0, keepdims=True)


def fused_kernel(
    lengths,
    block_in,
    cotangent,
    lead_embed,
    b_ada,
    w_ada_in,
    w_qkv_in,
    w_proj_in,
    w_fc1_in,
    w_fc2_in,
    out_block,
    out_input,
    out_fc2,
    out_fc1,
    out_qkvp,
    out_mod,
    w_ada,
    w_qkv,
    w_proj,
    w_fc1,
    w_fc2,
    xall,
    gall,
    mod_rows,
    entry,
    normed_own,
    q_all,
    kv_all,
    bias_keys,
    probs,
    mixed,
    middle_ref,
    active,
    gelu_slope,
    hidden_grad,
    grads_bf,
    send_out,
    entry_send,
    entry_recv,
    qkvp,
    core_out,
    core_in,
    hold,
    stage1,
    stage1_in,
    stage2,
    stage2_in,
    stage3,
    stage3_in,
    stage4,
    stage4_in,
    total,
    mod_own,
    mod_in,
    mod_all,
    local_sem,
    x_send,
    x_recv,
    f_send,
    f_recv,
    g_send,
    g_recv,
    o_send,
    o_recv,
    e_send,
    e_recv,
    m_send,
    m_recv,
    wave_send,
    wave_recv,
):
    items, span, width = block_in.shape
    own = items * span
    head_pairs = width // 128
    blocks = active.shape[0]
    inv_root = HEAD_DIM**-0.5
    batch, wide = lax.axis_index("batch"), lax.axis_index("wide")
    z, core = wide // 2, wide % 2
    y, x = batch // 2, batch % 2
    zb = z % 2

    def at(y_, x_, z_, core_):
        return (y_ * 2 + x_, z_ * 2 + core_)

    core_peer = at(y, x, z, 1 - core)
    x_peer = at(y, 1 - x, z, core)
    y_peer = at(1 - y, x, z, core)
    xy_peer = at(1 - y, 1 - x, z, core)
    z_pair = z + 1 - 2 * zb
    z1_peer = at(y, x, z_pair, core)
    z2_peer = at(y, x, (z + 2) % items, core)

    def remote(src, dst, send, recv, device):
        return pltpu.make_async_remote_copy(
            src_ref=src,
            dst_ref=dst,
            send_sem=send,
            recv_sem=recv,
            device_id=device,
            device_id_type=MESH,
        )

    def local(src, dst, index):
        copy = pltpu.make_async_copy(src, dst, local_sem.at[index])
        copy.start()
        return copy

    loads = [
        local(w_ada_in, w_ada, 0),
        local(w_qkv_in, w_qkv, 1),
        local(w_proj_in, w_proj, 2),
        local(w_fc1_in, w_fc1, 3),
        local(w_fc2_in, w_fc2, 4),
        local(block_in.at[z], xall.at[0, z], 5),
        local(cotangent.at[z], gall.at[z], 6),
    ]

    barrier = pltpu.get_barrier_semaphore()
    greet = [core_peer, x_peer, y_peer, xy_peer]
    greet += [at(y, x, (z + step) % items, core) for step in range(1, items)]
    for device in greet:
        pl.semaphore_signal(barrier, inc=1, device_id=device, device_id_type=MESH)
    pl.semaphore_wait(barrier, len(greet))

    x_copies, g_copies = [], []
    for step in range(1, items):
        there = (z + step) % items
        copy = remote(
            block_in.at[there],
            xall.at[0, z],
            x_send.at[step - 1],
            x_recv.at[step - 1],
            at(y, x, there, core),
        )
        copy.start()
        x_copies.append(copy)
    forwards = [
        remote(block_in.at[z], xall.at[1, z], f_send.at[0], f_recv.at[0], core_peer)
    ]
    forwards[0].start()
    for step in range(1, items):
        there = (z + step) % items
        copy = remote(
            cotangent.at[there],
            gall.at[z],
            g_send.at[step - 1],
            g_recv.at[step - 1],
            at(y, x, there, core),
        )
        copy.start()
        g_copies.append(copy)

    embed = lead_embed[...].astype(F32)
    condition = (embed / (1.0 + jnp.exp(-embed))).astype(B16)
    loads[0].wait()
    all_rows = dot(condition, w_ada[...], MM) + b_ada[...].astype(F32)
    mine = lax.broadcasted_iota(jnp.int32, (items, 1), 0) == z
    mod_rows[...] = jnp.sum(jnp.where(mine, all_rows, 0.0), axis=0, keepdims=True)
    pieces = [mod_rows[:, column * width : (column + 1) * width] for column in range(6)]
    shift_att, scale_att, gate_att, shift_mlp, scale_mlp, gate_mlp = pieces
    mod_own[...] = jnp.zeros(mod_own.shape, F32)
    mod_own[6:7, :] = jnp.sum(jnp.where(mine, condition.astype(F32), 0.0), axis=0, keepdims=True)

    row = lax.broadcasted_iota(jnp.int32, bias_keys.shape, 0)
    block_core = jnp.where(row // own == 0, core, 1 - core)
    position = ((row % own) // span * 2 + block_core) * span + row % span
    bias_keys[...] = jnp.where(position < lengths[z], 0.0, -1e30)

    loads[5].wait()
    for step in range(1, items):
        came = (z + items - step) % items
        x_copies[step - 1].wait_recv()
        copy = remote(
            xall.at[0, came],
            xall.at[1, came],
            f_send.at[step],
            f_recv.at[step],
            core_peer,
        )
        copy.start()
        forwards.append(copy)

    loads[1].wait()
    inputs = xall[0].reshape(own, width).astype(F32)
    normed, norm_inverse = norm_rows(inputs)
    normed_own[...] = normed
    entry[:own, :] = (normed * (1.0 + scale_att) + shift_att).astype(B16)
    q_all[...] = (dot(entry[:own, :], w_qkv[:, :width], MM).astype(B16) * inv_root).astype(B16)
    kv_all[:own, :] = dot(entry[:own, :], w_qkv[:, width:], MM).astype(B16)
    for copy in forwards:
        copy.wait_recv()
    other_normed, _ = norm_rows(xall[1].reshape(own, width).astype(F32))
    entry[own:, :] = (other_normed * (1.0 + scale_att) + shift_att).astype(B16)
    kv_all[own:, :] = dot(entry[own:, :], w_qkv[:, width:], MM).astype(B16)

    lane = lax.broadcasted_iota(jnp.int32, (1, 128), 1)
    halves = [
        jnp.where(lane < HEAD_DIM, 1.0, 0.0).astype(B16),
        jnp.where(lane < HEAD_DIM, 0.0, 1.0).astype(B16),
    ]
    for pair in range(head_pairs):
        lanes = slice(pair * 128, (pair + 1) * 128)
        v_lanes = slice(width + pair * 128, width + (pair + 1) * 128)
        keys, values, queries = kv_all[:, lanes], kv_all[:, v_lanes], q_all[:, lanes]
        parts = []
        for half in range(2):
            scores = dot(keys, queries * halves[half], NT) + bias_keys[...]
            exp_scores = jnp.exp(scores - jnp.max(scores, axis=0, keepdims=True))
            weights = exp_scores * (1.0 / jnp.sum(exp_scores, axis=0, keepdims=True))
            probs[pair * 2 + half] = weights
            out = dot(values, weights.astype(B16), TN)
            parts.append(out[half * HEAD_DIM : (half + 1) * HEAD_DIM])
        mixed[:, lanes] = jnp.concatenate(parts, axis=0).T.astype(B16)

    loads[2].wait()
    branch = dot(mixed[...], w_proj[...], MM)
    middle = inputs + gate_att * branch
    middle_ref[0] = branch
    second_normed, second_inverse = norm_rows(middle)
    middle_ref[1] = second_normed
    second = (second_normed * (1.0 + scale_mlp) + shift_mlp).astype(B16)
    grads_bf[0] = second
    loads[3].wait()
    loads[4].wait()
    mlp_out = jnp.zeros((own, width), F32)
    for block in range(blocks):
        columns = slice(block * width, (block + 1) * width)
        hidden = dot(second, w_fc1[:, columns], MM)
        cumulative = 0.5 * (1.0 + lax.erf(hidden * (0.5**0.5)))
        act = (hidden * cumulative).astype(B16)
        active[block] = act
        gelu_slope[block] = cumulative + hidden * (
            jnp.exp(-0.5 * hidden * hidden) * (1.0 / math.sqrt(2.0 * math.pi))
        )
        mlp_out = mlp_out + dot(act, w_fc2[columns, :], MM)

    def give_back(values, out, first):
        send_out[first // items] = values.astype(B16).reshape(items, span, width)
        copies = []
        for step in range(1, items):
            there = (z + step) % items
            copy = remote(
                send_out.at[first // items, there],
                out.at[z],
                o_send.at[first + step - 1],
                o_recv.at[first + step - 1],
                at(y, x, there, core),
            )
            copy.start()
            copies.append(copy)
        copies.append(local(send_out.at[first // items, z], out.at[z], 7 + first // items))
        return copies

    block_copies = give_back(middle + gate_mlp * mlp_out, out_block, 0)

    loads[6].wait()
    for copy in g_copies:
        copy.wait_recv()
    gradient = gall[...].reshape(own, width).astype(F32)
    mod_own[5:6, :] = col_sum(gradient * mlp_out)
    mlp_grad = (gate_mlp * gradient).astype(B16)
    grads_bf[1] = mlp_grad

    def wave_copy(wave, slot, src, dst, device):
        copy = remote(src, dst, wave_send.at[wave, slot], wave_recv.at[wave, slot], device)
        copy.start()
        return copy

    def core_start(wave):
        return wave_copy(wave, 0, core_out.at[wave], core_in.at[wave], core_peer)

    pending = []

    def rows_of(start, count):
        return pl.ds(pl.multiple_of(start, 16), count)

    def wave_part(wave, part):
        bits = (x, y) if part == 0 else (y, x)
        devices = (x_peer, y_peer) if part == 0 else (y_peer, x_peer)
        slot = 1 + part * 8
        chunk = hold.shape[1] // 2
        base = part * chunk

        n1 = chunk // 2
        away = base + (1 - bits[0]) * n1
        kept = base + bits[0] * n1
        stage1[wave, part] = hold[wave, rows_of(away, n1), :].astype(B16)
        copy1 = wave_copy(wave, slot, stage1.at[wave, part], stage1_in.at[wave, part], devices[0])
        pending.append(copy1)
        yield
        copy1.wait_recv()
        n2 = n1 // 2
        away, kept2 = (1 - bits[1]) * n2, bits[1] * n2
        stage2[wave, part] = (
            hold[wave, rows_of(kept + away, n2), :]
            + stage1_in[wave, part, rows_of(away, n2), :].astype(F32)
        ).astype(B16)
        copy2 = wave_copy(
            wave, slot + 1, stage2.at[wave, part], stage2_in.at[wave, part], devices[1]
        )
        pending.append(copy2)
        hold[wave, rows_of(kept + kept2, n2), :] += stage1_in[
            wave, part, rows_of(kept2, n2), :
        ].astype(F32)
        kept = kept + kept2
        yield
        copy2.wait_recv()
        n3 = n2 // 2
        away, kept3 = (1 - zb) * n3, zb * n3
        stage3[wave, part] = (
            hold[wave, rows_of(kept + away, n3), :]
            + stage2_in[wave, part, rows_of(away, n3), :].astype(F32)
        ).astype(B16)
        copy3 = wave_copy(wave, slot + 2, stage3.at[wave, part], stage3_in.at[wave, part], z1_peer)
        pending.append(copy3)
        hold[wave, rows_of(kept + kept3, n3), :] += stage2_in[
            wave, part, rows_of(kept3, n3), :
        ].astype(F32)
        place2 = kept
        kept = kept + kept3
        yield
        copy3.wait_recv()
        stage4[wave, part] = (
            hold[wave, rows_of(kept, n3), :] + stage3_in[wave, part].astype(F32)
        ).astype(B16)
        copy4 = wave_copy(wave, slot + 3, stage4.at[wave, part], stage4_in.at[wave, part], z2_peer)
        pending.append(copy4)
        yield
        copy4.wait_recv()
        here = core * hold.shape[1]
        result = total.at[wave, rows_of(here + kept, n3), :]
        result[...] = (
            stage4[wave, part].astype(F32) + stage4_in[wave, part].astype(F32)
        ).astype(B16)
        copy5 = wave_copy(wave, slot + 4, result, result, z1_peer)
        pending.append(copy5)
        yield
        copy5.wait_recv()
        result = total.at[wave, rows_of(here + place2, n2), :]
        copy6 = wave_copy(wave, slot + 5, result, result, devices[1])
        pending.append(copy6)
        yield
        copy6.wait_recv()
        result = total.at[wave, rows_of(here + base + bits[0] * n1, n1), :]
        copy7 = wave_copy(wave, slot + 6, result, result, devices[0])
        pending.append(copy7)
        yield
        copy7.wait_recv()
        result = total.at[wave, rows_of(here + base, chunk), :]
        copy8 = wave_copy(wave, slot + 7, result, result, core_peer)
        pending.append(copy8)
        pending_local.append(put(wave, 2 * core + part, 9 + wave * 4 + part))
        yield
        copy8.wait_recv()
        pending_local.append(put(wave, 2 * (1 - core) + part, 11 + wave * 4 + part))

    pending_local = []

    def put(wave, block, index):
        rows = rows_of(block * width, width)
        source = total.at[wave, rows, :]
        if wave == 0:
            return local(source, out_fc2.at[rows, :], index)
        columns = pl.ds(pl.multiple_of(block * width, 128), width)
        out = out_fc1 if wave == 1 else out_qkvp
        return local(source, out.at[:, columns], index)

    def core_add(wave, copy):
        copy.wait_recv()
        hold[wave] = hold[wave] + core_in[wave].astype(F32)

    def start_parts(wave):
        parts = [wave_part(wave, 0), wave_part(wave, 1)]
        for part in parts:
            next(part)
        return parts

    def advance(parts):
        for part in parts:
            next(part, None)

    per_core = blocks // 2
    for index in range(per_core):
        block = (1 - core) * per_core + index
        rows = slice(index * width, (index + 1) * width)
        core_out[0, rows, :] = dot(active[block], mlp_grad, TN).astype(B16)
    copies_core = [core_start(0)]
    for index in range(per_core):
        block = core * per_core + index
        rows = slice(index * width, (index + 1) * width)
        hold[0, rows, :] = dot(active[block], mlp_grad, TN)

    second_grad = jnp.zeros((own, width), F32)
    for block in range(blocks):
        columns = slice(block * width, (block + 1) * width)
        active_grad = dot(mlp_grad, w_fc2[columns, :], NT)
        hid = (active_grad * gelu_slope[block]).astype(B16)
        hidden_grad[block] = hid
        second_grad = second_grad + dot(hid, w_fc1[:, columns], NT)

    core_add(0, copies_core[0])
    parts0 = start_parts(0)

    for index in range(per_core):
        block = (1 - core) * per_core + index
        rows = slice(index * width, (index + 1) * width)
        core_out[1, rows, :] = dot(grads_bf[0], hidden_grad[block], TN).astype(B16)
    copies_core.append(core_start(1))
    for index in range(per_core):
        block = core * per_core + index
        rows = slice(index * width, (index + 1) * width)
        hold[1, rows, :] = dot(grads_bf[0], hidden_grad[block], TN)

    second_normed = middle_ref[1]
    mod_own[4:5, :] = col_sum(second_grad * second_normed)
    mod_own[3:4, :] = col_sum(second_grad)
    middle_grad = gradient + norm_back(
        second_normed, second_inverse, second_grad * (1.0 + scale_mlp)
    )
    mod_own[2:3, :] = col_sum(middle_grad * middle_ref[0])
    branch_grad = (gate_att * middle_grad).astype(B16)
    middle_ref[0] = middle_grad
    grads_bf[2] = dot(branch_grad, w_proj[...], NT).astype(B16)
    qkvp[3] = dot(mixed[...], branch_grad, TN)

    core_add(1, copies_core[1])
    parts1 = start_parts(1)

    dq, dkv = q_all, kv_all
    for pair in range(head_pairs):
        lanes = slice(pair * 128, (pair + 1) * 128)
        v_lanes = slice(width + pair * 128, width + (pair + 1) * 128)
        keys, values, queries = kv_all[:, lanes], kv_all[:, v_lanes], q_all[:, lanes]
        out_grad = grads_bf[2, :, lanes]
        parts = []
        key_grad = jnp.zeros((2 * own, 128), F32)
        value_grad = jnp.zeros((2 * own, 128), F32)
        for half in range(2):
            masked_grad = out_grad * halves[half]
            weights = probs[pair * 2 + half]
            weight_grad = dot(values, masked_grad, NT)
            score_grad = (
                weights * (weight_grad - col_sum(weights * weight_grad))
            ).astype(B16)
            value_grad = value_grad + dot(weights.astype(B16), masked_grad, MM)
            key_grad = key_grad + dot(score_grad, queries * halves[half], MM)
            query_grad = dot(keys, score_grad, TN)
            parts.append(query_grad[half * HEAD_DIM : (half + 1) * HEAD_DIM])
        query_grad = jnp.concatenate(parts, axis=0).T * inv_root
        dq[:, lanes] = query_grad.astype(B16)
        dkv[:, lanes] = key_grad.astype(B16)
        dkv[:, v_lanes] = value_grad.astype(B16)
        if pair == 0:
            advance(parts0)
        elif pair == 1:
            advance(parts1)

    qkvp[0] = dot(entry[:own, :], dq[...], TN)
    qkvp[1] = dot(entry[...], dkv[:, :width], TN)
    qkvp[2] = dot(entry[...], dkv[:, width:], TN)
    for index in range(per_core):
        rows = slice(index * width, (index + 1) * width)
        core_out[2, rows, :] = qkvp[(1 - core) * per_core + index].astype(B16)
        hold[2, rows, :] = qkvp[core * per_core + index]
    copies_core.append(core_start(2))

    entry_send[...] = dot(dkv[own:, :], w_qkv[:, width:], NT)
    entry_copy = remote(entry_send, entry_recv, e_send.at[0], e_recv.at[0], core_peer)
    entry_copy.start()
    entry_grad = dot(dkv[:own, :], w_qkv[:, width:], NT) + dot(dq[...], w_qkv[:, :width], NT)

    core_add(2, copies_core[2])
    parts2 = start_parts(2)
    advance(parts0)

    entry_copy.wait_recv()
    entry_grad = entry_grad + entry_recv[...]
    normed = normed_own[...]
    mod_own[1:2, :] = col_sum(entry_grad * normed)
    mod_own[0:1, :] = col_sum(entry_grad)
    mod_copies = [remote(mod_own, mod_in, m_send.at[0], m_recv.at[0], core_peer)]
    mod_copies[0].start()
    input_grad = middle_ref[0] + norm_back(normed, norm_inverse, entry_grad * (1.0 + scale_att))
    input_copies = give_back(input_grad, out_input, items)

    mod_copies[0].wait_recv()
    first_row = batch * items
    weight = jnp.where(lax.broadcasted_iota(jnp.int32, mod_own.shape, 0) == 6, 0.5, 1.0)
    mod_all[first_row + z] = (mod_own[...] + mod_in[...]) * weight
    for step in range(1, items):
        there = (z + step) % items
        place = mod_all.at[first_row + z]
        copy = remote(place, place, m_send.at[step], m_recv.at[step], at(y, x, there, core))
        copy.start()
        mod_copies.append(copy)
    advance(parts1)
    advance(parts2)
    advance(parts0)
    for copy in mod_copies[1:]:
        copy.wait_recv()
    for index, device in enumerate((x_peer, y_peer, xy_peer)):
        place = mod_all.at[pl.ds(first_row, items)]
        copy = remote(place, place, m_send.at[items + index], m_recv.at[items + index], device)
        copy.start()
        mod_copies.append(copy)
    advance(parts1)
    advance(parts2)
    advance(parts0)
    for copy in mod_copies[items:]:
        copy.wait_recv()
    out_mod[...] = mod_all[...]
    for _ in range(10):
        advance(parts1)
        advance(parts2)
        advance(parts0)

    for copy in x_copies + g_copies + forwards + copies_core + [entry_copy] + mod_copies + pending:
        copy.wait_send()
    for copies in (block_copies, input_copies):
        for copy in copies[:-1]:
            copy.wait()
        copies[-1].wait()
    for copy in pending_local:
        copy.wait()


def fused(block_in, lead_embed, lengths, w_ada, b_ada, w_qkv, w_proj, w_fc1, w_fc2, cotangent):
    items, span, width = block_in.shape
    hidden = w_fc1.shape[1]
    groups = lax.axis_size("batch")
    own = items * span
    blocks = hidden // width
    half = hidden // 2
    waves = 3
    vmem = pl.BlockSpec(memory_space=pltpu.VMEM)
    smem = pl.BlockSpec(memory_space=pltpu.SMEM)
    hbm = pl.BlockSpec(memory_space=pl.ANY)
    chunk = half // 2
    dma = pltpu.SemaphoreType.DMA
    scratch = [
        pltpu.VMEM(w_ada.shape, B16),
        pltpu.VMEM(w_qkv.shape, B16),
        pltpu.VMEM(w_proj.shape, B16),
        pltpu.VMEM(w_fc1.shape, B16),
        pltpu.VMEM(w_fc2.shape, B16),
        pltpu.VMEM((2, items, span, width), B16),
        pltpu.VMEM((items, span, width), B16),
        pltpu.VMEM((1, 6 * width), F32),
        pltpu.VMEM((2 * own, width), B16),
        pltpu.VMEM((own, width), F32),
        pltpu.VMEM((own, width), B16),
        pltpu.VMEM((2 * own, 2 * width), B16),
        pltpu.VMEM((2 * own, own), F32),
        pltpu.VMEM((HEADS, 2 * own, own), F32),
        pltpu.VMEM((own, width), B16),
        pltpu.VMEM((2, own, width), F32),
        pltpu.VMEM((blocks, own, width), B16),
        pltpu.VMEM((blocks, own, width), F32),
        pltpu.VMEM((blocks, own, width), B16),
        pltpu.VMEM((3, own, width), B16),
        pltpu.VMEM((2, items, span, width), B16),
        pltpu.VMEM((own, width), F32),
        pltpu.VMEM((own, width), F32),
        pltpu.VMEM((blocks, width, width), F32),
        pltpu.VMEM((waves, half, width), B16),
        pltpu.VMEM((waves, half, width), B16),
        pltpu.VMEM((waves, half, width), F32),
    ]
    for divide in (2, 4, 8, 8):
        scratch += [pltpu.VMEM((waves, 2, chunk // divide, width), B16)] * 2
    scratch += [
        pltpu.VMEM((waves, hidden, width), B16),
        pltpu.VMEM((8, width), F32),
        pltpu.VMEM((8, width), F32),
        pltpu.VMEM((groups * items, 8, width), F32),
        dma((9 + 4 * waves,)),
        dma((items - 1,)),
        dma((items - 1,)),
        dma((items,)),
        dma((items,)),
        dma((items - 1,)),
        dma((items - 1,)),
        dma((2 * items,)),
        dma((2 * items,)),
        dma((1,)),
        dma((1,)),
        dma((items + 3,)),
        dma((items + 3,)),
        dma((waves, 17)),
        dma((waves, 17)),
    ]
    out_block, out_input, fc2_sum, fc1_sum, qkvp_sum, mod = pl.pallas_call(
        fused_kernel,
        out_shape=(
            jax.ShapeDtypeStruct(block_in.shape, B16),
            jax.ShapeDtypeStruct(block_in.shape, B16),
            jax.ShapeDtypeStruct((hidden, width), B16),
            jax.ShapeDtypeStruct((width, hidden), B16),
            jax.ShapeDtypeStruct((width, 4 * width), B16),
            jax.ShapeDtypeStruct((groups * items, 8, width), F32),
        ),
        in_specs=[smem, hbm, hbm, vmem, vmem, hbm, hbm, hbm, hbm, hbm],
        out_specs=(hbm, hbm, hbm, hbm, hbm, vmem),
        scratch_shapes=scratch,
        name="fused_block",
        compiler_params=pltpu.CompilerParams(
            collective_id=0, has_side_effects=True, vmem_limit_bytes=56 * 2**20
        ),
    )(
        lengths,
        block_in,
        cotangent,
        lead_embed,
        b_ada.reshape(1, -1),
        w_ada,
        w_qkv,
        w_proj,
        w_fc1,
        w_fc2,
    )
    pieces = mod[:, :6].reshape(groups * items, 6 * width)
    ada_grad = lax.dot_general(mod[:, 6], pieces, TN, precision=lax.Precision.HIGHEST)
    return (
        out_block.astype(F32),
        out_input.astype(F32),
        ada_grad,
        jnp.sum(pieces, axis=0),
        qkvp_sum[:, : 3 * width].astype(F32),
        qkvp_sum[:, 3 * width :].astype(F32),
        fc1_sum.astype(F32),
        fc2_sum.astype(F32),
    )


def choose(*arrays):
    items, span, width = arrays[0].shape
    fits = (
        lax.axis_size("batch") == 4
        and items == 4
        and lax.axis_size("wide") == 2 * items
        and span == 64
        and width == HEADS * HEAD_DIM == 384
        and arrays[7].shape[1] == 4 * width
    )
    return (fused if fits else on_device)(*arrays)


def solution(mesh):
    return jax.shard_map(
        choose,
        mesh=mesh,
        in_specs=(
            P("batch", "wide", None),
            P("batch", None),
            P("batch"),
            P(),
            P(),
            P(),
            P(),
            P(),
            P(),
            P("batch", "wide", None),
        ),
        out_specs=(
            P("batch", "wide", None),
            P("batch", "wide", None),
            P(),
            P(),
            P(),
            P(),
            P(),
            P(),
        ),
        check_vma=False,
    )
```

```python
import math
from functools import partial

import jax
import jax.numpy as jnp
from jax import lax
from jax.experimental import pallas as pl
from jax.experimental.pallas import tpu as pltpu
from jax.sharding import PartitionSpec as P

HEADS = 6
HEAD_DIM = 64


EPS = 1e-06


def norm_rows(values):
    center = values - jnp.mean(values, axis=-1, keepdims=True)
    inverse = lax.rsqrt(jnp.mean(center * center, axis=-1, keepdims=True) + EPS)
    return (center * inverse, inverse)


def norm_back(normed, inverse, gradient):
    return inverse * (
        gradient
        - jnp.mean(gradient, axis=-1, keepdims=True)
        - normed * jnp.mean(gradient * normed, axis=-1, keepdims=True)
    )


def to_heads(tokens, part_count, head_count, head_size):
    item_count, span_len, _ = tokens.shape
    shaped = tokens.reshape(item_count, span_len, part_count, head_count, head_size)
    return shaped.transpose(2, 0, 3, 1, 4).reshape(
        part_count, item_count * head_count, span_len * head_size
    )


def from_heads(blocks, item_count, head_count, head_size):
    part_count = blocks.shape[0]
    span_len = blocks.shape[2] // head_size
    shaped = blocks.reshape(part_count, item_count, head_count, span_len, head_size)
    return shaped.transpose(1, 3, 0, 2, 4).reshape(
        item_count, span_len, part_count * head_count * head_size
    )


def split_rows(values, block_rows):
    pair_count, slot_len = (values.shape[0], values.shape[1])
    rest = values.shape[2:]
    shaped = values.reshape((pair_count, slot_len // block_rows, block_rows) + rest)
    return jnp.moveaxis(shaped, 1, 0)


def join_rows(values):
    merged = jnp.moveaxis(values, 0, 1)
    return merged.reshape((merged.shape[0], merged.shape[1] * merged.shape[2]) + merged.shape[3:])


def masked_scores(query_block, keys_all, key_valid, inv_root):
    scores = (
        jnp.einsum("pqd,pkd->pqk", query_block, keys_all, preferred_element_type=jnp.float32)
        * inv_root
    )
    return jnp.where(key_valid[:, None, :], scores, -1e30)


def attend_forward(queries, keys_all, values, key_valid, inv_root):
    block_rows = min(512, queries.shape[1])

    def one_block(query_block):
        scores = masked_scores(query_block, keys_all, key_valid, inv_root)
        row_peak = jnp.max(scores, axis=-1, keepdims=True)
        exp_scores = jnp.exp(scores - row_peak)
        row_total = jnp.sum(exp_scores, axis=-1, keepdims=True)
        weights = (exp_scores / row_total).astype(jnp.bfloat16)
        outcome = jnp.einsum("pqk,pkd->pqd", weights, values, preferred_element_type=jnp.float32)
        return (outcome.astype(jnp.bfloat16), (row_peak + jnp.log(row_total))[..., 0])

    outputs, logsum = lax.map(one_block, split_rows(queries, block_rows))
    return (join_rows(outputs), join_rows(logsum))


def attend_backward(queries, keys_all, values, out_grad, logsum, key_valid, inv_root):
    block_rows = min(512, queries.shape[1])
    zeros = jnp.zeros(keys_all.shape, jnp.float32)

    def one_block(carried, packed):
        key_grad, value_grad = carried
        query_block, grad_block, logsum_block = packed
        scores = masked_scores(query_block, keys_all, key_valid, inv_root)
        weights = jnp.exp(scores - logsum_block[..., None])
        weight_grad = jnp.einsum(
            "pqd,pkd->pqk", grad_block, values, preferred_element_type=jnp.float32
        )
        score_grad = weights * (
            weight_grad - jnp.sum(weights * weight_grad, axis=-1, keepdims=True)
        )
        score_grad = score_grad.astype(jnp.bfloat16)
        query_grad = (
            jnp.einsum("pqk,pkd->pqd", score_grad, keys_all, preferred_element_type=jnp.float32)
            * inv_root
        )
        key_grad = (
            key_grad
            + jnp.einsum(
                "pqk,pqd->pkd", score_grad, query_block, preferred_element_type=jnp.float32
            )
            * inv_root
        )
        value_grad = value_grad + jnp.einsum(
            "pqk,pqd->pkd",
            weights.astype(jnp.bfloat16),
            grad_block,
            preferred_element_type=jnp.float32,
        )
        return ((key_grad, value_grad), query_grad)

    packed = (
        split_rows(queries, block_rows),
        split_rows(out_grad, block_rows),
        split_rows(logsum, block_rows),
    )
    (key_grad, value_grad), query_grads = lax.scan(one_block, (zeros, zeros), packed)
    return jnp.stack([join_rows(query_grads), key_grad, value_grad]).astype(jnp.bfloat16)


def on_device(block_in, lead_embed, lengths, w_ada, b_ada, w_qkv, w_proj, w_fc1, w_fc2, cotangent):
    item_count, span_len, width = block_in.shape
    head_count = HEADS
    head_size = HEAD_DIM
    shards = lax.axis_size("wide")
    pair_count = item_count * head_count // shards
    slot_len = span_len * shards
    inv_root = HEAD_DIM ** (-0.5)
    inputs = block_in.astype(jnp.float32)
    condition = jax.nn.silu(lead_embed.astype(jnp.float32)).astype(jnp.bfloat16)
    modulation = jnp.dot(condition, w_ada, preferred_element_type=jnp.float32) + b_ada.astype(
        jnp.float32
    )
    pieces = [modulation[:, None, column * width : (column + 1) * width] for column in range(6)]
    shift_att, scale_att, gate_att, shift_mlp, scale_mlp, gate_mlp = pieces
    normed, norm_inverse = norm_rows(inputs)
    entry = (normed * (1.0 + scale_att) + shift_att).astype(jnp.bfloat16)
    triple = jnp.dot(entry, w_qkv, preferred_element_type=jnp.float32).astype(jnp.bfloat16)
    arrived = lax.all_to_all(
        to_heads(triple, 3, head_count, head_size), "wide", split_axis=1, concat_axis=2, tiled=True
    )
    heads_in = arrived.reshape(3, pair_count, slot_len, head_size)
    pair_ids = lax.axis_index("wide") * pair_count + jnp.arange(pair_count, dtype=jnp.int32)
    item_ids = pair_ids // head_count
    pair_length = jnp.sum(
        jnp.where(
            jnp.arange(item_count, dtype=jnp.int32)[None, :] == item_ids[:, None],
            lengths[None, :],
            0,
        ),
        axis=1,
    )
    key_valid = jnp.arange(slot_len, dtype=jnp.int32)[None, :] < pair_length[:, None]
    mixed_heads, logsum = attend_forward(heads_in[0], heads_in[1], heads_in[2], key_valid, inv_root)
    returned = lax.all_to_all(
        mixed_heads.reshape(pair_count, slot_len * head_size),
        "wide",
        split_axis=1,
        concat_axis=0,
        tiled=True,
    )
    mixed_tok = from_heads(returned[None], item_count, head_count, head_size)
    branch = jnp.dot(mixed_tok, w_proj, preferred_element_type=jnp.float32)
    middle = inputs + gate_att * branch
    second_normed, second_inverse = norm_rows(middle)
    second = (second_normed * (1.0 + scale_mlp) + shift_mlp).astype(jnp.bfloat16)
    hidden = jnp.dot(second, w_fc1, preferred_element_type=jnp.float32)
    active = jax.nn.gelu(hidden, approximate=False).astype(jnp.bfloat16)
    mlp_out = jnp.dot(active, w_fc2, preferred_element_type=jnp.float32)
    block_out = middle + gate_mlp * mlp_out
    gradient = cotangent.astype(jnp.float32)
    mlp_grad = (gate_mlp * gradient).astype(jnp.bfloat16)
    gate_mlp_grad = jnp.sum(gradient * mlp_out, axis=1)
    fc2_grad = jnp.einsum("isf,isd->fd", active, mlp_grad, preferred_element_type=jnp.float32)
    active_grad = jnp.dot(mlp_grad, w_fc2.T, preferred_element_type=jnp.float32)
    hidden_grad = jax.vjp(partial(jax.nn.gelu, approximate=False), hidden)[1](active_grad)[0]
    hidden_grad = hidden_grad.astype(jnp.bfloat16)
    fc1_grad = jnp.einsum("isd,isf->df", second, hidden_grad, preferred_element_type=jnp.float32)
    second_grad = jnp.dot(hidden_grad, w_fc1.T, preferred_element_type=jnp.float32)
    scale_mlp_grad = jnp.sum(second_grad * second_normed, axis=1)
    shift_mlp_grad = jnp.sum(second_grad, axis=1)
    middle_grad = gradient + norm_back(
        second_normed, second_inverse, second_grad * (1.0 + scale_mlp)
    )
    branch_grad = (gate_att * middle_grad).astype(jnp.bfloat16)
    gate_att_grad = jnp.sum(middle_grad * branch, axis=1)
    proj_grad = jnp.einsum(
        "isd,ise->de", mixed_tok, branch_grad, preferred_element_type=jnp.float32
    )
    mixed_grad = jnp.dot(branch_grad, w_proj.T, preferred_element_type=jnp.float32).astype(
        jnp.bfloat16
    )
    heads_grad = lax.all_to_all(
        to_heads(mixed_grad, 1, head_count, head_size)[0],
        "wide",
        split_axis=0,
        concat_axis=1,
        tiled=True,
    )
    heads_grad = heads_grad.reshape(pair_count, slot_len, head_size)
    again_in, _ = lax.optimization_barrier((inputs, heads_grad))
    again_normed, _ = norm_rows(again_in)
    again_entry = (again_normed * (1.0 + scale_att) + shift_att).astype(jnp.bfloat16)
    again_triple = jnp.dot(again_entry, w_qkv, preferred_element_type=jnp.float32).astype(
        jnp.bfloat16
    )
    again_heads = lax.all_to_all(
        to_heads(again_triple, 3, head_count, head_size),
        "wide",
        split_axis=1,
        concat_axis=2,
        tiled=True,
    )
    used_heads = again_heads.reshape(3, pair_count, slot_len, head_size)
    triple_grad = attend_backward(
        used_heads[0], used_heads[1], used_heads[2], heads_grad, logsum, key_valid, inv_root
    )
    sent_back = lax.all_to_all(
        triple_grad.reshape(3, pair_count, slot_len * head_size),
        "wide",
        split_axis=2,
        concat_axis=1,
        tiled=True,
    )
    token_grad = from_heads(sent_back, item_count, head_count, head_size)
    qkv_grad = jnp.einsum("isd,ise->de", entry, token_grad, preferred_element_type=jnp.float32)
    entry_grad = jnp.dot(token_grad, w_qkv.T, preferred_element_type=jnp.float32)
    scale_att_grad = jnp.sum(entry_grad * normed, axis=1)
    shift_att_grad = jnp.sum(entry_grad, axis=1)
    input_grad = middle_grad + norm_back(normed, norm_inverse, entry_grad * (1.0 + scale_att))
    modulation_grad = jnp.concatenate(
        [
            shift_att_grad,
            scale_att_grad,
            gate_att_grad,
            shift_mlp_grad,
            scale_mlp_grad,
            gate_mlp_grad,
        ],
        axis=-1,
    )
    ada_grad = jnp.dot(
        condition.astype(jnp.float32).T, modulation_grad, precision=lax.Precision.HIGHEST
    )
    bias_grad = jnp.sum(modulation_grad, axis=0)
    totals = lax.psum(
        (ada_grad, bias_grad, qkv_grad, proj_grad, fc1_grad, fc2_grad), ("batch", "wide")
    )
    return (block_out, input_grad, totals[0], totals[1], totals[2], totals[3], totals[4], totals[5])


MESH = pl.DeviceIdType.MESH
MM = (((1,), (0,)), ((), ()))
NT = (((1,), (1,)), ((), ()))
TN = (((0,), (0,)), ((), ()))
B16 = jnp.bfloat16
F32 = jnp.float32

STREAMS = (
    (0, 0, 256, "zpqZ"),
    (0, 256, 128, "pqzZ"),
    (0, 384, 256, "pqzZ"),
    (0, 640, 128, "pzZq"),
    (1, 0, 256, "D"),
    (1, 256, 256, "pqzZ"),
    (1, 512, 256, "zpqZ"),
    (2, 0, 256, "pqzZ"),
    (2, 256, 128, "pzqZ"),
    (2, 384, 256, "pqzZ"),
    (2, 640, 128, "zpqZ"),
)
ORDER = (
    -1, -1, -1, -1, -1, -1, -1, -1, 0, 1, 2, 3, -1, -1, -1, 4, 5, 6, -1, 1,
    7, 8, 3, 0, 2, -1, -1, 4, 6, 3, 9, 10, 1, -1, 8, 0, 2, -1, 5, 4,
    1, 7, 6, 3, 9, 10, 0, 8, -1, 2, 5, 3, 6, 4, 7, 1, 8, 10, 9, 0,
    5, -1, 2, 3, 1, 10, 7, 6, 8, 4, 9, 0, 2, 5, 3, 4, 1, 6, 8, 10,
    0, 7, 2, 5, 9, 3, 8, 10, 1, 6, 3, 1, 7, 5, 9, 10, 2, 8, -1, 0,
    2, 8, 7, 0, 6, 9, 5, 6, 5, 7, 10, 9, 7, 10, 9,
)


def dot(left, right, dims):
    return lax.dot_general(left, right, dims, preferred_element_type=F32)


def col_sum(values):
    return jnp.sum(values, axis=0, keepdims=True)


def fused_kernel(
    lengths_in,
    block_in,
    cotangent,
    lead_embed_in,
    b_ada_in,
    w_ada_in,
    w_qkv_in,
    w_proj_in,
    w_fc1_in,
    w_fc2_in,
    out_block,
    out_input,
    out_fc2,
    out_fc1,
    out_qkvp,
    out_mod,
    lengths,
    lead_embed,
    b_ada,
    w_ada,
    w_qkv,
    w_proj,
    w_fc1,
    w_fc2,
    xall,
    gall,
    mod_rows,
    entry,
    normed_own,
    q_all,
    kv_all,
    bias_keys,
    probs,
    inverses,
    mixed,
    branch_ref,
    second_ref,
    active,
    gelu_slope,
    hidden_grad,
    grads_bf,
    send_out,
    entry_send,
    entry_recv,
    qkvp,
    core_out,
    core_in,
    hold,
    stage,
    stage_in,
    total,
    mod_own,
    mod_in,
    mod_all,
    load_sem,
    put_sem,
    x_send,
    x_recv,
    f_send,
    f_recv,
    g_send,
    g_recv,
    o_send,
    o_recv,
    e_send,
    e_recv,
    m_send,
    m_recv,
    c_send,
    c_recv,
    s_send,
    s_recv,
):
    items, span, width = block_in.shape
    own = items * span
    head_pairs = width // 128
    blocks = active.shape[0]
    half_rows = hold.shape[1]
    inv_root = HEAD_DIM**-0.5
    batch, wide = lax.axis_index("batch"), lax.axis_index("wide")
    z, core = wide // 2, wide % 2
    y, x = batch // 2, batch % 2
    zb = z % 2

    def at(y_, x_, z_, core_):
        return (y_ * 2 + x_, z_ * 2 + core_)

    core_peer = at(y, x, z, 1 - core)
    x_peer = at(y, 1 - x, z, core)
    y_peer = at(1 - y, x, z, core)
    xy_peer = at(1 - y, 1 - x, z, core)
    flip_x, flip_y = 1 - 2 * x, 1 - 2 * y
    peers = {
        "p": at(y + flip_y * core, x + flip_x * (1 - core), z, core),
        "q": at(y + flip_y * (1 - core), x + flip_x * core, z, core),
        "z": at(y, x, z + 1 - 2 * zb, core),
        "Z": at(y, x, (z + 2) % items, core),
    }
    sides = {
        "p": x * (1 - core) + y * core,
        "q": y * (1 - core) + x * core,
        "z": zb,
        "Z": z // 2,
    }

    def remote(src, dst, send, recv, device):
        copy = pltpu.make_async_remote_copy(
            src_ref=src,
            dst_ref=dst,
            send_sem=send,
            recv_sem=recv,
            device_id=device,
            device_id_type=MESH,
        )
        copy.start()
        return copy

    def load(src, dst, index):
        copy = pltpu.make_async_copy(src, dst, load_sem.at[index])
        copy.start()
        return copy

    puts = []

    def put(src, dst):
        copy = pltpu.make_async_copy(src, dst, put_sem.at[len(puts)])
        copy.start()
        puts.append(copy)

    barrier = pltpu.get_barrier_semaphore()
    greet = [core_peer, x_peer, y_peer, xy_peer]
    greet += [at(y, x, (z + step) % items, core) for step in range(1, items)]
    for device in greet:
        pl.semaphore_signal(barrier, inc=1, device_id=device, device_id_type=MESH)
    loads = [
        load(block_in.at[z], xall.at[0, z], 0),
        load(w_ada_in, w_ada, 1),
        load(w_qkv_in, w_qkv, 2),
        load(w_proj_in, w_proj, 3),
        load(w_fc1_in, w_fc1, 4),
        load(w_fc2_in, w_fc2, 5),
        load(cotangent.at[z], gall.at[z], 6),
        load(lead_embed_in, lead_embed, 7),
        load(b_ada_in, b_ada, 8),
        load(lengths_in, lengths, 9),
    ]
    pl.semaphore_wait(barrier, len(greet))

    x_copies, g_copies = [], []
    for step in range(1, items):
        there = (z + step) % items
        x_copies.append(
            remote(
                block_in.at[there],
                xall.at[0, z],
                x_send.at[step - 1],
                x_recv.at[step - 1],
                at(y, x, there, core),
            )
        )
    forwards = [
        remote(block_in.at[z], xall.at[1, z], f_send.at[0], f_recv.at[0], core_peer)
    ]

    for index in (7, 8, 9):
        loads[index].wait()
    embed = lead_embed[...].astype(F32)
    condition = (embed / (1.0 + jnp.exp(-embed))).astype(B16)
    loads[1].wait()
    all_rows = dot(condition, w_ada[...], MM) + b_ada[...].astype(F32).reshape(1, -1)
    mine = lax.broadcasted_iota(jnp.int32, (items, 1), 0) == z
    mod_rows[...] = jnp.sum(jnp.where(mine, all_rows, 0.0), axis=0, keepdims=True)
    pieces = [mod_rows[:, column * width : (column + 1) * width] for column in range(6)]
    shift_att, scale_att, gate_att, shift_mlp, scale_mlp, gate_mlp = pieces
    mod_own[...] = jnp.zeros(mod_own.shape, F32)
    inverses[...] = jnp.zeros(inverses.shape, F32)
    mod_own[6:7, :] = jnp.sum(jnp.where(mine, condition.astype(F32), 0.0), axis=0, keepdims=True)

    lane = lax.broadcasted_iota(jnp.int32, (1, 128), 1)
    halves, marks = [], []
    row = lax.broadcasted_iota(jnp.int32, (2 * own, 128), 0)
    block_core = jnp.where(row // own == 0, core, 1 - core)
    position = ((row % own) // span * 2 + block_core) * span + row % span
    bias = jnp.where(position < lengths[z], 0.0, -1e30)
    for half in range(2):
        inside = lane // HEAD_DIM == half
        halves.append(jnp.where(inside, 1.0, 0.0).astype(B16))
        mark = jnp.where(lane == (1 - half) * HEAD_DIM, 1.0, 0.0)
        marks.append(mark.astype(B16))
        bias_keys[half] = (bias * mark).astype(B16)

    loads[0].wait()
    for step in range(1, items):
        came = (z + items - step) % items
        x_copies[step - 1].wait_recv()
        forwards.append(
            remote(
                xall.at[0, came],
                xall.at[1, came],
                f_send.at[step],
                f_recv.at[step],
                core_peer,
            )
        )
    for step in range(1, items):
        there = (z + step) % items
        g_copies.append(
            remote(
                cotangent.at[there],
                gall.at[z],
                g_send.at[step - 1],
                g_recv.at[step - 1],
                at(y, x, there, core),
            )
        )

    loads[2].wait()
    inputs = xall[0].reshape(own, width).astype(F32)
    normed, norm_inverse = norm_rows(inputs)
    normed_own[...] = normed
    entry[:own, :] = (normed * (1.0 + scale_att) + shift_att).astype(B16)
    q_all[...] = (dot(entry[:own, :], w_qkv[:, :width], MM).astype(B16) * inv_root).astype(B16)
    kv_all[:own, :] = dot(entry[:own, :], w_qkv[:, width:], MM).astype(B16)
    for copy in forwards:
        copy.wait_recv()
    other_normed, _ = norm_rows(xall[1].reshape(own, width).astype(F32))
    entry[own:, :] = (other_normed * (1.0 + scale_att) + shift_att).astype(B16)
    kv_all[own:, :] = dot(entry[own:, :], w_qkv[:, width:], MM).astype(B16)

    for pair in range(head_pairs):
        lanes = slice(pair * 128, (pair + 1) * 128)
        v_lanes = slice(width + pair * 128, width + (pair + 1) * 128)
        keys, values, queries = kv_all[:, lanes], kv_all[:, v_lanes], q_all[:, lanes]
        parts = []
        for half in range(2):
            head = pair * 2 + half
            scores = dot(
                keys * halves[half] + bias_keys[half], queries * halves[half] + marks[half], NT
            )
            exp_scores = jnp.exp(scores - jnp.max(scores, axis=0, keepdims=True))
            inverse = 1.0 / jnp.sum(exp_scores, axis=0, keepdims=True)
            inverses[head : head + 1, :] = inverse
            weights = exp_scores.astype(B16)
            probs[head] = weights
            out = dot(values, weights, TN)[half * HEAD_DIM : (half + 1) * HEAD_DIM] * inverse
            parts.append(out)
        mixed[:, lanes] = jnp.concatenate(parts, axis=0).T.astype(B16)

    loads[3].wait()
    branch = dot(mixed[...], w_proj[...], MM)
    middle = inputs + gate_att * branch
    branch_ref[...] = branch
    second_normed, second_inverse = norm_rows(middle)
    second_ref[...] = second_normed
    second = (second_normed * (1.0 + scale_mlp) + shift_mlp).astype(B16)
    grads_bf[0] = second
    loads[4].wait()
    loads[5].wait()
    mlp_out = jnp.zeros((own, width), F32)
    for block in range(blocks):
        columns = slice(block * width, (block + 1) * width)
        hidden = dot(second, w_fc1[:, columns], MM)
        cumulative = 0.5 * (1.0 + lax.erf(hidden * (0.5**0.5)))
        act = (hidden * cumulative).astype(B16)
        active[block] = act
        gelu_slope[block] = cumulative + hidden * (
            jnp.exp(-0.5 * hidden * hidden) * (1.0 / math.sqrt(2.0 * math.pi))
        )
        mlp_out = mlp_out + dot(act, w_fc2[columns, :], MM)

    outs = []

    def give_back(out, which):
        for step in range(1, items):
            there = (z + step) % items
            slot = which * items + step
            outs.append(
                remote(
                    send_out.at[which, there],
                    out.at[z],
                    o_send.at[slot],
                    o_recv.at[slot],
                    at(y, x, there, core),
                )
            )
        put(send_out.at[which, z], out.at[z])

    def rows_of(start, count):
        return pl.ds(pl.multiple_of(start, 16), count)

    core_copies = {}
    core_done = set()
    sent = []

    def core_start(wave, first, count):
        rows = pl.ds(first, count)
        core_copies[wave, first] = remote(
            core_out.at[wave, rows],
            core_in.at[wave, rows],
            c_send.at[len(core_copies)],
            c_recv.at[len(core_copies)],
            core_peer,
        )

    def write_out(wave, at_core, base, count):
        first = at_core * half_rows + base
        if wave == 0:
            rows = rows_of(first, count)
            put(total.at[wave, rows, :], out_fc2.at[rows, :])
            return
        done = 0
        while done < count:
            block, inside = divmod(base + done, width)
            size = min(count - done, width - inside)
            rows, out_rows = rows_of(first + done, size), pl.ds(inside, size)
            if wave == 1:
                columns = pl.ds(pl.multiple_of((at_core * 2 + block) * width, 128), width)
                put(total.at[wave, rows, :], out_fc1.at[out_rows, columns])
            else:
                if block == 0:
                    start, stride = at_core * 3 * width, width - at_core * (width - 128)
                else:
                    start, stride = 128 + at_core * 128, width
                for piece in range(3):
                    columns = pl.ds(pl.multiple_of(start + piece * stride, 128), 128)
                    put(
                        total.at[wave, rows, pl.ds(piece * 128, 128)],
                        out_qkvp.at[out_rows, columns],
                    )
            done += size

    groups = {
        "xy": (y * 2 + x, ((y * 2 + 1 - x, x_peer), (2 - y * 2 + x, y_peer), (3 - y * 2 - x, xy_peer))),
        "z": (
            z,
            tuple(
                ((z + step) % items, at(y, x, (z + step) % items, core)) for step in range(1, items)
            ),
        ),
    }

    def direct(index, wave, base, count, order):
        slot, kept, size, place = 0, base, count, base
        before = core_in
        places = []
        for name in order:
            side, others = groups[name]
            size //= 4
            copies = []
            for number, (other, device) in reversed(list(enumerate(others))):
                away = kept + other * size
                area = pl.ds(place + number * size, size)
                values = hold[wave, rows_of(away, size), :]
                if before is not None:
                    values = values + before[wave, rows_of(away, size), :].astype(F32)
                stage[wave, area, :] = values.astype(B16)
                copies.append(
                    remote(
                        stage.at[wave, area],
                        stage_in.at[wave, area],
                        s_send.at[index, slot],
                        s_recv.at[index, slot],
                        device,
                    )
                )
                slot += 1
            sent.extend(copies)
            kept = kept + side * size
            yield
            for copy in copies:
                copy.wait_recv()
            values = hold[wave, rows_of(kept, size), :]
            if before is not None:
                values = values + before[wave, rows_of(kept, size), :].astype(F32)
            for number in range(3):
                area = pl.ds(place + number * size, size)
                values = values + stage_in[wave, area, :].astype(F32)
            if len(places) == 0:
                hold[wave, rows_of(kept, size), :] = values
            else:
                total[wave, rows_of(core * half_rows + kept, size), :] = values.astype(B16)
            places.append((others, kept, size))
            before, place = None, place + 3 * size
        for others, start, size in reversed(places):
            area = total.at[wave, rows_of(core * half_rows + start, size)]
            copies = []
            for _, device in reversed(others):
                copies.append(
                    remote(area, area, s_send.at[index, slot], s_recv.at[index, slot], device)
                )
                slot += 1
            sent.extend(copies)
            yield
            for copy in copies:
                copy.wait_recv()
        area = total.at[wave, rows_of(core * half_rows + base, count)]
        copy = remote(area, area, s_send.at[index, slot], s_recv.at[index, slot], core_peer)
        sent.append(copy)
        write_out(wave, core, base, count)
        yield
        copy.wait_recv()
        write_out(wave, 1 - core, base, count)

    def stream(index, wave, base, count, dims):
        keys = [first for kept_wave, first in core_copies if kept_wave == wave]
        for key in [first for first in keys if first < base + count]:
            if (wave, key) in core_done:
                continue
            core_done.add((wave, key))
            core_copies[wave, key].wait_recv()
        if dims in "DE":
            yield from direct(index, wave, base, count, ("xy", "z") if dims == "D" else ("z", "xy"))
            return
        slot = 0
        kept, size, place = base, count, base
        before, before_at = core_in, base
        places = []
        for dim in dims[:-1]:
            size //= 2
            away, keep = (1 - sides[dim]) * size, sides[dim] * size
            area = pl.ds(place, size)
            stage[wave, area, :] = (
                hold[wave, rows_of(kept + away, size), :]
                + before[wave, rows_of(before_at + away, size), :].astype(F32)
            ).astype(B16)
            copy = remote(
                stage.at[wave, area],
                stage_in.at[wave, area],
                s_send.at[index, slot],
                s_recv.at[index, slot],
                peers[dim],
            )
            sent.append(copy)
            hold[wave, rows_of(kept + keep, size), :] += before[
                wave, rows_of(before_at + keep, size), :
            ].astype(F32)
            places.append((dim, kept + keep, size))
            kept, slot = kept + keep, slot + 1
            before, before_at, place = stage_in, place, place + size
            yield
            copy.wait_recv()
        area = pl.ds(place, size)
        stage[wave, area, :] = (
            hold[wave, rows_of(kept, size), :]
            + before[wave, rows_of(before_at, size), :].astype(F32)
        ).astype(B16)
        copy = remote(
            stage.at[wave, area],
            stage_in.at[wave, area],
            s_send.at[index, slot],
            s_recv.at[index, slot],
            peers[dims[-1]],
        )
        sent.append(copy)
        slot += 1
        yield
        copy.wait_recv()
        here = core * half_rows
        total[wave, rows_of(here + kept, size), :] = (
            stage[wave, area, :].astype(F32) + stage_in[wave, area, :].astype(F32)
        ).astype(B16)
        for dim, start, size in reversed(places):
            area = total.at[wave, rows_of(here + start, size)]
            copy = remote(area, area, s_send.at[index, slot], s_recv.at[index, slot], peers[dim])
            sent.append(copy)
            slot += 1
            yield
            copy.wait_recv()
        area = total.at[wave, rows_of(here + base, count)]
        copy = remote(area, area, s_send.at[index, slot], s_recv.at[index, slot], core_peer)
        sent.append(copy)
        write_out(wave, core, base, count)
        yield
        copy.wait_recv()
        write_out(wave, 1 - core, base, count)

    def compute():
        per_core = blocks // 2
        block_result = middle + gate_mlp * mlp_out
        send_out[0] = block_result.astype(B16).reshape(items, span, width)
        loads[6].wait()
        for copy in g_copies:
            copy.wait_recv()
        gradient = gall[...].reshape(own, width).astype(F32)
        mlp_grad = (gate_mlp * gradient).astype(B16)
        grads_bf[1] = mlp_grad
        for index in range(per_core):
            block = (1 - core) * per_core + index
            rows = slice(index * width, (index + 1) * width)
            core_out[0, rows, :] = dot(active[block], mlp_grad, TN).astype(B16)
        core_start(0, 0, half_rows)
        yield
        for index in range(per_core):
            block = core * per_core + index
            rows = slice(index * width, (index + 1) * width)
            hold[0, rows, :] = dot(active[block], mlp_grad, TN)
        yield
        second_grad = jnp.zeros((own, width), F32)
        for block in range(blocks):
            columns = slice(block * width, (block + 1) * width)
            active_grad = dot(mlp_grad, w_fc2[columns, :], NT)
            hid = (active_grad * gelu_slope[block]).astype(B16)
            hidden_grad[block] = hid
            second_grad = second_grad + dot(hid, w_fc1[:, columns], NT)
            yield
        for index in range(per_core):
            block = (1 - core) * per_core + index
            rows = slice(index * width, (index + 1) * width)
            core_out[1, rows, :] = dot(grads_bf[0], hidden_grad[block], TN).astype(B16)
        core_start(1, 0, half_rows)
        yield
        for index in range(per_core):
            block = core * per_core + index
            rows = slice(index * width, (index + 1) * width)
            hold[1, rows, :] = dot(grads_bf[0], hidden_grad[block], TN)
        yield
        second_normed = second_ref[...]
        middle_grad = gradient + norm_back(
            second_normed, second_inverse, second_grad * (1.0 + scale_mlp)
        )
        branch_grad = (gate_att * middle_grad).astype(B16)
        grads_bf[2] = dot(branch_grad, w_proj[...], NT).astype(B16)
        qkvp[3] = dot(mixed[...], branch_grad, TN)
        yield
        mod_own[5:6, :] = col_sum(gradient * mlp_out)
        mod_own[4:5, :] = col_sum(second_grad * second_normed)
        mod_own[3:4, :] = col_sum(second_grad)
        mod_own[2:3, :] = col_sum(middle_grad * branch_ref[...])
        yield

        dq, dkv = q_all, kv_all
        inverse_columns = inverses[...].T
        for pair in range(head_pairs):
            lanes = slice(pair * 128, (pair + 1) * 128)
            v_lanes = slice(width + pair * 128, width + (pair + 1) * 128)
            keys, values, queries = kv_all[:, lanes], kv_all[:, v_lanes], q_all[:, lanes]
            out_grad = grads_bf[2, :, lanes].astype(F32)
            parts = []
            key_grad = jnp.zeros((2 * own, 128), F32)
            value_grad = jnp.zeros((2 * own, 128), F32)
            for half in range(2):
                head = pair * 2 + half
                masked_grad = (
                    out_grad * inverse_columns[:, head : head + 1] * halves[half].astype(F32)
                ).astype(B16)
                weights = probs[head]
                wide_weights = weights.astype(F32)
                weight_grad = dot(values, masked_grad, NT)
                row_sum = col_sum(wide_weights * weight_grad) * inverses[head : head + 1, :]
                score_grad = (wide_weights * (weight_grad - row_sum)).astype(B16)
                value_grad = value_grad + dot(weights, masked_grad, MM)
                key_grad = key_grad + dot(score_grad, queries * halves[half], MM)
                query_grad = dot(keys, score_grad, TN)
                parts.append(query_grad[half * HEAD_DIM : (half + 1) * HEAD_DIM])
            query_grad = jnp.concatenate(parts, axis=0).T * inv_root
            dq[:, lanes] = query_grad.astype(B16)
            dkv[:, lanes] = key_grad.astype(B16)
            dkv[:, v_lanes] = value_grad.astype(B16)
            qkvp[pair, :, :128] = dot(entry[:own, :], dq[:, lanes], TN)
            qkvp[pair, :, 128:256] = dot(entry[...], dkv[:, lanes], TN)
            qkvp[pair, :, 256:] = dot(entry[...], dkv[:, v_lanes], TN)
            if pair == 0:
                core_out[2, :width, :] = qkvp[3 * (1 - core)].astype(B16)
                core_start(2, 0, width)
                hold[2, :width, :] = qkvp[3 * core]
            elif pair == 2:
                core_out[2, width:, :] = qkvp[2 - core].astype(B16)
                core_start(2, width, width)
                hold[2, width:, :] = qkvp[1 + core]
            yield

        entry_send[...] = dot(dkv[own:, :], w_qkv[:, width:], NT)
        entry_copy = remote(entry_send, entry_recv, e_send.at[0], e_recv.at[0], core_peer)
        sent.append(entry_copy)
        entry_grad = dot(dkv[:own, :], w_qkv[:, width:], NT) + dot(dq[...], w_qkv[:, :width], NT)
        yield
        entry_copy.wait_recv()
        entry_grad = entry_grad + entry_recv[...]
        normed = normed_own[...]
        mod_own[1:2, :] = col_sum(entry_grad * normed)
        mod_own[0:1, :] = col_sum(entry_grad)
        mod_copy = remote(mod_own, mod_in, m_send.at[0], m_recv.at[0], core_peer)
        sent.append(mod_copy)
        input_grad = middle_grad + norm_back(
            normed, norm_inverse, entry_grad * (1.0 + scale_att)
        )
        send_out[1] = input_grad.astype(B16).reshape(items, span, width)
        yield
        mod_copy.wait_recv()
        first_row = batch * items
        weight = jnp.where(lax.broadcasted_iota(jnp.int32, mod_own.shape, 0) == 6, 0.5, 1.0)
        mod_all[first_row + z] = (mod_own[...] + mod_in[...]) * weight
        mod_copies = []
        for step in range(1, items):
            place = mod_all.at[first_row + z]
            there = at(y, x, (z + step) % items, core)
            mod_copies.append(remote(place, place, m_send.at[step], m_recv.at[step], there))
        sent.extend(mod_copies)
        yield
        for copy in mod_copies:
            copy.wait_recv()
        mod_copies = []
        for index, device in enumerate((x_peer, y_peer, xy_peer)):
            place = mod_all.at[pl.ds(first_row, items)]
            slot = items + index
            mod_copies.append(remote(place, place, m_send.at[slot], m_recv.at[slot], device))
        sent.extend(mod_copies)
        yield
        for copy in mod_copies:
            copy.wait_recv()
        put(mod_all, out_mod)
        yield
        give_back(out_block, 0)
        give_back(out_input, 1)

    steps = compute()
    streams = [stream(index, *what) for index, what in enumerate(STREAMS)]
    for step in ORDER:
        next(steps if step < 0 else streams[step], None)
    for rest in [steps] + streams:
        for _ in rest:
            raise AssertionError

    for copy in x_copies + g_copies + forwards + list(core_copies.values()) + sent:
        copy.wait_send()
    for copy in outs + puts:
        copy.wait()


def widen_kernel(
    mod_in,
    block_in_,
    input_in,
    fc2_in,
    fc1_in,
    qkvp_in,
    block_out,
    input_out,
    ada_out,
    bias_out,
    qkv_out,
    proj_out,
    fc1_out,
    fc2_out,
    block_16,
    input_16,
    fc2_16,
    fc1_16,
    qkvp_16,
    mod,
    block_32,
    input_32,
    ada_32,
    bias_32,
    qkvp_32,
    fc1_32,
    fc2_32,
    by_piece,
    in_sem,
    out_sem,
):
    width = fc1_in.shape[0]
    pairs = (
        (fc2_in, fc2_16),
        (fc1_in, fc1_16),
        (qkvp_in, qkvp_16),
        (block_in_, block_16),
        (input_in, input_16),
    )
    rows_load = pltpu.make_async_copy(mod_in, mod, in_sem.at[5])
    rows_load.start()
    loads = []
    for index, (src, dst) in enumerate(pairs):
        copy = pltpu.make_async_copy(src, dst, in_sem.at[index])
        copy.start()
        loads.append(copy)
    stores = []

    def store(src, dst):
        copy = pltpu.make_async_copy(src, dst, out_sem.at[len(stores)])
        copy.start()
        stores.append(copy)

    rows_load.wait()
    count = mod.shape[0] // 8
    for piece in range(7):
        for item in range(count):
            by_piece[piece, item : item + 1, :] = mod[item * 8 + piece : item * 8 + piece + 1, :]
    conditions = jnp.concatenate([by_piece[6].astype(B16)] * 3, axis=0)
    for piece in range(6):
        columns = slice(piece * width, (piece + 1) * width)
        rows = by_piece[piece]
        bias_32[columns] = jnp.sum(rows, axis=0)
        high = rows.astype(B16)
        rest = rows - high.astype(F32)
        middle = rest.astype(B16)
        low = (rest - middle.astype(F32)).astype(B16)
        parts = jnp.concatenate([high, middle, low], axis=0)
        ada_32[:, columns] = dot(conditions, parts, TN)
        store(ada_32.at[:, pl.ds(piece * width, width)], ada_out.at[:, pl.ds(piece * width, width)])
    store(bias_32, bias_out)
    loads[0].wait()
    fc2_32[...] = fc2_16[...].astype(F32)
    store(fc2_32, fc2_out)
    loads[1].wait()
    fc1_32[...] = fc1_16[...].astype(F32)
    store(fc1_32, fc1_out)
    loads[2].wait()
    qkvp_32[...] = qkvp_16[...].astype(F32)
    store(qkvp_32.at[:, pl.ds(0, 3 * width)], qkv_out)
    store(qkvp_32.at[:, pl.ds(3 * width, width)], proj_out)
    loads[3].wait()
    block_32[...] = block_16[...].astype(F32)
    store(block_32, block_out)
    loads[4].wait()
    input_32[...] = input_16[...].astype(F32)
    store(input_32, input_out)
    for copy in stores:
        copy.wait()


def widen(mod, out_block, out_input, fc2_sum, fc1_sum, qkvp_sum):
    width, hidden = fc1_sum.shape
    arrays = (out_block, out_input, fc2_sum, fc1_sum, qkvp_sum)
    out_shapes = (
        out_block.shape,
        out_input.shape,
        (width, 6 * width),
        (6 * width,),
        (width, 3 * width),
        (width, width),
        fc1_sum.shape,
        fc2_sum.shape,
    )
    wide = (
        out_block.shape,
        out_input.shape,
        (width, 6 * width),
        (6 * width,),
        qkvp_sum.shape,
        fc1_sum.shape,
        fc2_sum.shape,
    )
    hbm = pl.BlockSpec(memory_space=pl.ANY)
    return pl.pallas_call(
        widen_kernel,
        out_shape=tuple(jax.ShapeDtypeStruct(shape, F32) for shape in out_shapes),
        in_specs=[hbm] * 6,
        out_specs=(hbm,) * 8,
        scratch_shapes=[pltpu.VMEM(array.shape, B16) for array in arrays]
        + [pltpu.VMEM(mod.shape, F32)]
        + [pltpu.VMEM(shape, F32) for shape in wide]
        + [pltpu.VMEM((7, mod.shape[0] // 8, width), F32)]
        + [pltpu.SemaphoreType.DMA((6,)), pltpu.SemaphoreType.DMA((13,))],
        name="widen",
        compiler_params=pltpu.CompilerParams(vmem_limit_bytes=60 * 2**20),
    )(mod, *arrays)


def fused(block_in, lead_embed, lengths, w_ada, b_ada, w_qkv, w_proj, w_fc1, w_fc2, cotangent):
    items, span, width = block_in.shape
    hidden = w_fc1.shape[1]
    groups = lax.axis_size("batch")
    own = items * span
    blocks = hidden // width
    half = hidden // 2
    waves = 3
    hbm = pl.BlockSpec(memory_space=pl.ANY)
    dma = pltpu.SemaphoreType.DMA
    scratch = [
        pltpu.SMEM(lengths.shape, jnp.int32),
        pltpu.VMEM(lead_embed.shape, B16),
        pltpu.VMEM(b_ada.shape, B16),
        pltpu.VMEM(w_ada.shape, B16),
        pltpu.VMEM(w_qkv.shape, B16),
        pltpu.VMEM(w_proj.shape, B16),
        pltpu.VMEM(w_fc1.shape, B16),
        pltpu.VMEM(w_fc2.shape, B16),
        pltpu.VMEM((2, items, span, width), B16),
        pltpu.VMEM((items, span, width), B16),
        pltpu.VMEM((1, 6 * width), F32),
        pltpu.VMEM((2 * own, width), B16),
        pltpu.VMEM((own, width), F32),
        pltpu.VMEM((own, width), B16),
        pltpu.VMEM((2 * own, 2 * width), B16),
        pltpu.VMEM((2, 2 * own, 128), B16),
        pltpu.VMEM((HEADS, 2 * own, own), B16),
        pltpu.VMEM((8, own), F32),
        pltpu.VMEM((own, width), B16),
        pltpu.VMEM((own, width), F32),
        pltpu.VMEM((own, width), F32),
        pltpu.VMEM((blocks, own, width), B16),
        pltpu.VMEM((blocks, own, width), F32),
        pltpu.VMEM((blocks, own, width), B16),
        pltpu.VMEM((3, own, width), B16),
        pltpu.VMEM((2, items, span, width), B16),
        pltpu.VMEM((own, width), F32),
        pltpu.VMEM((own, width), F32),
        pltpu.VMEM((blocks, width, width), F32),
        pltpu.VMEM((waves, half, width), B16),
        pltpu.VMEM((waves, half, width), B16),
        pltpu.VMEM((waves, half, width), F32),
        pltpu.VMEM((waves, half, width), B16),
        pltpu.VMEM((waves, half, width), B16),
        pltpu.VMEM((waves, hidden, width), B16),
        pltpu.VMEM((8, width), F32),
        pltpu.VMEM((8, width), F32),
        pltpu.VMEM((groups * items, 8, width), F32),
        dma((10,)),
        dma((3 + 6 * len(STREAMS),)),
    ]
    for count in (items - 1, items, items - 1, 2 * items, 1, items + 3, 4):
        scratch += [dma((count,))] * 2
    scratch += [dma((len(STREAMS), 13))] * 2
    out_block, out_input, fc2_sum, fc1_sum, qkvp_sum, mod = pl.pallas_call(
        fused_kernel,
        out_shape=(
            jax.ShapeDtypeStruct(block_in.shape, B16),
            jax.ShapeDtypeStruct(block_in.shape, B16),
            jax.ShapeDtypeStruct((hidden, width), B16),
            jax.ShapeDtypeStruct((width, hidden), B16),
            jax.ShapeDtypeStruct((width, 4 * width), B16),
            jax.ShapeDtypeStruct((groups * items, 8, width), F32),
        ),
        in_specs=[hbm] * 10,
        out_specs=(hbm,) * 6,
        scratch_shapes=scratch,
        name="fused_block",
        compiler_params=pltpu.CompilerParams(
            collective_id=0, has_side_effects=True, vmem_limit_bytes=56 * 2**20
        ),
    )(
        lengths,
        block_in,
        cotangent,
        lead_embed,
        b_ada,
        w_ada,
        w_qkv,
        w_proj,
        w_fc1,
        w_fc2,
    )
    return widen(
        mod.reshape(groups * items * 8, width), out_block, out_input, fc2_sum, fc1_sum, qkvp_sum
    )


def choose(*arrays):
    items, span, width = arrays[0].shape
    fits = (
        lax.axis_size("batch") == 4
        and items == 4
        and lax.axis_size("wide") == 2 * items
        and span == 64
        and width == HEADS * HEAD_DIM == 384
        and arrays[7].shape[1] == 4 * width
    )
    return (fused if fits else on_device)(*arrays)


def solution(mesh):
    return jax.shard_map(
        choose,
        mesh=mesh,
        in_specs=(
            P("batch", "wide", None),
            P("batch", None),
            P("batch"),
            P(),
            P(),
            P(),
            P(),
            P(),
            P(),
            P("batch", "wide", None),
        ),
        out_specs=(
            P("batch", "wide", None),
            P("batch", "wide", None),
            P(),
            P(),
            P(),
            P(),
            P(),
            P(),
        ),
        check_vma=False,
    )
```

```python
import math
from functools import partial

import jax
import jax.numpy as jnp
from jax import lax
from jax.experimental import pallas as pl
from jax.experimental.pallas import tpu as pltpu
from jax.sharding import PartitionSpec as P

HEADS = 6
HEAD_DIM = 64


EPS = 1e-06


def norm_rows(values):
    center = values - jnp.mean(values, axis=-1, keepdims=True)
    inverse = lax.rsqrt(jnp.mean(center * center, axis=-1, keepdims=True) + EPS)
    return (center * inverse, inverse)


def norm_back(normed, inverse, gradient):
    return inverse * (
        gradient
        - jnp.mean(gradient, axis=-1, keepdims=True)
        - normed * jnp.mean(gradient * normed, axis=-1, keepdims=True)
    )


def to_heads(tokens, part_count, head_count, head_size):
    item_count, span_len, _ = tokens.shape
    shaped = tokens.reshape(item_count, span_len, part_count, head_count, head_size)
    return shaped.transpose(2, 0, 3, 1, 4).reshape(
        part_count, item_count * head_count, span_len * head_size
    )


def from_heads(blocks, item_count, head_count, head_size):
    part_count = blocks.shape[0]
    span_len = blocks.shape[2] // head_size
    shaped = blocks.reshape(part_count, item_count, head_count, span_len, head_size)
    return shaped.transpose(1, 3, 0, 2, 4).reshape(
        item_count, span_len, part_count * head_count * head_size
    )


def split_rows(values, block_rows):
    pair_count, slot_len = (values.shape[0], values.shape[1])
    rest = values.shape[2:]
    shaped = values.reshape((pair_count, slot_len // block_rows, block_rows) + rest)
    return jnp.moveaxis(shaped, 1, 0)


def join_rows(values):
    merged = jnp.moveaxis(values, 0, 1)
    return merged.reshape((merged.shape[0], merged.shape[1] * merged.shape[2]) + merged.shape[3:])


def masked_scores(query_block, keys_all, key_valid, inv_root):
    scores = (
        jnp.einsum("pqd,pkd->pqk", query_block, keys_all, preferred_element_type=jnp.float32)
        * inv_root
    )
    return jnp.where(key_valid[:, None, :], scores, -1e30)


def attend_forward(queries, keys_all, values, key_valid, inv_root):
    block_rows = min(512, queries.shape[1])

    def one_block(query_block):
        scores = masked_scores(query_block, keys_all, key_valid, inv_root)
        row_peak = jnp.max(scores, axis=-1, keepdims=True)
        exp_scores = jnp.exp(scores - row_peak)
        row_total = jnp.sum(exp_scores, axis=-1, keepdims=True)
        weights = (exp_scores / row_total).astype(jnp.bfloat16)
        outcome = jnp.einsum("pqk,pkd->pqd", weights, values, preferred_element_type=jnp.float32)
        return (outcome.astype(jnp.bfloat16), (row_peak + jnp.log(row_total))[..., 0])

    outputs, logsum = lax.map(one_block, split_rows(queries, block_rows))
    return (join_rows(outputs), join_rows(logsum))


def attend_backward(queries, keys_all, values, out_grad, logsum, key_valid, inv_root):
    block_rows = min(512, queries.shape[1])
    zeros = jnp.zeros(keys_all.shape, jnp.float32)

    def one_block(carried, packed):
        key_grad, value_grad = carried
        query_block, grad_block, logsum_block = packed
        scores = masked_scores(query_block, keys_all, key_valid, inv_root)
        weights = jnp.exp(scores - logsum_block[..., None])
        weight_grad = jnp.einsum(
            "pqd,pkd->pqk", grad_block, values, preferred_element_type=jnp.float32
        )
        score_grad = weights * (
            weight_grad - jnp.sum(weights * weight_grad, axis=-1, keepdims=True)
        )
        score_grad = score_grad.astype(jnp.bfloat16)
        query_grad = (
            jnp.einsum("pqk,pkd->pqd", score_grad, keys_all, preferred_element_type=jnp.float32)
            * inv_root
        )
        key_grad = (
            key_grad
            + jnp.einsum(
                "pqk,pqd->pkd", score_grad, query_block, preferred_element_type=jnp.float32
            )
            * inv_root
        )
        value_grad = value_grad + jnp.einsum(
            "pqk,pqd->pkd",
            weights.astype(jnp.bfloat16),
            grad_block,
            preferred_element_type=jnp.float32,
        )
        return ((key_grad, value_grad), query_grad)

    packed = (
        split_rows(queries, block_rows),
        split_rows(out_grad, block_rows),
        split_rows(logsum, block_rows),
    )
    (key_grad, value_grad), query_grads = lax.scan(one_block, (zeros, zeros), packed)
    return jnp.stack([join_rows(query_grads), key_grad, value_grad]).astype(jnp.bfloat16)


def on_device(block_in, lead_embed, lengths, w_ada, b_ada, w_qkv, w_proj, w_fc1, w_fc2, cotangent):
    item_count, span_len, width = block_in.shape
    head_count = HEADS
    head_size = HEAD_DIM
    shards = lax.axis_size("wide")
    pair_count = item_count * head_count // shards
    slot_len = span_len * shards
    inv_root = HEAD_DIM ** (-0.5)
    inputs = block_in.astype(jnp.float32)
    condition = jax.nn.silu(lead_embed.astype(jnp.float32)).astype(jnp.bfloat16)
    modulation = jnp.dot(condition, w_ada, preferred_element_type=jnp.float32) + b_ada.astype(
        jnp.float32
    )
    pieces = [modulation[:, None, column * width : (column + 1) * width] for column in range(6)]
    shift_att, scale_att, gate_att, shift_mlp, scale_mlp, gate_mlp = pieces
    normed, norm_inverse = norm_rows(inputs)
    entry = (normed * (1.0 + scale_att) + shift_att).astype(jnp.bfloat16)
    triple = jnp.dot(entry, w_qkv, preferred_element_type=jnp.float32).astype(jnp.bfloat16)
    arrived = lax.all_to_all(
        to_heads(triple, 3, head_count, head_size), "wide", split_axis=1, concat_axis=2, tiled=True
    )
    heads_in = arrived.reshape(3, pair_count, slot_len, head_size)
    pair_ids = lax.axis_index("wide") * pair_count + jnp.arange(pair_count, dtype=jnp.int32)
    item_ids = pair_ids // head_count
    pair_length = jnp.sum(
        jnp.where(
            jnp.arange(item_count, dtype=jnp.int32)[None, :] == item_ids[:, None],
            lengths[None, :],
            0,
        ),
        axis=1,
    )
    key_valid = jnp.arange(slot_len, dtype=jnp.int32)[None, :] < pair_length[:, None]
    mixed_heads, logsum = attend_forward(heads_in[0], heads_in[1], heads_in[2], key_valid, inv_root)
    returned = lax.all_to_all(
        mixed_heads.reshape(pair_count, slot_len * head_size),
        "wide",
        split_axis=1,
        concat_axis=0,
        tiled=True,
    )
    mixed_tok = from_heads(returned[None], item_count, head_count, head_size)
    branch = jnp.dot(mixed_tok, w_proj, preferred_element_type=jnp.float32)
    middle = inputs + gate_att * branch
    second_normed, second_inverse = norm_rows(middle)
    second = (second_normed * (1.0 + scale_mlp) + shift_mlp).astype(jnp.bfloat16)
    hidden = jnp.dot(second, w_fc1, preferred_element_type=jnp.float32)
    active = jax.nn.gelu(hidden, approximate=False).astype(jnp.bfloat16)
    mlp_out = jnp.dot(active, w_fc2, preferred_element_type=jnp.float32)
    block_out = middle + gate_mlp * mlp_out
    gradient = cotangent.astype(jnp.float32)
    mlp_grad = (gate_mlp * gradient).astype(jnp.bfloat16)
    gate_mlp_grad = jnp.sum(gradient * mlp_out, axis=1)
    fc2_grad = jnp.einsum("isf,isd->fd", active, mlp_grad, preferred_element_type=jnp.float32)
    active_grad = jnp.dot(mlp_grad, w_fc2.T, preferred_element_type=jnp.float32)
    hidden_grad = jax.vjp(partial(jax.nn.gelu, approximate=False), hidden)[1](active_grad)[0]
    hidden_grad = hidden_grad.astype(jnp.bfloat16)
    fc1_grad = jnp.einsum("isd,isf->df", second, hidden_grad, preferred_element_type=jnp.float32)
    second_grad = jnp.dot(hidden_grad, w_fc1.T, preferred_element_type=jnp.float32)
    scale_mlp_grad = jnp.sum(second_grad * second_normed, axis=1)
    shift_mlp_grad = jnp.sum(second_grad, axis=1)
    middle_grad = gradient + norm_back(
        second_normed, second_inverse, second_grad * (1.0 + scale_mlp)
    )
    branch_grad = (gate_att * middle_grad).astype(jnp.bfloat16)
    gate_att_grad = jnp.sum(middle_grad * branch, axis=1)
    proj_grad = jnp.einsum(
        "isd,ise->de", mixed_tok, branch_grad, preferred_element_type=jnp.float32
    )
    mixed_grad = jnp.dot(branch_grad, w_proj.T, preferred_element_type=jnp.float32).astype(
        jnp.bfloat16
    )
    heads_grad = lax.all_to_all(
        to_heads(mixed_grad, 1, head_count, head_size)[0],
        "wide",
        split_axis=0,
        concat_axis=1,
        tiled=True,
    )
    heads_grad = heads_grad.reshape(pair_count, slot_len, head_size)
    again_in, _ = lax.optimization_barrier((inputs, heads_grad))
    again_normed, _ = norm_rows(again_in)
    again_entry = (again_normed * (1.0 + scale_att) + shift_att).astype(jnp.bfloat16)
    again_triple = jnp.dot(again_entry, w_qkv, preferred_element_type=jnp.float32).astype(
        jnp.bfloat16
    )
    again_heads = lax.all_to_all(
        to_heads(again_triple, 3, head_count, head_size),
        "wide",
        split_axis=1,
        concat_axis=2,
        tiled=True,
    )
    used_heads = again_heads.reshape(3, pair_count, slot_len, head_size)
    triple_grad = attend_backward(
        used_heads[0], used_heads[1], used_heads[2], heads_grad, logsum, key_valid, inv_root
    )
    sent_back = lax.all_to_all(
        triple_grad.reshape(3, pair_count, slot_len * head_size),
        "wide",
        split_axis=2,
        concat_axis=1,
        tiled=True,
    )
    token_grad = from_heads(sent_back, item_count, head_count, head_size)
    qkv_grad = jnp.einsum("isd,ise->de", entry, token_grad, preferred_element_type=jnp.float32)
    entry_grad = jnp.dot(token_grad, w_qkv.T, preferred_element_type=jnp.float32)
    scale_att_grad = jnp.sum(entry_grad * normed, axis=1)
    shift_att_grad = jnp.sum(entry_grad, axis=1)
    input_grad = middle_grad + norm_back(normed, norm_inverse, entry_grad * (1.0 + scale_att))
    modulation_grad = jnp.concatenate(
        [
            shift_att_grad,
            scale_att_grad,
            gate_att_grad,
            shift_mlp_grad,
            scale_mlp_grad,
            gate_mlp_grad,
        ],
        axis=-1,
    )
    ada_grad = jnp.dot(
        condition.astype(jnp.float32).T, modulation_grad, precision=lax.Precision.HIGHEST
    )
    bias_grad = jnp.sum(modulation_grad, axis=0)
    totals = lax.psum(
        (ada_grad, bias_grad, qkv_grad, proj_grad, fc1_grad, fc2_grad), ("batch", "wide")
    )
    return (block_out, input_grad, totals[0], totals[1], totals[2], totals[3], totals[4], totals[5])


MESH = pl.DeviceIdType.MESH
MM = (((1,), (0,)), ((), ()))
NT = (((1,), (1,)), ((), ()))
TN = (((0,), (0,)), ((), ()))
B16 = jnp.bfloat16
F32 = jnp.float32

STREAMS = (
    (0, 0, 256, "zpqZ"),
    (0, 256, 128, "pqzZ"),
    (0, 384, 256, "pqzZ"),
    (0, 640, 128, "pzZq"),
    (1, 0, 256, "XW"),
    (1, 256, 256, "pqzZ"),
    (1, 512, 256, "zpqZ"),
    (2, 0, 256, "pqzZ*"),
    (2, 256, 128, "pzqZ"),
    (2, 384, 256, "pqzZ*"),
    (2, 640, 128, "zpqZ*"),
)
ORDER = (
    -1, -1, -1, -1, -1, -1, -1, -1, 0, 1, 2, 3, -1, -1, -1, 4, 5, 6, -1, 1,
    7, 8, 3, 0, 2, -1, -1, 6, 4, 3, 9, 10, 1, -1, 8, 0, 2, 5, -1, 6,
    7, 4, 1, 3, 9, 0, 10, 5, 8, 2, 6, -1, 7, 3, 9, 10, 8, 4, 1, 5,
    -1, 0, 10, 3, 7, 1, 9, 2, 6, 8, 4, 0, 5, 10, 4, 1, 3, 6, 8, 7,
    2, 0, 9, 5, 10, 1, 8, 3, 6, 7, 2, 1, 5, 3, 9, 8, -1, 10, 8, 0,
    10, 0, 6, 7, 6, 9, 7, 2, 5, 9, 2, 5,
)


def copies_in(dims):
    steps = dims.rstrip("*")
    back = len(steps) - (steps[-1] not in "XW") - (dims[-1] == "*")
    return len(steps) + back + 1


def dot(left, right, dims):
    return lax.dot_general(left, right, dims, preferred_element_type=F32)


def col_sum(values):
    return jnp.sum(values, axis=0, keepdims=True)


def fused_kernel(
    lengths_in,
    block_in,
    cotangent,
    lead_embed_in,
    b_ada_in,
    w_ada_in,
    w_qkv_in,
    w_proj_in,
    w_fc1_in,
    w_fc2_in,
    out_block,
    out_input,
    total,
    mod_all,
    lengths,
    lead_embed,
    b_ada,
    w_ada,
    w_qkv,
    w_proj,
    w_fc1,
    w_fc2,
    xall,
    gall,
    mod_rows,
    entry,
    normed_own,
    q_all,
    kv_all,
    bias_keys,
    probs,
    inverses,
    mixed,
    branch_ref,
    second_ref,
    active,
    gelu_slope,
    hidden_grad,
    grads_bf,
    send_out,
    entry_send,
    entry_recv,
    qkvp,
    core_out,
    core_in,
    hold,
    stage,
    stage_in,
    mod_own,
    mod_in,
    load_sem,
    send_sem,
    x_recv,
    group_recv,
    c_recv,
    s_recv,
):
    items, span, width = block_in.shape
    own = items * span
    head_pairs = width // 128
    blocks = active.shape[0]
    half_rows = hold.shape[1]
    inv_root = HEAD_DIM**-0.5
    batch, wide = lax.axis_index("batch"), lax.axis_index("wide")
    z, core = wide // 2, wide % 2
    y, x = batch // 2, batch % 2
    zb = z % 2

    def at(y_, x_, z_, core_):
        return (y_ * 2 + x_, z_ * 2 + core_)

    core_peer = at(y, x, z, 1 - core)
    x_peer = at(y, 1 - x, z, core)
    y_peer = at(1 - y, x, z, core)
    xy_peer = at(1 - y, 1 - x, z, core)
    flip_x, flip_y = 1 - 2 * x, 1 - 2 * y
    peers = {
        "p": at(y + flip_y * core, x + flip_x * (1 - core), z, core),
        "q": at(y + flip_y * (1 - core), x + flip_x * core, z, core),
        "z": at(y, x, z + 1 - 2 * zb, core),
        "Z": at(y, x, (z + 2) % items, core),
    }
    sides = {
        "p": x * (1 - core) + y * core,
        "q": y * (1 - core) + x * core,
        "z": zb,
        "Z": z // 2,
    }

    sent_rows = {}

    def remote(src, dst, send, rows, recv, device):
        sent_rows[send] = sent_rows.get(send, 0) + rows
        copy = pltpu.make_async_remote_copy(
            src_ref=src,
            dst_ref=dst,
            send_sem=send_sem.at[send],
            recv_sem=recv,
            device_id=device,
            device_id_type=MESH,
        )
        copy.start()
        return copy

    def load(src, dst, index):
        copy = pltpu.make_async_copy(src, dst, load_sem.at[index])
        copy.start()
        return copy

    def wait_rows(sem, rows):
        planes = next(p for p in (1, 2, 3) if rows % (16 * p) == 0 and rows <= p * total.shape[1])
        area = total.at[pl.ds(0, planes), pl.ds(0, rows // planes)]
        pltpu.make_async_copy(area, area, sem).wait()

    barrier = pltpu.get_barrier_semaphore()
    greet = [core_peer, x_peer, y_peer, xy_peer]
    greet += [at(y, x, (z + step) % items, core) for step in range(1, items)]
    for device in greet:
        pl.semaphore_signal(barrier, inc=1, device_id=device, device_id_type=MESH)
    loads = [
        load(block_in.at[z], xall.at[0, z], 0),
        load(w_ada_in, w_ada, 1),
        load(w_qkv_in, w_qkv, 2),
        load(w_proj_in, w_proj, 3),
        load(w_fc1_in, w_fc1, 4),
        load(w_fc2_in, w_fc2, 5),
        load(cotangent.at[z], gall.at[z], 6),
        load(lead_embed_in, lead_embed, 7),
        load(b_ada_in, b_ada, 8),
        load(lengths_in, lengths, 9),
    ]
    pl.semaphore_wait(barrier, len(greet))

    x_copies = []
    for step in range(1, items):
        there = (z + step) % items
        x_copies.append(
            remote(
                block_in.at[there],
                xall.at[0, z],
                0,
                span,
                x_recv.at[step - 1],
                at(y, x, there, core),
            )
        )
    remote(block_in.at[z], xall.at[1, z], 0, span, group_recv.at[0], core_peer)

    for index in (7, 8, 9):
        loads[index].wait()
    embed = lead_embed[...].astype(F32)
    condition = (embed / (1.0 + jnp.exp(-embed))).astype(B16)
    loads[1].wait()
    all_rows = dot(condition, w_ada[...], MM) + b_ada[...].astype(F32).reshape(1, -1)
    mine = lax.broadcasted_iota(jnp.int32, (items, 1), 0) == z
    mod_rows[...] = jnp.sum(jnp.where(mine, all_rows, 0.0), axis=0, keepdims=True)
    pieces = [mod_rows[:, column * width : (column + 1) * width] for column in range(6)]
    shift_att, scale_att, gate_att, shift_mlp, scale_mlp, gate_mlp = pieces
    mod_own[...] = jnp.zeros(mod_own.shape, F32)
    inverses[...] = jnp.zeros(inverses.shape, F32)
    mod_own[6:7, :] = jnp.sum(jnp.where(mine, condition.astype(F32), 0.0), axis=0, keepdims=True)

    lane = lax.broadcasted_iota(jnp.int32, (1, 128), 1)
    halves, marks = [], []
    row = lax.broadcasted_iota(jnp.int32, (2 * own, 128), 0)
    block_core = jnp.where(row // own == 0, core, 1 - core)
    position = ((row % own) // span * 2 + block_core) * span + row % span
    bias = jnp.where(position < lengths[z], 0.0, -1e30)
    for half in range(2):
        inside = lane // HEAD_DIM == half
        halves.append(jnp.where(inside, 1.0, 0.0).astype(B16))
        mark = jnp.where(lane == (1 - half) * HEAD_DIM, 1.0, 0.0)
        marks.append(mark.astype(B16))
        bias_keys[half] = (bias * mark).astype(B16)

    loads[0].wait()
    for step in range(1, items):
        came = (z + items - step) % items
        x_copies[step - 1].wait_recv()
        remote(
            xall.at[0, came],
            xall.at[1, came],
            0,
            span,
            group_recv.at[0],
            core_peer,
        )
    for step in range(1, items):
        there = (z + step) % items
        remote(
            cotangent.at[there],
            gall.at[z],
            0,
            span,
            group_recv.at[1],
            at(y, x, there, core),
        )

    loads[2].wait()
    inputs = xall[0].reshape(own, width).astype(F32)
    normed, norm_inverse = norm_rows(inputs)
    normed_own[...] = normed
    entry[:own, :] = (normed * (1.0 + scale_att) + shift_att).astype(B16)
    q_all[...] = (dot(entry[:own, :], w_qkv[:, :width], MM).astype(B16) * inv_root).astype(B16)
    kv_all[:own, :] = dot(entry[:own, :], w_qkv[:, width:], MM).astype(B16)
    wait_rows(group_recv.at[0], own)
    other_normed, _ = norm_rows(xall[1].reshape(own, width).astype(F32))
    entry[own:, :] = (other_normed * (1.0 + scale_att) + shift_att).astype(B16)
    kv_all[own:, :] = dot(entry[own:, :], w_qkv[:, width:], MM).astype(B16)

    def head_scores(head):
        pair, half = divmod(head, 2)
        lanes = slice(pair * 128, (pair + 1) * 128)
        return dot(
            kv_all[:, lanes] * halves[half] + bias_keys[half],
            q_all[:, lanes] * halves[half] + marks[half],
            NT,
        )

    scores, parts = head_scores(0), []
    for head in range(HEADS):
        pair, half = divmod(head, 2)
        following = head_scores(head + 1) if head + 1 < HEADS else None
        exp_scores = jnp.exp(scores - jnp.max(scores, axis=0, keepdims=True))
        inverse = 1.0 / jnp.sum(exp_scores, axis=0, keepdims=True)
        inverses[head : head + 1, :] = inverse
        weights = exp_scores.astype(B16)
        probs[head] = weights
        out = dot(kv_all[:, width + pair * 128 : width + (pair + 1) * 128], weights, TN)
        parts.append(out[half * HEAD_DIM : (half + 1) * HEAD_DIM] * inverse)
        if half == 1:
            mixed[:, pair * 128 : (pair + 1) * 128] = (
                jnp.concatenate(parts, axis=0).T.astype(B16)
            )
            parts = []
        scores = following

    loads[3].wait()
    branch = dot(mixed[...], w_proj[...], MM)
    middle = inputs + gate_att * branch
    branch_ref[...] = branch
    second_normed, second_inverse = norm_rows(middle)
    second_ref[...] = second_normed
    second = (second_normed * (1.0 + scale_mlp) + shift_mlp).astype(B16)
    grads_bf[0] = second
    loads[4].wait()
    loads[5].wait()
    mlp_out = jnp.zeros((own, width), F32)
    for block in range(blocks):
        columns = slice(block * width, (block + 1) * width)
        hidden = dot(second, w_fc1[:, columns], MM)
        cumulative = 0.5 * (1.0 + lax.erf(hidden * (0.5**0.5)))
        act = (hidden * cumulative).astype(B16)
        active[block] = act
        gelu_slope[block] = cumulative + hidden * (
            jnp.exp(-0.5 * hidden * hidden) * (1.0 / math.sqrt(2.0 * math.pi))
        )
        mlp_out = mlp_out + dot(act, w_fc2[columns, :], MM)

    def give_back(out, which):
        for step in range(1, items):
            there = (z + step) % items
            remote(
                send_out.at[which, there],
                out.at[z],
                0,
                span,
                group_recv.at[2 + which],
                at(y, x, there, core),
            )
        out[z] = send_out[which, z]

    def rows_of(start, count):
        return pl.ds(pl.multiple_of(start, 16), count)

    first_slot = [sum(copies_in(what[3]) for what in STREAMS[:k]) for k in range(len(STREAMS))]
    core_copies = {}
    core_done = set()

    def core_start(wave, first, count):
        rows = pl.ds(first, count)
        core_copies[wave, first] = remote(
            core_out.at[wave, rows],
            core_in.at[wave, rows],
            1 + wave,
            count,
            c_recv.at[len(core_copies)],
            core_peer,
        )

    groups = {
        "X": (y * 2 + x, ((y * 2 + 1 - x, x_peer), (2 - y * 2 + x, y_peer), (3 - y * 2 - x, xy_peer))),
        "W": (
            z,
            tuple(
                ((z + step) % items, at(y, x, (z + step) % items, core)) for step in range(1, items)
            ),
        ),
    }

    def stream(index, wave, base, count, dims):
        keys = [first for kept_wave, first in core_copies if kept_wave == wave]
        for key in [first for first in keys if first < base + count]:
            if (wave, key) in core_done:
                continue
            core_done.add((wave, key))
            core_copies[wave, key].wait_recv()
        slot = first_slot[index]
        kept, size, place = base, count, base
        terms, terms_at, terms_step, term_count = core_in, base, 0, 1
        back = []

        def summed(offset, rows):
            values = hold[wave, rows_of(kept + offset, rows), :]
            for number in range(term_count):
                area = rows_of(terms_at + number * terms_step + offset, rows)
                values = values + terms[wave, area, :].astype(F32)
            return values

        def send(area, device):
            return remote(
                stage.at[wave, area],
                stage_in.at[wave, area],
                4 + index,
                area.size,
                s_recv.at[slot],
                device,
            )

        result = None
        steps = dims.rstrip("*")
        for number, dim in enumerate(steps):
            last = number == len(steps) - 1
            if dim in groups:
                side, others = groups[dim]
                size //= 4
                for other_number, (other, device) in reversed(list(enumerate(others))):
                    area = pl.ds(place + other_number * size, size)
                    stage[wave, area, :] = summed(other * size, size).astype(B16)
                    send(area, device)
                mine = summed(side * size, size)
                hold[wave, rows_of(kept + side * size, size), :] = mine
                kept = kept + side * size
                back.append((dim, kept, size))
                terms, terms_at, terms_step, term_count = stage_in, place, size, 3
                place = place + 3 * size
            elif not last:
                size //= 2
                away, keep = (1 - sides[dim]) * size, sides[dim] * size
                area = pl.ds(place, size)
                stage[wave, area, :] = summed(away, size).astype(B16)
                send(area, peers[dim])
                mine = summed(keep, size)
                hold[wave, rows_of(kept + keep, size), :] = mine
                kept = kept + keep
                back.append((dim, kept, size))
                terms, terms_at, terms_step, term_count = stage_in, place, 0, 1
                place = place + size
            else:
                area = pl.ds(place, size)
                stage[wave, area, :] = summed(0, size).astype(B16)
                send(area, peers[dim])
                result = area
            yield
            wait_rows(s_recv.at[slot], 3 * size if dim in groups else size)
            slot += 1
        if result is None:
            values = summed(0, size)
        else:
            values = stage[wave, result, :].astype(F32) + stage_in[wave, result, :].astype(F32)
        total[wave, rows_of(core * half_rows + kept, size), :] = values.astype(B16)

        back.reverse()
        while back:
            dim, start, size = back.pop(0)
            if dims.endswith("*") and dim in "pq" and back and back[0][0] in "pq":
                back.pop(0)
                dim = "X"
            area = total.at[wave, rows_of(core * half_rows + start, size)]
            devices = [device for _, device in reversed(groups[dim][1])] if dim in groups else [peers[dim]]
            for device in devices:
                remote(area, area, 4 + index, size, s_recv.at[slot], device)
            yield
            wait_rows(s_recv.at[slot], len(devices) * size)
            slot += 1
        area = total.at[wave, rows_of(core * half_rows + base, count)]
        copy = remote(area, area, 4 + index, count, s_recv.at[slot], core_peer)
        yield
        copy.wait_recv()

    def compute():
        per_core = blocks // 2
        block_result = middle + gate_mlp * mlp_out
        send_out[0] = block_result.astype(B16).reshape(items, span, width)
        loads[6].wait()
        wait_rows(group_recv.at[1], own - span)
        gradient = gall[...].reshape(own, width).astype(F32)
        mlp_grad = (gate_mlp * gradient).astype(B16)
        grads_bf[1] = mlp_grad
        for index in range(per_core):
            block = (1 - core) * per_core + index
            rows = slice(index * width, (index + 1) * width)
            core_out[0, rows, :] = dot(active[block], mlp_grad, TN).astype(B16)
        core_start(0, 0, half_rows)
        yield
        for index in range(per_core):
            block = core * per_core + index
            rows = slice(index * width, (index + 1) * width)
            hold[0, rows, :] = dot(active[block], mlp_grad, TN)
        yield
        second_grad = jnp.zeros((own, width), F32)
        for block in range(blocks):
            columns = slice(block * width, (block + 1) * width)
            active_grad = dot(mlp_grad, w_fc2[columns, :], NT)
            hid = (active_grad * gelu_slope[block]).astype(B16)
            hidden_grad[block] = hid
            second_grad = second_grad + dot(hid, w_fc1[:, columns], NT)
            yield
        for index in range(per_core):
            block = (1 - core) * per_core + index
            rows = slice(index * width, (index + 1) * width)
            core_out[1, rows, :] = dot(grads_bf[0], hidden_grad[block], TN).astype(B16)
        core_start(1, 0, half_rows)
        yield
        for index in range(per_core):
            block = core * per_core + index
            rows = slice(index * width, (index + 1) * width)
            hold[1, rows, :] = dot(grads_bf[0], hidden_grad[block], TN)
        yield
        second_normed = second_ref[...]
        middle_grad = gradient + norm_back(
            second_normed, second_inverse, second_grad * (1.0 + scale_mlp)
        )
        branch_grad = (gate_att * middle_grad).astype(B16)
        grads_bf[2] = dot(branch_grad, w_proj[...], NT).astype(B16)
        qkvp[3] = dot(mixed[...], branch_grad, TN)
        yield
        mod_own[5:6, :] = col_sum(gradient * mlp_out)
        mod_own[4:5, :] = col_sum(second_grad * second_normed)
        mod_own[3:4, :] = col_sum(second_grad)
        mod_own[2:3, :] = col_sum(middle_grad * branch_ref[...])
        yield

        dq, dkv = q_all, kv_all
        inverse_columns = inverses[...].T
        for pair in range(head_pairs):
            lanes = slice(pair * 128, (pair + 1) * 128)
            v_lanes = slice(width + pair * 128, width + (pair + 1) * 128)
            keys, values, queries = kv_all[:, lanes], kv_all[:, v_lanes], q_all[:, lanes]
            out_grad = grads_bf[2, :, lanes].astype(F32)
            parts = []
            key_grad = jnp.zeros((2 * own, 128), F32)
            value_grad = jnp.zeros((2 * own, 128), F32)
            for half in range(2):
                head = pair * 2 + half
                masked_grad = (
                    out_grad * inverse_columns[:, head : head + 1] * halves[half].astype(F32)
                ).astype(B16)
                weights = probs[head]
                wide_weights = weights.astype(F32)
                weight_grad = dot(values, masked_grad, NT)
                row_sum = col_sum(wide_weights * weight_grad) * inverses[head : head + 1, :]
                score_grad = (wide_weights * (weight_grad - row_sum)).astype(B16)
                value_grad = value_grad + dot(weights, masked_grad, MM)
                key_grad = key_grad + dot(score_grad, queries * halves[half], MM)
                query_grad = dot(keys, score_grad, TN)
                parts.append(query_grad[half * HEAD_DIM : (half + 1) * HEAD_DIM])
            query_grad = jnp.concatenate(parts, axis=0).T * inv_root
            dq[:, lanes] = query_grad.astype(B16)
            dkv[:, lanes] = key_grad.astype(B16)
            dkv[:, v_lanes] = value_grad.astype(B16)
            qkvp[pair, :, :128] = dot(entry[:own, :], dq[:, lanes], TN)
            qkvp[pair, :, 128:256] = dot(entry[...], dkv[:, lanes], TN)
            qkvp[pair, :, 256:] = dot(entry[...], dkv[:, v_lanes], TN)
            if pair == 0:
                core_out[2, :width, :] = qkvp[3 * (1 - core)].astype(B16)
                core_start(2, 0, width)
                hold[2, :width, :] = qkvp[3 * core]
            elif pair == 2:
                core_out[2, width:, :] = qkvp[2 - core].astype(B16)
                core_start(2, width, width)
                hold[2, width:, :] = qkvp[1 + core]
            yield

        entry_send[...] = dot(dkv[own:, :], w_qkv[:, width:], NT)
        entry_copy = remote(entry_send, entry_recv, 0, 2 * own, group_recv.at[4], core_peer)
        entry_grad = dot(dkv[:own, :], w_qkv[:, width:], NT) + dot(dq[...], w_qkv[:, :width], NT)
        yield
        entry_copy.wait_recv()
        entry_grad = entry_grad + entry_recv[...]
        normed = normed_own[...]
        mod_own[1:2, :] = col_sum(entry_grad * normed)
        mod_own[0:1, :] = col_sum(entry_grad)
        mod_copy = remote(mod_own, mod_in, 0, 16, group_recv.at[5], core_peer)
        input_grad = middle_grad + norm_back(
            normed, norm_inverse, entry_grad * (1.0 + scale_att)
        )
        send_out[1] = input_grad.astype(B16).reshape(items, span, width)
        yield
        mod_copy.wait_recv()
        first_row = batch * items
        weight = jnp.where(lax.broadcasted_iota(jnp.int32, mod_own.shape, 0) == 6, 0.5, 1.0)
        mod_all[first_row + z] = (mod_own[...] + mod_in[...]) * weight
        for step in range(1, items):
            place = mod_all.at[first_row + z]
            there = at(y, x, (z + step) % items, core)
            remote(place, place, 0, 16, group_recv.at[6], there)
        yield
        wait_rows(group_recv.at[6], 16 * (items - 1))
        for device in (x_peer, y_peer, xy_peer):
            place = mod_all.at[pl.ds(first_row, items)]
            remote(place, place, 0, 16 * items, group_recv.at[7], device)
        yield
        wait_rows(group_recv.at[7], 3 * 16 * items)
        yield
        give_back(out_block, 0)
        give_back(out_input, 1)

    steps = compute()
    streams = [stream(index, *what) for index, what in enumerate(STREAMS)]
    for step in ORDER:
        next(steps if step < 0 else streams[step], None)
    for rest in [steps] + streams:
        for _ in rest:
            raise AssertionError

    for which in range(2):
        wait_rows(group_recv.at[2 + which], own - span)
    for index, rows in sent_rows.items():
        wait_rows(send_sem.at[index], rows)


def widen_kernel(
    block_16,
    input_16,
    total,
    mod,
    block_out,
    input_out,
    ada_out,
    bias_out,
    qkv_out,
    proj_out,
    fc1_out,
    fc2_out,
    block_32,
    input_32,
    ada_32,
    bias_32,
    qkv_32,
    proj_32,
    fc1_32,
    fc2_32,
    by_piece,
    sem,
):
    count, _, width = mod.shape
    blocks = fc2_32.shape[0] // width
    stores = []

    def store(src, dst):
        copy = pltpu.make_async_copy(src, dst, sem.at[len(stores)])
        copy.start()
        stores.append(copy)

    def part(index):
        return pl.ds(index * width, width)

    for block in range(blocks):
        fc2_32[part(block), :] = total[0, part(block), :].astype(F32)
        store(fc2_32.at[part(block), :], fc2_out.at[part(block), :])
    for piece in range(7):
        for item in range(count):
            by_piece[piece, item : item + 1, :] = mod[item, piece : piece + 1, :]
    conditions = jnp.concatenate([by_piece[6].astype(B16)] * 3, axis=0)
    for piece in range(6):
        columns = slice(piece * width, (piece + 1) * width)
        rows = by_piece[piece]
        bias_32[columns] = jnp.sum(rows, axis=0)
        high = rows.astype(B16)
        rest = rows - high.astype(F32)
        middle = rest.astype(B16)
        low = (rest - middle.astype(F32)).astype(B16)
        parts = jnp.concatenate([high, middle, low], axis=0)
        ada_32[:, columns] = dot(conditions, parts, TN)
        store(ada_32.at[:, part(piece)], ada_out.at[:, part(piece)])
    store(bias_32, bias_out)
    for block in range(blocks):
        columns = slice(block * width, (block + 1) * width)
        fc1_32[:, columns] = total[1, part(block), :].astype(F32)
        store(fc1_32.at[:, part(block)], fc1_out.at[:, part(block)])
    proj_32[...] = total[2, part(2), :].astype(F32)
    store(proj_32, proj_out)
    for pair, block in enumerate((0, 1, 3)):
        for piece in range(3):
            start = piece * width + pair * 128
            qkv_32[:, start : start + 128] = total[
                2, part(block), piece * 128 : (piece + 1) * 128
            ].astype(F32)
    store(qkv_32, qkv_out)
    block_32[...] = block_16[...].astype(F32)
    store(block_32, block_out)
    input_32[...] = input_16[...].astype(F32)
    store(input_32, input_out)
    for copy in stores:
        copy.wait()


def widen(out_block, out_input, total, mod):
    waves, hidden, width = total.shape
    shapes = (
        out_block.shape,
        out_input.shape,
        (width, 6 * width),
        (6 * width,),
        (width, 3 * width),
        (width, width),
        (width, hidden),
        (hidden, width),
    )
    return pl.pallas_call(
        widen_kernel,
        out_shape=tuple(jax.ShapeDtypeStruct(shape, F32) for shape in shapes),
        in_specs=[pl.BlockSpec(memory_space=pltpu.VMEM)] * 4,
        out_specs=(pl.BlockSpec(memory_space=pl.ANY),) * 8,
        scratch_shapes=[pltpu.VMEM(shape, F32) for shape in shapes]
        + [
            pltpu.VMEM((7, mod.shape[0], width), F32),
            pltpu.SemaphoreType.DMA((11 + 2 * (hidden // width),)),
        ],
        name="widen",
        compiler_params=pltpu.CompilerParams(vmem_limit_bytes=30 * 2**20),
    )(out_block, out_input, total, mod)


def fused(block_in, lead_embed, lengths, w_ada, b_ada, w_qkv, w_proj, w_fc1, w_fc2, cotangent):
    items, span, width = block_in.shape
    hidden = w_fc1.shape[1]
    groups = lax.axis_size("batch")
    own = items * span
    blocks = hidden // width
    half = hidden // 2
    waves = 3
    hbm = pl.BlockSpec(memory_space=pl.ANY)
    dma = pltpu.SemaphoreType.DMA
    scratch = [
        pltpu.SMEM(lengths.shape, jnp.int32),
        pltpu.VMEM(lead_embed.shape, B16),
        pltpu.VMEM(b_ada.shape, B16),
        pltpu.VMEM(w_ada.shape, B16),
        pltpu.VMEM(w_qkv.shape, B16),
        pltpu.VMEM(w_proj.shape, B16),
        pltpu.VMEM(w_fc1.shape, B16),
        pltpu.VMEM(w_fc2.shape, B16),
        pltpu.VMEM((2, items, span, width), B16),
        pltpu.VMEM((items, span, width), B16),
        pltpu.VMEM((1, 6 * width), F32),
        pltpu.VMEM((2 * own, width), B16),
        pltpu.VMEM((own, width), F32),
        pltpu.VMEM((own, width), B16),
        pltpu.VMEM((2 * own, 2 * width), B16),
        pltpu.VMEM((2, 2 * own, 128), B16),
        pltpu.VMEM((HEADS, 2 * own, own), B16),
        pltpu.VMEM((8, own), F32),
        pltpu.VMEM((own, width), B16),
        pltpu.VMEM((own, width), F32),
        pltpu.VMEM((own, width), F32),
        pltpu.VMEM((blocks, own, width), B16),
        pltpu.VMEM((blocks, own, width), F32),
        pltpu.VMEM((blocks, own, width), B16),
        pltpu.VMEM((3, own, width), B16),
        pltpu.VMEM((2, items, span, width), B16),
        pltpu.VMEM((own, width), F32),
        pltpu.VMEM((own, width), F32),
        pltpu.VMEM((blocks, width, width), F32),
        pltpu.VMEM((waves, half, width), B16),
        pltpu.VMEM((waves, half, width), B16),
        pltpu.VMEM((waves, half, width), F32),
        pltpu.VMEM((waves, half, width), B16),
        pltpu.VMEM((waves, half, width), B16),
        pltpu.VMEM((8, width), F32),
        pltpu.VMEM((8, width), F32),
        dma((10,)),
        dma((4 + len(STREAMS),)),
        dma((items - 1,)),
        dma((8,)),
        dma((4,)),
        dma((sum(copies_in(what[3]) for what in STREAMS),)),
    ]
    results = pl.pallas_call(
        fused_kernel,
        out_shape=(
            pltpu.VMEM(block_in.shape, B16),
            pltpu.VMEM(block_in.shape, B16),
            pltpu.VMEM((waves, hidden, width), B16),
            pltpu.VMEM((groups * items, 8, width), F32),
        ),
        in_specs=[hbm] * 10,
        out_specs=(pl.BlockSpec(memory_space=pltpu.VMEM),) * 4,
        scratch_shapes=scratch,
        name="fused_block",
        compiler_params=pltpu.CompilerParams(
            collective_id=0, has_side_effects=True, vmem_limit_bytes=58 * 2**20
        ),
    )(
        lengths,
        block_in,
        cotangent,
        lead_embed,
        b_ada,
        w_ada,
        w_qkv,
        w_proj,
        w_fc1,
        w_fc2,
    )
    return widen(*results)


def choose(*arrays):
    items, span, width = arrays[0].shape
    fits = (
        lax.axis_size("batch") == 4
        and items == 4
        and lax.axis_size("wide") == 2 * items
        and span == 64
        and width == HEADS * HEAD_DIM == 384
        and arrays[7].shape[1] == 4 * width
    )
    return (fused if fits else on_device)(*arrays)


def solution(mesh):
    return jax.shard_map(
        choose,
        mesh=mesh,
        in_specs=(
            P("batch", "wide", None),
            P("batch", None),
            P("batch"),
            P(),
            P(),
            P(),
            P(),
            P(),
            P(),
            P("batch", "wide", None),
        ),
        out_specs=(
            P("batch", "wide", None),
            P("batch", "wide", None),
            P(),
            P(),
            P(),
            P(),
            P(),
            P(),
        ),
        check_vma=False,
    )
```

```python
import math
from functools import partial

import jax
import jax.numpy as jnp
from jax import lax
from jax.experimental import pallas as pl
from jax.experimental.pallas import tpu as pltpu
from jax.sharding import PartitionSpec as P

HEADS = 6
HEAD_DIM = 64


EPS = 1e-06


def norm_rows(values):
    center = values - jnp.mean(values, axis=-1, keepdims=True)
    inverse = lax.rsqrt(jnp.mean(center * center, axis=-1, keepdims=True) + EPS)
    return (center * inverse, inverse)


def norm_back(normed, inverse, gradient):
    return inverse * (
        gradient
        - jnp.mean(gradient, axis=-1, keepdims=True)
        - normed * jnp.mean(gradient * normed, axis=-1, keepdims=True)
    )


def to_heads(tokens, part_count, head_count, head_size):
    item_count, span_len, _ = tokens.shape
    shaped = tokens.reshape(item_count, span_len, part_count, head_count, head_size)
    return shaped.transpose(2, 0, 3, 1, 4).reshape(
        part_count, item_count * head_count, span_len * head_size
    )


def from_heads(blocks, item_count, head_count, head_size):
    part_count = blocks.shape[0]
    span_len = blocks.shape[2] // head_size
    shaped = blocks.reshape(part_count, item_count, head_count, span_len, head_size)
    return shaped.transpose(1, 3, 0, 2, 4).reshape(
        item_count, span_len, part_count * head_count * head_size
    )


def split_rows(values, block_rows):
    pair_count, slot_len = (values.shape[0], values.shape[1])
    rest = values.shape[2:]
    shaped = values.reshape((pair_count, slot_len // block_rows, block_rows) + rest)
    return jnp.moveaxis(shaped, 1, 0)


def join_rows(values):
    merged = jnp.moveaxis(values, 0, 1)
    return merged.reshape((merged.shape[0], merged.shape[1] * merged.shape[2]) + merged.shape[3:])


def masked_scores(query_block, keys_all, key_valid, inv_root):
    scores = (
        jnp.einsum("pqd,pkd->pqk", query_block, keys_all, preferred_element_type=jnp.float32)
        * inv_root
    )
    return jnp.where(key_valid[:, None, :], scores, -1e30)


def attend_forward(queries, keys_all, values, key_valid, inv_root):
    block_rows = min(512, queries.shape[1])

    def one_block(query_block):
        scores = masked_scores(query_block, keys_all, key_valid, inv_root)
        row_peak = jnp.max(scores, axis=-1, keepdims=True)
        exp_scores = jnp.exp(scores - row_peak)
        row_total = jnp.sum(exp_scores, axis=-1, keepdims=True)
        weights = (exp_scores / row_total).astype(jnp.bfloat16)
        outcome = jnp.einsum("pqk,pkd->pqd", weights, values, preferred_element_type=jnp.float32)
        return (outcome.astype(jnp.bfloat16), (row_peak + jnp.log(row_total))[..., 0])

    outputs, logsum = lax.map(one_block, split_rows(queries, block_rows))
    return (join_rows(outputs), join_rows(logsum))


def attend_backward(queries, keys_all, values, out_grad, logsum, key_valid, inv_root):
    block_rows = min(512, queries.shape[1])
    zeros = jnp.zeros(keys_all.shape, jnp.float32)

    def one_block(carried, packed):
        key_grad, value_grad = carried
        query_block, grad_block, logsum_block = packed
        scores = masked_scores(query_block, keys_all, key_valid, inv_root)
        weights = jnp.exp(scores - logsum_block[..., None])
        weight_grad = jnp.einsum(
            "pqd,pkd->pqk", grad_block, values, preferred_element_type=jnp.float32
        )
        score_grad = weights * (
            weight_grad - jnp.sum(weights * weight_grad, axis=-1, keepdims=True)
        )
        score_grad = score_grad.astype(jnp.bfloat16)
        query_grad = (
            jnp.einsum("pqk,pkd->pqd", score_grad, keys_all, preferred_element_type=jnp.float32)
            * inv_root
        )
        key_grad = (
            key_grad
            + jnp.einsum(
                "pqk,pqd->pkd", score_grad, query_block, preferred_element_type=jnp.float32
            )
            * inv_root
        )
        value_grad = value_grad + jnp.einsum(
            "pqk,pqd->pkd",
            weights.astype(jnp.bfloat16),
            grad_block,
            preferred_element_type=jnp.float32,
        )
        return ((key_grad, value_grad), query_grad)

    packed = (
        split_rows(queries, block_rows),
        split_rows(out_grad, block_rows),
        split_rows(logsum, block_rows),
    )
    (key_grad, value_grad), query_grads = lax.scan(one_block, (zeros, zeros), packed)
    return jnp.stack([join_rows(query_grads), key_grad, value_grad]).astype(jnp.bfloat16)


def on_device(block_in, lead_embed, lengths, w_ada, b_ada, w_qkv, w_proj, w_fc1, w_fc2, cotangent):
    item_count, span_len, width = block_in.shape
    head_count = HEADS
    head_size = HEAD_DIM
    shards = lax.axis_size("wide")
    pair_count = item_count * head_count // shards
    slot_len = span_len * shards
    inv_root = HEAD_DIM ** (-0.5)
    inputs = block_in.astype(jnp.float32)
    condition = jax.nn.silu(lead_embed.astype(jnp.float32)).astype(jnp.bfloat16)
    modulation = jnp.dot(condition, w_ada, preferred_element_type=jnp.float32) + b_ada.astype(
        jnp.float32
    )
    pieces = [modulation[:, None, column * width : (column + 1) * width] for column in range(6)]
    shift_att, scale_att, gate_att, shift_mlp, scale_mlp, gate_mlp = pieces
    normed, norm_inverse = norm_rows(inputs)
    entry = (normed * (1.0 + scale_att) + shift_att).astype(jnp.bfloat16)
    triple = jnp.dot(entry, w_qkv, preferred_element_type=jnp.float32).astype(jnp.bfloat16)
    arrived = lax.all_to_all(
        to_heads(triple, 3, head_count, head_size), "wide", split_axis=1, concat_axis=2, tiled=True
    )
    heads_in = arrived.reshape(3, pair_count, slot_len, head_size)
    pair_ids = lax.axis_index("wide") * pair_count + jnp.arange(pair_count, dtype=jnp.int32)
    item_ids = pair_ids // head_count
    pair_length = jnp.sum(
        jnp.where(
            jnp.arange(item_count, dtype=jnp.int32)[None, :] == item_ids[:, None],
            lengths[None, :],
            0,
        ),
        axis=1,
    )
    key_valid = jnp.arange(slot_len, dtype=jnp.int32)[None, :] < pair_length[:, None]
    mixed_heads, logsum = attend_forward(heads_in[0], heads_in[1], heads_in[2], key_valid, inv_root)
    returned = lax.all_to_all(
        mixed_heads.reshape(pair_count, slot_len * head_size),
        "wide",
        split_axis=1,
        concat_axis=0,
        tiled=True,
    )
    mixed_tok = from_heads(returned[None], item_count, head_count, head_size)
    branch = jnp.dot(mixed_tok, w_proj, preferred_element_type=jnp.float32)
    middle = inputs + gate_att * branch
    second_normed, second_inverse = norm_rows(middle)
    second = (second_normed * (1.0 + scale_mlp) + shift_mlp).astype(jnp.bfloat16)
    hidden = jnp.dot(second, w_fc1, preferred_element_type=jnp.float32)
    active = jax.nn.gelu(hidden, approximate=False).astype(jnp.bfloat16)
    mlp_out = jnp.dot(active, w_fc2, preferred_element_type=jnp.float32)
    block_out = middle + gate_mlp * mlp_out
    gradient = cotangent.astype(jnp.float32)
    mlp_grad = (gate_mlp * gradient).astype(jnp.bfloat16)
    gate_mlp_grad = jnp.sum(gradient * mlp_out, axis=1)
    fc2_grad = jnp.einsum("isf,isd->fd", active, mlp_grad, preferred_element_type=jnp.float32)
    active_grad = jnp.dot(mlp_grad, w_fc2.T, preferred_element_type=jnp.float32)
    hidden_grad = jax.vjp(partial(jax.nn.gelu, approximate=False), hidden)[1](active_grad)[0]
    hidden_grad = hidden_grad.astype(jnp.bfloat16)
    fc1_grad = jnp.einsum("isd,isf->df", second, hidden_grad, preferred_element_type=jnp.float32)
    second_grad = jnp.dot(hidden_grad, w_fc1.T, preferred_element_type=jnp.float32)
    scale_mlp_grad = jnp.sum(second_grad * second_normed, axis=1)
    shift_mlp_grad = jnp.sum(second_grad, axis=1)
    middle_grad = gradient + norm_back(
        second_normed, second_inverse, second_grad * (1.0 + scale_mlp)
    )
    branch_grad = (gate_att * middle_grad).astype(jnp.bfloat16)
    gate_att_grad = jnp.sum(middle_grad * branch, axis=1)
    proj_grad = jnp.einsum(
        "isd,ise->de", mixed_tok, branch_grad, preferred_element_type=jnp.float32
    )
    mixed_grad = jnp.dot(branch_grad, w_proj.T, preferred_element_type=jnp.float32).astype(
        jnp.bfloat16
    )
    heads_grad = lax.all_to_all(
        to_heads(mixed_grad, 1, head_count, head_size)[0],
        "wide",
        split_axis=0,
        concat_axis=1,
        tiled=True,
    )
    heads_grad = heads_grad.reshape(pair_count, slot_len, head_size)
    again_in, _ = lax.optimization_barrier((inputs, heads_grad))
    again_normed, _ = norm_rows(again_in)
    again_entry = (again_normed * (1.0 + scale_att) + shift_att).astype(jnp.bfloat16)
    again_triple = jnp.dot(again_entry, w_qkv, preferred_element_type=jnp.float32).astype(
        jnp.bfloat16
    )
    again_heads = lax.all_to_all(
        to_heads(again_triple, 3, head_count, head_size),
        "wide",
        split_axis=1,
        concat_axis=2,
        tiled=True,
    )
    used_heads = again_heads.reshape(3, pair_count, slot_len, head_size)
    triple_grad = attend_backward(
        used_heads[0], used_heads[1], used_heads[2], heads_grad, logsum, key_valid, inv_root
    )
    sent_back = lax.all_to_all(
        triple_grad.reshape(3, pair_count, slot_len * head_size),
        "wide",
        split_axis=2,
        concat_axis=1,
        tiled=True,
    )
    token_grad = from_heads(sent_back, item_count, head_count, head_size)
    qkv_grad = jnp.einsum("isd,ise->de", entry, token_grad, preferred_element_type=jnp.float32)
    entry_grad = jnp.dot(token_grad, w_qkv.T, preferred_element_type=jnp.float32)
    scale_att_grad = jnp.sum(entry_grad * normed, axis=1)
    shift_att_grad = jnp.sum(entry_grad, axis=1)
    input_grad = middle_grad + norm_back(normed, norm_inverse, entry_grad * (1.0 + scale_att))
    modulation_grad = jnp.concatenate(
        [
            shift_att_grad,
            scale_att_grad,
            gate_att_grad,
            shift_mlp_grad,
            scale_mlp_grad,
            gate_mlp_grad,
        ],
        axis=-1,
    )
    ada_grad = jnp.dot(
        condition.astype(jnp.float32).T, modulation_grad, precision=lax.Precision.HIGHEST
    )
    bias_grad = jnp.sum(modulation_grad, axis=0)
    totals = lax.psum(
        (ada_grad, bias_grad, qkv_grad, proj_grad, fc1_grad, fc2_grad), ("batch", "wide")
    )
    return (block_out, input_grad, totals[0], totals[1], totals[2], totals[3], totals[4], totals[5])


MESH = pl.DeviceIdType.MESH
MM = (((1,), (0,)), ((), ()))
NT = (((1,), (1,)), ((), ()))
TN = (((0,), (0,)), ((), ()))
B16 = jnp.bfloat16
F32 = jnp.float32

STREAMS = (
    (0, 0, 256, "zpqZ"),
    (0, 256, 128, "pqzZ"),
    (0, 384, 256, "pqzZ"),
    (0, 640, 128, "pzZq"),
    (1, 0, 256, "XW"),
    (1, 256, 256, "pqzZ"),
    (1, 512, 256, "zpqZ"),
    (2, 0, 256, "pqzZ*"),
    (2, 256, 128, "pzqZ"),
    (2, 384, 384, "pqzZ*"),
)
ORDER = (
    -1, -1, -1, -1, -1, -1, -1, -1, 0, 1, 2, 3, -1, -1, 4, 5, 6, -1, -1, -1,
    1, -1, -1, 0, 7, 8, 3, -1, 6, -1, 4, 1, 2, 9, 3, -1, 0, 5, 8, 6,
    1, 7, 4, 2, 3, -1, 0, 8, 5, 6, 1, 9, 7, 3, 8, 4, 2, -1, 0, 5,
    1, 9, 6, 7, 3, 8, 2, 0, 5, 9, 1, 3, 7, 4, 8, 6, 2, 0, 5, 4,
    1, 3, -1, 7, 9, 8, 1, 6, 3, 2, 5, 0, -1, 9, 0, 7, 8, 7, 8, 2,
    6, 5, 9, 2, 6, 5, 9,
)


def copies_in(dims):
    steps = dims.rstrip("*")
    back = len(steps) - (steps[-1] not in "XW") - (dims[-1] == "*")
    return len(steps) + back + 1


def dot(left, right, dims):
    return lax.dot_general(left, right, dims, preferred_element_type=F32)


def col_sum(values):
    return jnp.sum(values, axis=0, keepdims=True)


def fused_kernel(
    lengths_in,
    block_in,
    cotangent,
    lead_embed_in,
    b_ada_in,
    w_ada_in,
    w_qkv_in,
    w_proj_in,
    w_fc1_in,
    w_fc2_in,
    out_block,
    out_input,
    total,
    mod_all,
    lengths,
    lead_embed,
    b_ada,
    w_ada,
    w_qkv,
    w_proj,
    w_fc1,
    w_fc2,
    xall,
    gall,
    mod_rows,
    entry,
    normed_own,
    q_all,
    kv_all,
    bias_keys,
    probs,
    inverses,
    mixed,
    branch_ref,
    second_ref,
    active,
    gelu_slope,
    hidden_grad,
    mixed_grad,
    entry_t,
    second_t,
    mixed_t,
    keys_t,
    send_out,
    entry_send,
    entry_recv,
    qkvp,
    core_out,
    core_in,
    hold,
    stage,
    stage_in,
    mod_own,
    mod_in,
    load_sem,
    send_sem,
    x_recv,
    group_recv,
    c_recv,
    s_recv,
):
    items, span, width = block_in.shape
    own = items * span
    head_pairs = width // 128
    blocks = active.shape[0]
    half_rows = hold.shape[1]
    inv_root = HEAD_DIM**-0.5
    batch, wide = lax.axis_index("batch"), lax.axis_index("wide")
    z, core = wide // 2, wide % 2
    y, x = batch // 2, batch % 2
    zb = z % 2

    def at(y_, x_, z_, core_):
        return (y_ * 2 + x_, z_ * 2 + core_)

    core_peer = at(y, x, z, 1 - core)
    x_peer = at(y, 1 - x, z, core)
    y_peer = at(1 - y, x, z, core)
    xy_peer = at(1 - y, 1 - x, z, core)
    flip_x, flip_y = 1 - 2 * x, 1 - 2 * y
    peers = {
        "p": at(y + flip_y * core, x + flip_x * (1 - core), z, core),
        "q": at(y + flip_y * (1 - core), x + flip_x * core, z, core),
        "z": at(y, x, z + 1 - 2 * zb, core),
        "Z": at(y, x, (z + 2) % items, core),
    }
    sides = {
        "p": x * (1 - core) + y * core,
        "q": y * (1 - core) + x * core,
        "z": zb,
        "Z": z // 2,
    }

    sent_rows = {}

    def remote(src, dst, send, rows, recv, device):
        sent_rows[send] = sent_rows.get(send, 0) + rows
        copy = pltpu.make_async_remote_copy(
            src_ref=src,
            dst_ref=dst,
            send_sem=send_sem.at[send],
            recv_sem=recv,
            device_id=device,
            device_id_type=MESH,
        )
        copy.start()
        return copy

    def load(src, dst, index):
        copy = pltpu.make_async_copy(src, dst, load_sem.at[index])
        copy.start()
        return copy

    def wait_rows(sem, rows):
        planes = next(p for p in (1, 2, 3) if rows % (16 * p) == 0 and rows <= p * total.shape[1])
        area = total.at[pl.ds(0, planes), pl.ds(0, rows // planes)]
        pltpu.make_async_copy(area, area, sem).wait()

    barrier = pltpu.get_barrier_semaphore()
    greet = [core_peer, x_peer, y_peer, xy_peer]
    greet += [at(y, x, (z + step) % items, core) for step in range(1, items)]
    for device in greet:
        pl.semaphore_signal(barrier, inc=1, device_id=device, device_id_type=MESH)
    loads = [
        load(block_in.at[z], xall.at[0, z], 0),
        load(w_ada_in, w_ada, 1),
        load(w_qkv_in, w_qkv, 2),
        load(w_proj_in, w_proj, 3),
        load(w_fc1_in, w_fc1, 4),
        load(w_fc2_in, w_fc2, 5),
        load(cotangent.at[z], gall.at[z], 6),
        load(lead_embed_in, lead_embed, 7),
        load(b_ada_in, b_ada, 8),
        load(lengths_in, lengths, 9),
    ]
    pl.semaphore_wait(barrier, len(greet))

    x_copies = []
    for step in range(1, items):
        there = (z + step) % items
        x_copies.append(
            remote(
                block_in.at[there],
                xall.at[0, z],
                0,
                span,
                x_recv.at[step - 1],
                at(y, x, there, core),
            )
        )
    remote(block_in.at[z], xall.at[1, z], 0, span, group_recv.at[0], core_peer)

    for index in (7, 8, 9):
        loads[index].wait()
    embed = lead_embed[...].astype(F32)
    condition = (embed / (1.0 + jnp.exp(-embed))).astype(B16)
    loads[1].wait()
    all_rows = dot(condition, w_ada[...], MM) + b_ada[...].astype(F32).reshape(1, -1)
    mine = lax.broadcasted_iota(jnp.int32, (items, 1), 0) == z
    mod_rows[...] = jnp.sum(jnp.where(mine, all_rows, 0.0), axis=0, keepdims=True)
    pieces = [mod_rows[:, column * width : (column + 1) * width] for column in range(6)]
    shift_att, scale_att, gate_att, shift_mlp, scale_mlp, gate_mlp = pieces
    mod_own[...] = jnp.zeros(mod_own.shape, F32)
    inverses[...] = jnp.zeros(inverses.shape, F32)
    mod_own[6:7, :] = jnp.sum(jnp.where(mine, condition.astype(F32), 0.0), axis=0, keepdims=True)

    lane = lax.broadcasted_iota(jnp.int32, (1, 128), 1)
    halves, marks = [], []
    row = lax.broadcasted_iota(jnp.int32, (2 * own, 128), 0)
    block_core = jnp.where(row // own == 0, core, 1 - core)
    position = ((row % own) // span * 2 + block_core) * span + row % span
    bias = jnp.where(position < lengths[z], 0.0, -1e30)
    for half in range(2):
        inside = lane // HEAD_DIM == half
        halves.append(jnp.where(inside, 1.0, 0.0).astype(B16))
        mark = jnp.where(lane == (1 - half) * HEAD_DIM, 1.0, 0.0)
        marks.append(mark.astype(B16))
        bias_keys[half] = (bias * mark).astype(B16)

    loads[0].wait()
    for step in range(1, items):
        came = (z + items - step) % items
        x_copies[step - 1].wait_recv()
        remote(
            xall.at[0, came],
            xall.at[1, came],
            0,
            span,
            group_recv.at[0],
            core_peer,
        )
    for step in range(1, items):
        there = (z + step) % items
        remote(
            cotangent.at[there],
            gall.at[z],
            0,
            span,
            group_recv.at[1],
            at(y, x, there, core),
        )

    loads[2].wait()
    inputs = xall[0].reshape(own, width).astype(F32)
    normed, norm_inverse = norm_rows(inputs)
    normed_own[...] = normed
    entry[:own, :] = (normed * (1.0 + scale_att) + shift_att).astype(B16)
    q_all[...] = (dot(entry[:own, :], w_qkv[:, :width], MM).astype(B16) * inv_root).astype(B16)
    kv_all[:own, :] = dot(entry[:own, :], w_qkv[:, width:], MM).astype(B16)
    wait_rows(group_recv.at[0], own)
    other_normed, _ = norm_rows(xall[1].reshape(own, width).astype(F32))
    entry[own:, :] = (other_normed * (1.0 + scale_att) + shift_att).astype(B16)
    kv_all[own:, :] = dot(entry[own:, :], w_qkv[:, width:], MM).astype(B16)

    def head_scores(head):
        pair, half = divmod(head, 2)
        lanes = slice(pair * 128, (pair + 1) * 128)
        return dot(
            kv_all[:, lanes] * halves[half] + bias_keys[half],
            q_all[:, lanes] * halves[half] + marks[half],
            NT,
        )

    scores, parts = head_scores(0), []
    for head in range(HEADS):
        pair, half = divmod(head, 2)
        following = head_scores(head + 1) if head + 1 < HEADS else None
        exp_scores = jnp.exp(scores - jnp.max(scores, axis=0, keepdims=True))
        inverse = 1.0 / jnp.sum(exp_scores, axis=0, keepdims=True)
        inverses[head : head + 1, :] = inverse
        weights = exp_scores.astype(B16)
        probs[head] = weights
        out = dot(kv_all[:, width + pair * 128 : width + (pair + 1) * 128], weights, TN)
        parts.append(out[half * HEAD_DIM : (half + 1) * HEAD_DIM] * inverse)
        if half == 1:
            mixed[:, pair * 128 : (pair + 1) * 128] = (
                jnp.concatenate(parts, axis=0).T.astype(B16)
            )
            parts = []
        scores = following

    loads[3].wait()
    branch = dot(mixed[...], w_proj[...], MM)
    middle = inputs + gate_att * branch
    branch_ref[...] = branch
    second_normed, second_inverse = norm_rows(middle)
    second_ref[...] = second_normed
    second = (second_normed * (1.0 + scale_mlp) + shift_mlp).astype(B16)
    loads[4].wait()
    loads[5].wait()
    mlp_out = jnp.zeros((own, width), F32)
    for block in range(blocks):
        columns = slice(block * width, (block + 1) * width)
        hidden = dot(second, w_fc1[:, columns], MM)
        cumulative = 0.5 * (1.0 + lax.erf(hidden * (0.5**0.5)))
        act = (hidden * cumulative).astype(B16)
        active[block] = act.T
        gelu_slope[block] = cumulative + hidden * (
            jnp.exp(-0.5 * hidden * hidden) * (1.0 / math.sqrt(2.0 * math.pi))
        )
        mlp_out = mlp_out + dot(act, w_fc2[columns, :], MM)

    entry_t[...] = entry[...].T
    second_t[...] = second.T
    mixed_t[...] = mixed[...].T
    keys_t[...] = kv_all[:, :width].T

    def give_back(out, which):
        for step in range(1, items):
            there = (z + step) % items
            remote(
                send_out.at[which, there],
                out.at[z],
                0,
                span,
                group_recv.at[2 + which],
                at(y, x, there, core),
            )
        out[z] = send_out[which, z]

    def rows_of(start, count):
        return pl.ds(pl.multiple_of(start, 16), count)

    first_slot = [sum(copies_in(what[3]) for what in STREAMS[:k]) for k in range(len(STREAMS))]
    core_copies = {}
    core_done = set()

    def core_start(wave, first, count):
        rows = pl.ds(first, count)
        core_copies[wave, first] = remote(
            core_out.at[wave, rows],
            core_in.at[wave, rows],
            1 + wave,
            count,
            c_recv.at[len(core_copies)],
            core_peer,
        )

    groups = {
        "X": (y * 2 + x, ((y * 2 + 1 - x, x_peer), (2 - y * 2 + x, y_peer), (3 - y * 2 - x, xy_peer))),
        "W": (
            z,
            tuple(
                ((z + step) % items, at(y, x, (z + step) % items, core)) for step in range(1, items)
            ),
        ),
    }

    def stream(index, wave, base, count, dims):
        keys = [first for kept_wave, first in core_copies if kept_wave == wave]
        for key in [first for first in keys if first < base + count]:
            if (wave, key) in core_done:
                continue
            core_done.add((wave, key))
            core_copies[wave, key].wait_recv()
        slot = first_slot[index]
        kept, size, place = base, count, base
        terms = [(core_in, base)]
        back = []

        def summed(offset, rows):
            values = hold[wave, rows_of(kept + offset, rows), :]
            for array, at_row in terms:
                values = values + array[wave, rows_of(at_row + offset, rows), :].astype(F32)
            return values

        def send(area, device):
            return remote(
                stage.at[wave, area],
                stage_in.at[wave, area],
                4 + index,
                area.size,
                s_recv.at[slot],
                device,
            )

        result = None
        steps = dims.rstrip("*")
        for number, dim in enumerate(steps):
            last = number == len(steps) - 1
            if dim in groups:
                side, others = groups[dim]
                size //= 4
                for other_number, (other, device) in reversed(list(enumerate(others))):
                    area = pl.ds(place + other_number * size, size)
                    stage[wave, area, :] = summed(other * size, size).astype(B16)
                    send(area, device)
                kept = kept + side * size
                back.append((dim, kept, size))
                terms = [(array, at_row + side * size) for array, at_row in terms]
                terms += [(stage_in, place + other_number * size) for other_number in range(3)]
                place = place + 3 * size
            elif not last:
                size //= 2
                away, keep = (1 - sides[dim]) * size, sides[dim] * size
                area = pl.ds(place, size)
                stage[wave, area, :] = summed(away, size).astype(B16)
                send(area, peers[dim])
                kept = kept + keep
                back.append((dim, kept, size))
                terms = [(array, at_row + keep) for array, at_row in terms] + [(stage_in, place)]
                place = place + size
            else:
                area = pl.ds(place, size)
                stage[wave, area, :] = summed(0, size).astype(B16)
                send(area, peers[dim])
                result = area
            yield
            wait_rows(s_recv.at[slot], 3 * size if dim in groups else size)
            slot += 1
        if result is None:
            values = summed(0, size)
        else:
            values = stage[wave, result, :].astype(F32) + stage_in[wave, result, :].astype(F32)
        total[wave, rows_of(core * half_rows + kept, size), :] = values.astype(B16)

        back.reverse()
        while back:
            dim, start, size = back.pop(0)
            if dims.endswith("*") and dim in "pq" and back and back[0][0] in "pq":
                back.pop(0)
                dim = "X"
            area = total.at[wave, rows_of(core * half_rows + start, size)]
            devices = [device for _, device in reversed(groups[dim][1])] if dim in groups else [peers[dim]]
            for device in devices:
                remote(area, area, 4 + index, size, s_recv.at[slot], device)
            yield
            wait_rows(s_recv.at[slot], len(devices) * size)
            slot += 1
        area = total.at[wave, rows_of(core * half_rows + base, count)]
        copy = remote(area, area, 4 + index, count, s_recv.at[slot], core_peer)
        yield
        copy.wait_recv()

    def compute():
        per_core = blocks // 2
        block_result = middle + gate_mlp * mlp_out
        send_out[0] = block_result.astype(B16).reshape(items, span, width)
        loads[6].wait()
        wait_rows(group_recv.at[1], own - span)
        gradient = gall[...].reshape(own, width).astype(F32)
        mlp_grad = (gate_mlp * gradient).astype(B16)
        for index in range(per_core):
            block = (1 - core) * per_core + index
            rows = slice(index * width, (index + 1) * width)
            core_out[0, rows, :] = dot(active[block], mlp_grad, MM).astype(B16)
        core_start(0, 0, half_rows)
        yield
        for index in range(per_core):
            block = core * per_core + index
            rows = slice(index * width, (index + 1) * width)
            hold[0, rows, :] = dot(active[block], mlp_grad, MM)
        yield
        second_grad = jnp.zeros((own, width), F32)
        for block in range(blocks):
            columns = slice(block * width, (block + 1) * width)
            active_grad = dot(mlp_grad, w_fc2[columns, :], NT)
            hid = (active_grad * gelu_slope[block]).astype(B16)
            hidden_grad[block] = hid
            second_grad = second_grad + dot(hid, w_fc1[:, columns], NT)
            yield
        for index in range(per_core):
            block = (1 - core) * per_core + index
            rows = slice(index * width, (index + 1) * width)
            core_out[1, rows, :] = dot(second_t[...], hidden_grad[block], MM).astype(B16)
        core_start(1, 0, half_rows)
        yield
        for index in range(per_core):
            block = core * per_core + index
            rows = slice(index * width, (index + 1) * width)
            hold[1, rows, :] = dot(second_t[...], hidden_grad[block], MM)
        yield
        second_normed = second_ref[...]
        middle_grad = gradient + norm_back(
            second_normed, second_inverse, second_grad * (1.0 + scale_mlp)
        )
        branch_grad = (gate_att * middle_grad).astype(B16)
        mixed_grad[...] = dot(branch_grad, w_proj[...], NT).astype(B16)
        qkvp[3] = dot(mixed_t[...], branch_grad, MM)
        yield
        mod_own[5:6, :] = col_sum(gradient * mlp_out)
        mod_own[4:5, :] = col_sum(second_grad * second_normed)
        mod_own[3:4, :] = col_sum(second_grad)
        mod_own[2:3, :] = col_sum(middle_grad * branch_ref[...])
        yield

        dq, dkv = q_all, kv_all
        inverse_columns = inverses[...].T
        for pair in range(head_pairs):
            lanes = slice(pair * 128, (pair + 1) * 128)
            v_lanes = slice(width + pair * 128, width + (pair + 1) * 128)
            values, queries = kv_all[:, v_lanes], q_all[:, lanes]
            out_grad = mixed_grad[:, lanes].astype(F32)
            parts = []
            key_grad = jnp.zeros((2 * own, 128), F32)
            value_grad = jnp.zeros((2 * own, 128), F32)
            for half in range(2):
                head = pair * 2 + half
                masked_grad = (
                    out_grad * inverse_columns[:, head : head + 1] * halves[half].astype(F32)
                ).astype(B16)
                weights = probs[head]
                wide_weights = weights.astype(F32)
                weight_grad = dot(values, masked_grad, NT)
                row_sum = col_sum(wide_weights * weight_grad) * inverses[head : head + 1, :]
                score_grad = (wide_weights * (weight_grad - row_sum)).astype(B16)
                value_grad = value_grad + dot(weights, masked_grad, MM)
                key_grad = key_grad + dot(score_grad, queries * halves[half], MM)
                query_grad = dot(keys_t[lanes, :], score_grad, MM)
                parts.append(query_grad[half * HEAD_DIM : (half + 1) * HEAD_DIM])
                if half == 0:
                    yield
            query_grad = jnp.concatenate(parts, axis=0).T * inv_root
            dq[:, lanes] = query_grad.astype(B16)
            dkv[:, lanes] = key_grad.astype(B16)
            dkv[:, v_lanes] = value_grad.astype(B16)
            qkvp[pair, :, :128] = dot(entry_t[:, :own], dq[:, lanes], MM)
            pair_grads = jnp.concatenate([key_grad, value_grad], axis=1).astype(B16)
            qkvp[pair, :, 128:] = dot(entry_t[...], pair_grads, MM)
            if pair == 0:
                core_out[2, :width, :] = qkvp[3 * (1 - core)].astype(B16)
                core_start(2, 0, width)
                hold[2, :width, :] = qkvp[3 * core]
            elif pair == 2:
                core_out[2, width:, :] = qkvp[2 - core].astype(B16)
                core_start(2, width, width)
                hold[2, width:, :] = qkvp[1 + core]
            yield

        entry_send[...] = dot(dkv[own:, :], w_qkv[:, width:], NT)
        entry_copy = remote(entry_send, entry_recv, 0, 2 * own, group_recv.at[4], core_peer)
        entry_grad = dot(dkv[:own, :], w_qkv[:, width:], NT) + dot(dq[...], w_qkv[:, :width], NT)
        yield
        entry_copy.wait_recv()
        entry_grad = entry_grad + entry_recv[...]
        normed = normed_own[...]
        mod_own[1:2, :] = col_sum(entry_grad * normed)
        mod_own[0:1, :] = col_sum(entry_grad)
        mod_copy = remote(mod_own, mod_in, 0, 16, group_recv.at[5], core_peer)
        input_grad = middle_grad + norm_back(
            normed, norm_inverse, entry_grad * (1.0 + scale_att)
        )
        send_out[1] = input_grad.astype(B16).reshape(items, span, width)
        yield
        mod_copy.wait_recv()
        first_row = batch * items
        weight = jnp.where(lax.broadcasted_iota(jnp.int32, mod_own.shape, 0) == 6, 0.5, 1.0)
        mod_all[first_row + z] = (mod_own[...] + mod_in[...]) * weight
        for step in range(1, items):
            place = mod_all.at[first_row + z]
            there = at(y, x, (z + step) % items, core)
            remote(place, place, 0, 16, group_recv.at[6], there)
        yield
        wait_rows(group_recv.at[6], 16 * (items - 1))
        for device in (x_peer, y_peer, xy_peer):
            place = mod_all.at[pl.ds(first_row, items)]
            remote(place, place, 0, 16 * items, group_recv.at[7], device)
        yield
        wait_rows(group_recv.at[7], 3 * 16 * items)
        yield
        give_back(out_block, 0)
        give_back(out_input, 1)

    steps = compute()
    streams = [stream(index, *what) for index, what in enumerate(STREAMS)]
    for step in ORDER:
        next(steps if step < 0 else streams[step], None)
    for rest in [steps] + streams:
        for _ in rest:
            raise AssertionError

    for which in range(2):
        wait_rows(group_recv.at[2 + which], own - span)
    for index, rows in sent_rows.items():
        wait_rows(send_sem.at[index], rows)


def widen_kernel(
    block_16,
    input_16,
    total,
    mod,
    block_out,
    input_out,
    ada_out,
    bias_out,
    qkv_out,
    proj_out,
    fc1_out,
    fc2_out,
    block_32,
    input_32,
    ada_32,
    bias_32,
    qkv_32,
    proj_32,
    fc1_32,
    fc2_32,
    by_piece,
    sem,
):
    count, _, width = mod.shape
    blocks = fc2_32.shape[0] // width
    stores = []

    def store(src, dst):
        copy = pltpu.make_async_copy(src, dst, sem.at[len(stores)])
        copy.start()
        stores.append(copy)

    def part(index):
        return pl.ds(index * width, width)

    for block in range(blocks):
        fc2_32[part(block), :] = total[0, part(block), :].astype(F32)
        store(fc2_32.at[part(block), :], fc2_out.at[part(block), :])
    for piece in range(7):
        for item in range(count):
            by_piece[piece, item : item + 1, :] = mod[item, piece : piece + 1, :]
    conditions = jnp.concatenate([by_piece[6].astype(B16)] * 3, axis=0)
    for piece in range(6):
        columns = slice(piece * width, (piece + 1) * width)
        rows = by_piece[piece]
        bias_32[columns] = jnp.sum(rows, axis=0)
        high = rows.astype(B16)
        rest = rows - high.astype(F32)
        middle = rest.astype(B16)
        low = (rest - middle.astype(F32)).astype(B16)
        parts = jnp.concatenate([high, middle, low], axis=0)
        ada_32[:, columns] = dot(conditions, parts, TN)
        store(ada_32.at[:, part(piece)], ada_out.at[:, part(piece)])
    store(bias_32, bias_out)
    for block in range(blocks):
        columns = slice(block * width, (block + 1) * width)
        fc1_32[:, columns] = total[1, part(block), :].astype(F32)
        store(fc1_32.at[:, part(block)], fc1_out.at[:, part(block)])
    proj_32[...] = total[2, part(2), :].astype(F32)
    store(proj_32, proj_out)
    for pair, block in enumerate((0, 1, 3)):
        for piece in range(3):
            start = piece * width + pair * 128
            qkv_32[:, start : start + 128] = total[
                2, part(block), piece * 128 : (piece + 1) * 128
            ].astype(F32)
    store(qkv_32, qkv_out)
    block_32[...] = block_16[...].astype(F32)
    store(block_32, block_out)
    input_32[...] = input_16[...].astype(F32)
    store(input_32, input_out)
    for copy in stores:
        copy.wait()


def widen(out_block, out_input, total, mod):
    waves, hidden, width = total.shape
    shapes = (
        out_block.shape,
        out_input.shape,
        (width, 6 * width),
        (6 * width,),
        (width, 3 * width),
        (width, width),
        (width, hidden),
        (hidden, width),
    )
    return pl.pallas_call(
        widen_kernel,
        out_shape=tuple(jax.ShapeDtypeStruct(shape, F32) for shape in shapes),
        in_specs=[pl.BlockSpec(memory_space=pltpu.VMEM)] * 4,
        out_specs=(pl.BlockSpec(memory_space=pl.ANY),) * 8,
        scratch_shapes=[pltpu.VMEM(shape, F32) for shape in shapes]
        + [
            pltpu.VMEM((7, mod.shape[0], width), F32),
            pltpu.SemaphoreType.DMA((11 + 2 * (hidden // width),)),
        ],
        name="widen",
        compiler_params=pltpu.CompilerParams(vmem_limit_bytes=30 * 2**20),
    )(out_block, out_input, total, mod)


def fused(block_in, lead_embed, lengths, w_ada, b_ada, w_qkv, w_proj, w_fc1, w_fc2, cotangent):
    items, span, width = block_in.shape
    hidden = w_fc1.shape[1]
    groups = lax.axis_size("batch")
    own = items * span
    blocks = hidden // width
    half = hidden // 2
    waves = 3
    hbm = pl.BlockSpec(memory_space=pl.ANY)
    dma = pltpu.SemaphoreType.DMA
    scratch = [
        pltpu.SMEM(lengths.shape, jnp.int32),
        pltpu.VMEM(lead_embed.shape, B16),
        pltpu.VMEM(b_ada.shape, B16),
        pltpu.VMEM(w_ada.shape, B16),
        pltpu.VMEM(w_qkv.shape, B16),
        pltpu.VMEM(w_proj.shape, B16),
        pltpu.VMEM(w_fc1.shape, B16),
        pltpu.VMEM(w_fc2.shape, B16),
        pltpu.VMEM((2, items, span, width), B16),
        pltpu.VMEM((items, span, width), B16),
        pltpu.VMEM((1, 6 * width), F32),
        pltpu.VMEM((2 * own, width), B16),
        pltpu.VMEM((own, width), F32),
        pltpu.VMEM((own, width), B16),
        pltpu.VMEM((2 * own, 2 * width), B16),
        pltpu.VMEM((2, 2 * own, 128), B16),
        pltpu.VMEM((HEADS, 2 * own, own), B16),
        pltpu.VMEM((8, own), F32),
        pltpu.VMEM((own, width), B16),
        pltpu.VMEM((own, width), F32),
        pltpu.VMEM((own, width), F32),
        pltpu.VMEM((blocks, width, own), B16),
        pltpu.VMEM((blocks, own, width), F32),
        pltpu.VMEM((blocks, own, width), B16),
        pltpu.VMEM((own, width), B16),
        pltpu.VMEM((width, 2 * own), B16),
        pltpu.VMEM((width, own), B16),
        pltpu.VMEM((width, own), B16),
        pltpu.VMEM((width, 2 * own), B16),
        pltpu.VMEM((2, items, span, width), B16),
        pltpu.VMEM((own, width), F32),
        pltpu.VMEM((own, width), F32),
        pltpu.VMEM((blocks, width, width), F32),
        pltpu.VMEM((waves, half, width), B16),
        pltpu.VMEM((waves, half, width), B16),
        pltpu.VMEM((waves, half, width), F32),
        pltpu.VMEM((waves, half, width), B16),
        pltpu.VMEM((waves, half, width), B16),
        pltpu.VMEM((8, width), F32),
        pltpu.VMEM((8, width), F32),
        dma((10,)),
        dma((4 + len(STREAMS),)),
        dma((items - 1,)),
        dma((8,)),
        dma((4,)),
        dma((sum(copies_in(what[3]) for what in STREAMS),)),
    ]
    results = pl.pallas_call(
        fused_kernel,
        out_shape=(
            pltpu.VMEM(block_in.shape, B16),
            pltpu.VMEM(block_in.shape, B16),
            pltpu.VMEM((waves, hidden, width), B16),
            pltpu.VMEM((groups * items, 8, width), F32),
        ),
        in_specs=[hbm] * 10,
        out_specs=(pl.BlockSpec(memory_space=pltpu.VMEM),) * 4,
        scratch_shapes=scratch,
        name="fused_block",
        compiler_params=pltpu.CompilerParams(
            collective_id=0, has_side_effects=True, vmem_limit_bytes=58 * 2**20
        ),
    )(
        lengths,
        block_in,
        cotangent,
        lead_embed,
        b_ada,
        w_ada,
        w_qkv,
        w_proj,
        w_fc1,
        w_fc2,
    )
    return widen(*results)


def choose(*arrays):
    items, span, width = arrays[0].shape
    fits = (
        lax.axis_size("batch") == 4
        and items == 4
        and lax.axis_size("wide") == 2 * items
        and span == 64
        and width == HEADS * HEAD_DIM == 384
        and arrays[7].shape[1] == 4 * width
    )
    return (fused if fits else on_device)(*arrays)


def solution(mesh):
    return jax.shard_map(
        choose,
        mesh=mesh,
        in_specs=(
            P("batch", "wide", None),
            P("batch", None),
            P("batch"),
            P(),
            P(),
            P(),
            P(),
            P(),
            P(),
            P("batch", "wide", None),
        ),
        out_specs=(
            P("batch", "wide", None),
            P("batch", "wide", None),
            P(),
            P(),
            P(),
            P(),
            P(),
            P(),
        ),
        check_vma=False,
    )
```

```python
import math
from functools import partial

import jax
import jax.numpy as jnp
from jax import lax
from jax.experimental import pallas as pl
from jax.experimental.pallas import tpu as pltpu
from jax.sharding import PartitionSpec as P

HEADS = 6
HEAD_DIM = 64


EPS = 1e-06


def norm_rows(values):
    center = values - jnp.mean(values, axis=-1, keepdims=True)
    inverse = lax.rsqrt(jnp.mean(center * center, axis=-1, keepdims=True) + EPS)
    return (center * inverse, inverse)


def norm_back(normed, inverse, gradient):
    return inverse * (
        gradient
        - jnp.mean(gradient, axis=-1, keepdims=True)
        - normed * jnp.mean(gradient * normed, axis=-1, keepdims=True)
    )


def to_heads(tokens, part_count, head_count, head_size):
    item_count, span_len, _ = tokens.shape
    shaped = tokens.reshape(item_count, span_len, part_count, head_count, head_size)
    return shaped.transpose(2, 0, 3, 1, 4).reshape(
        part_count, item_count * head_count, span_len * head_size
    )


def from_heads(blocks, item_count, head_count, head_size):
    part_count = blocks.shape[0]
    span_len = blocks.shape[2] // head_size
    shaped = blocks.reshape(part_count, item_count, head_count, span_len, head_size)
    return shaped.transpose(1, 3, 0, 2, 4).reshape(
        item_count, span_len, part_count * head_count * head_size
    )


def split_rows(values, block_rows):
    pair_count, slot_len = (values.shape[0], values.shape[1])
    rest = values.shape[2:]
    shaped = values.reshape((pair_count, slot_len // block_rows, block_rows) + rest)
    return jnp.moveaxis(shaped, 1, 0)


def join_rows(values):
    merged = jnp.moveaxis(values, 0, 1)
    return merged.reshape((merged.shape[0], merged.shape[1] * merged.shape[2]) + merged.shape[3:])


def masked_scores(query_block, keys_all, key_valid, inv_root):
    scores = (
        jnp.einsum("pqd,pkd->pqk", query_block, keys_all, preferred_element_type=jnp.float32)
        * inv_root
    )
    return jnp.where(key_valid[:, None, :], scores, -1e30)


def attend_forward(queries, keys_all, values, key_valid, inv_root):
    block_rows = min(512, queries.shape[1])

    def one_block(query_block):
        scores = masked_scores(query_block, keys_all, key_valid, inv_root)
        row_peak = jnp.max(scores, axis=-1, keepdims=True)
        exp_scores = jnp.exp(scores - row_peak)
        row_total = jnp.sum(exp_scores, axis=-1, keepdims=True)
        weights = (exp_scores / row_total).astype(jnp.bfloat16)
        outcome = jnp.einsum("pqk,pkd->pqd", weights, values, preferred_element_type=jnp.float32)
        return (outcome.astype(jnp.bfloat16), (row_peak + jnp.log(row_total))[..., 0])

    outputs, logsum = lax.map(one_block, split_rows(queries, block_rows))
    return (join_rows(outputs), join_rows(logsum))


def attend_backward(queries, keys_all, values, out_grad, logsum, key_valid, inv_root):
    block_rows = min(512, queries.shape[1])
    zeros = jnp.zeros(keys_all.shape, jnp.float32)

    def one_block(carried, packed):
        key_grad, value_grad = carried
        query_block, grad_block, logsum_block = packed
        scores = masked_scores(query_block, keys_all, key_valid, inv_root)
        weights = jnp.exp(scores - logsum_block[..., None])
        weight_grad = jnp.einsum(
            "pqd,pkd->pqk", grad_block, values, preferred_element_type=jnp.float32
        )
        score_grad = weights * (
            weight_grad - jnp.sum(weights * weight_grad, axis=-1, keepdims=True)
        )
        score_grad = score_grad.astype(jnp.bfloat16)
        query_grad = (
            jnp.einsum("pqk,pkd->pqd", score_grad, keys_all, preferred_element_type=jnp.float32)
            * inv_root
        )
        key_grad = (
            key_grad
            + jnp.einsum(
                "pqk,pqd->pkd", score_grad, query_block, preferred_element_type=jnp.float32
            )
            * inv_root
        )
        value_grad = value_grad + jnp.einsum(
            "pqk,pqd->pkd",
            weights.astype(jnp.bfloat16),
            grad_block,
            preferred_element_type=jnp.float32,
        )
        return ((key_grad, value_grad), query_grad)

    packed = (
        split_rows(queries, block_rows),
        split_rows(out_grad, block_rows),
        split_rows(logsum, block_rows),
    )
    (key_grad, value_grad), query_grads = lax.scan(one_block, (zeros, zeros), packed)
    return jnp.stack([join_rows(query_grads), key_grad, value_grad]).astype(jnp.bfloat16)


def on_device(block_in, lead_embed, lengths, w_ada, b_ada, w_qkv, w_proj, w_fc1, w_fc2, cotangent):
    item_count, span_len, width = block_in.shape
    head_count = HEADS
    head_size = HEAD_DIM
    shards = lax.axis_size("wide")
    pair_count = item_count * head_count // shards
    slot_len = span_len * shards
    inv_root = HEAD_DIM ** (-0.5)
    inputs = block_in.astype(jnp.float32)
    condition = jax.nn.silu(lead_embed.astype(jnp.float32)).astype(jnp.bfloat16)
    modulation = jnp.dot(condition, w_ada, preferred_element_type=jnp.float32) + b_ada.astype(
        jnp.float32
    )
    pieces = [modulation[:, None, column * width : (column + 1) * width] for column in range(6)]
    shift_att, scale_att, gate_att, shift_mlp, scale_mlp, gate_mlp = pieces
    normed, norm_inverse = norm_rows(inputs)
    entry = (normed * (1.0 + scale_att) + shift_att).astype(jnp.bfloat16)
    triple = jnp.dot(entry, w_qkv, preferred_element_type=jnp.float32).astype(jnp.bfloat16)
    arrived = lax.all_to_all(
        to_heads(triple, 3, head_count, head_size), "wide", split_axis=1, concat_axis=2, tiled=True
    )
    heads_in = arrived.reshape(3, pair_count, slot_len, head_size)
    pair_ids = lax.axis_index("wide") * pair_count + jnp.arange(pair_count, dtype=jnp.int32)
    item_ids = pair_ids // head_count
    pair_length = jnp.sum(
        jnp.where(
            jnp.arange(item_count, dtype=jnp.int32)[None, :] == item_ids[:, None],
            lengths[None, :],
            0,
        ),
        axis=1,
    )
    key_valid = jnp.arange(slot_len, dtype=jnp.int32)[None, :] < pair_length[:, None]
    mixed_heads, logsum = attend_forward(heads_in[0], heads_in[1], heads_in[2], key_valid, inv_root)
    returned = lax.all_to_all(
        mixed_heads.reshape(pair_count, slot_len * head_size),
        "wide",
        split_axis=1,
        concat_axis=0,
        tiled=True,
    )
    mixed_tok = from_heads(returned[None], item_count, head_count, head_size)
    branch = jnp.dot(mixed_tok, w_proj, preferred_element_type=jnp.float32)
    middle = inputs + gate_att * branch
    second_normed, second_inverse = norm_rows(middle)
    second = (second_normed * (1.0 + scale_mlp) + shift_mlp).astype(jnp.bfloat16)
    hidden = jnp.dot(second, w_fc1, preferred_element_type=jnp.float32)
    active = jax.nn.gelu(hidden, approximate=False).astype(jnp.bfloat16)
    mlp_out = jnp.dot(active, w_fc2, preferred_element_type=jnp.float32)
    block_out = middle + gate_mlp * mlp_out
    gradient = cotangent.astype(jnp.float32)
    mlp_grad = (gate_mlp * gradient).astype(jnp.bfloat16)
    gate_mlp_grad = jnp.sum(gradient * mlp_out, axis=1)
    fc2_grad = jnp.einsum("isf,isd->fd", active, mlp_grad, preferred_element_type=jnp.float32)
    active_grad = jnp.dot(mlp_grad, w_fc2.T, preferred_element_type=jnp.float32)
    hidden_grad = jax.vjp(partial(jax.nn.gelu, approximate=False), hidden)[1](active_grad)[0]
    hidden_grad = hidden_grad.astype(jnp.bfloat16)
    fc1_grad = jnp.einsum("isd,isf->df", second, hidden_grad, preferred_element_type=jnp.float32)
    second_grad = jnp.dot(hidden_grad, w_fc1.T, preferred_element_type=jnp.float32)
    scale_mlp_grad = jnp.sum(second_grad * second_normed, axis=1)
    shift_mlp_grad = jnp.sum(second_grad, axis=1)
    middle_grad = gradient + norm_back(
        second_normed, second_inverse, second_grad * (1.0 + scale_mlp)
    )
    branch_grad = (gate_att * middle_grad).astype(jnp.bfloat16)
    gate_att_grad = jnp.sum(middle_grad * branch, axis=1)
    proj_grad = jnp.einsum(
        "isd,ise->de", mixed_tok, branch_grad, preferred_element_type=jnp.float32
    )
    mixed_grad = jnp.dot(branch_grad, w_proj.T, preferred_element_type=jnp.float32).astype(
        jnp.bfloat16
    )
    heads_grad = lax.all_to_all(
        to_heads(mixed_grad, 1, head_count, head_size)[0],
        "wide",
        split_axis=0,
        concat_axis=1,
        tiled=True,
    )
    heads_grad = heads_grad.reshape(pair_count, slot_len, head_size)
    again_in, _ = lax.optimization_barrier((inputs, heads_grad))
    again_normed, _ = norm_rows(again_in)
    again_entry = (again_normed * (1.0 + scale_att) + shift_att).astype(jnp.bfloat16)
    again_triple = jnp.dot(again_entry, w_qkv, preferred_element_type=jnp.float32).astype(
        jnp.bfloat16
    )
    again_heads = lax.all_to_all(
        to_heads(again_triple, 3, head_count, head_size),
        "wide",
        split_axis=1,
        concat_axis=2,
        tiled=True,
    )
    used_heads = again_heads.reshape(3, pair_count, slot_len, head_size)
    triple_grad = attend_backward(
        used_heads[0], used_heads[1], used_heads[2], heads_grad, logsum, key_valid, inv_root
    )
    sent_back = lax.all_to_all(
        triple_grad.reshape(3, pair_count, slot_len * head_size),
        "wide",
        split_axis=2,
        concat_axis=1,
        tiled=True,
    )
    token_grad = from_heads(sent_back, item_count, head_count, head_size)
    qkv_grad = jnp.einsum("isd,ise->de", entry, token_grad, preferred_element_type=jnp.float32)
    entry_grad = jnp.dot(token_grad, w_qkv.T, preferred_element_type=jnp.float32)
    scale_att_grad = jnp.sum(entry_grad * normed, axis=1)
    shift_att_grad = jnp.sum(entry_grad, axis=1)
    input_grad = middle_grad + norm_back(normed, norm_inverse, entry_grad * (1.0 + scale_att))
    modulation_grad = jnp.concatenate(
        [
            shift_att_grad,
            scale_att_grad,
            gate_att_grad,
            shift_mlp_grad,
            scale_mlp_grad,
            gate_mlp_grad,
        ],
        axis=-1,
    )
    ada_grad = jnp.dot(
        condition.astype(jnp.float32).T, modulation_grad, precision=lax.Precision.HIGHEST
    )
    bias_grad = jnp.sum(modulation_grad, axis=0)
    totals = lax.psum(
        (ada_grad, bias_grad, qkv_grad, proj_grad, fc1_grad, fc2_grad), ("batch", "wide")
    )
    return (block_out, input_grad, totals[0], totals[1], totals[2], totals[3], totals[4], totals[5])


MESH = pl.DeviceIdType.MESH
MM = (((1,), (0,)), ((), ()))
NT = (((1,), (1,)), ((), ()))
TN = (((0,), (0,)), ((), ()))
B16 = jnp.bfloat16
F32 = jnp.float32

STREAMS = (
    (0, 0, 256, "zpqZ"),
    (0, 256, 128, "pqzZ"),
    (0, 384, 256, "pqzZ"),
    (0, 640, 128, "pzZq"),
    (1, 0, 256, "XW"),
    (1, 256, 256, "pqzZ"),
    (1, 512, 256, "zpqZ"),
    (2, 0, 256, "pqzZ*"),
    (2, 256, 128, "pzqZ"),
    (2, 384, 384, "pqzZ*"),
)
ORDER = (
    -1, -1, -1, -1, -1, -1, -1, -1, 0, 1, 2, 3, -1, -1, 4, 5, 6, -1, -1, -1,
    1, -1, -1, 0, 7, 8, 3, -1, 6, -1, 4, 1, 2, 9, 3, -1, 0, 5, 8, 6,
    1, 7, 4, 2, 3, -1, 0, 8, 5, 6, 1, 9, 7, 3, 8, 4, 2, -1, 0, 5,
    1, 9, 6, 7, 3, 8, 2, 0, 5, 9, 1, 3, 7, 4, 8, 6, 2, 0, 5, 4,
    1, 3, -1, 7, 9, 8, 1, 6, 3, 2, 5, 0, -1, 9, 0, 7, 8, 7, 8, 2,
    6, 5, 9, 2, 6, 5, 9,
)


def copies_in(dims):
    steps = dims.rstrip("*")
    back = len(steps) - (steps[-1] not in "XW") - (dims[-1] == "*")
    return len(steps) + back + 1


def dot(left, right, dims):
    return lax.dot_general(left, right, dims, preferred_element_type=F32)


def col_sum(values):
    return jnp.sum(values, axis=0, keepdims=True)


def fused_kernel(
    lengths_in,
    block_in,
    cotangent,
    lead_embed_in,
    b_ada_in,
    w_ada_in,
    w_qkv_in,
    w_proj_in,
    w_fc1_in,
    w_fc2_in,
    out_block,
    out_input,
    total,
    mod_all,
    lengths,
    lead_embed,
    b_ada,
    w_ada,
    w_qkv,
    w_proj,
    w_fc1,
    w_fc2,
    xall,
    gall,
    mod_rows,
    entry,
    normed_own,
    q_all,
    kv_all,
    bias_keys,
    probs,
    inverses,
    mixed,
    branch_ref,
    second_ref,
    active,
    gelu_slope,
    hidden_grad,
    mixed_grad,
    entry_t,
    second_t,
    mixed_t,
    keys_t,
    send_out,
    entry_send,
    entry_recv,
    qkvp,
    core_out,
    core_in,
    hold,
    stage,
    stage_in,
    mod_own,
    mod_in,
    load_sem,
    send_sem,
    x_recv,
    group_recv,
    c_recv,
    s_recv,
):
    items, span, width = block_in.shape
    own = items * span
    head_pairs = width // 128
    blocks = active.shape[0]
    half_rows = hold.shape[1]
    inv_root = HEAD_DIM**-0.5
    batch, wide = lax.axis_index("batch"), lax.axis_index("wide")
    z, core = wide // 2, wide % 2
    y, x = batch // 2, batch % 2
    zb = z % 2

    def at(y_, x_, z_, core_):
        return (y_ * 2 + x_, z_ * 2 + core_)

    core_peer = at(y, x, z, 1 - core)
    x_peer = at(y, 1 - x, z, core)
    y_peer = at(1 - y, x, z, core)
    xy_peer = at(1 - y, 1 - x, z, core)
    flip_x, flip_y = 1 - 2 * x, 1 - 2 * y
    peers = {
        "p": at(y + flip_y * core, x + flip_x * (1 - core), z, core),
        "q": at(y + flip_y * (1 - core), x + flip_x * core, z, core),
        "z": at(y, x, z + 1 - 2 * zb, core),
        "Z": at(y, x, (z + 2) % items, core),
    }
    sides = {
        "p": x * (1 - core) + y * core,
        "q": y * (1 - core) + x * core,
        "z": zb,
        "Z": z // 2,
    }

    sent_rows = {}

    def remote(src, dst, send, rows, recv, device):
        sent_rows[send] = sent_rows.get(send, 0) + rows
        copy = pltpu.make_async_remote_copy(
            src_ref=src,
            dst_ref=dst,
            send_sem=send_sem.at[send],
            recv_sem=recv,
            device_id=device,
            device_id_type=MESH,
        )
        copy.start()
        return copy

    def load(src, dst, index):
        copy = pltpu.make_async_copy(src, dst, load_sem.at[index])
        copy.start()
        return copy

    def wait_rows(sem, rows):
        planes = next(p for p in (1, 2, 3) if rows % (16 * p) == 0 and rows <= p * total.shape[1])
        area = total.at[pl.ds(0, planes), pl.ds(0, rows // planes)]
        pltpu.make_async_copy(area, area, sem).wait()

    barrier = pltpu.get_barrier_semaphore()
    greet = [at(y, x, (z + step) % items, core) for step in (2, 3, 1)]
    greet += [xy_peer, x_peer, y_peer, core_peer]
    for device in greet:
        pl.semaphore_signal(barrier, inc=1, device_id=device, device_id_type=MESH)
    loads = [
        load(block_in.at[z], xall.at[0, z], 0),
        load(w_ada_in, w_ada, 1),
        load(w_qkv_in, w_qkv, 2),
        load(w_proj_in, w_proj, 3),
        load(w_fc1_in, w_fc1, 4),
        load(w_fc2_in, w_fc2, 5),
        load(cotangent.at[z], gall.at[z], 6),
        load(lead_embed_in, lead_embed, 7),
        load(b_ada_in, b_ada, 8),
        load(lengths_in, lengths, 9),
    ]
    pl.semaphore_wait(barrier, len(greet))

    x_copies = []
    for step in range(1, items):
        there = (z + step) % items
        x_copies.append(
            remote(
                block_in.at[there],
                xall.at[0, z],
                0,
                span,
                x_recv.at[step - 1],
                at(y, x, there, core),
            )
        )
    remote(block_in.at[z], xall.at[1, z], 0, span, group_recv.at[0], core_peer)

    for index in (7, 8, 9):
        loads[index].wait()
    embed = lead_embed[...].astype(F32)
    condition = (embed / (1.0 + jnp.exp(-embed))).astype(B16)
    loads[1].wait()
    all_rows = dot(condition, w_ada[...], MM) + b_ada[...].astype(F32).reshape(1, -1)
    mine = lax.broadcasted_iota(jnp.int32, (items, 1), 0) == z
    mod_rows[...] = jnp.sum(jnp.where(mine, all_rows, 0.0), axis=0, keepdims=True)
    pieces = [mod_rows[:, column * width : (column + 1) * width] for column in range(6)]
    shift_att, scale_att, gate_att, shift_mlp, scale_mlp, gate_mlp = pieces
    mod_own[...] = jnp.zeros(mod_own.shape, F32)
    inverses[...] = jnp.zeros(inverses.shape, F32)
    mod_own[6:7, :] = jnp.sum(jnp.where(mine, condition.astype(F32), 0.0), axis=0, keepdims=True)

    lane = lax.broadcasted_iota(jnp.int32, (1, 128), 1)
    halves, marks = [], []
    row = lax.broadcasted_iota(jnp.int32, (2 * own, 128), 0)
    block_core = jnp.where(row // own == 0, core, 1 - core)
    position = ((row % own) // span * 2 + block_core) * span + row % span
    bias = jnp.where(position < lengths[z], 0.0, -1e30)
    for half in range(2):
        inside = lane // HEAD_DIM == half
        halves.append(jnp.where(inside, 1.0, 0.0).astype(B16))
        mark = jnp.where(lane == (1 - half) * HEAD_DIM, 1.0, 0.0)
        marks.append(mark.astype(B16))
        bias_keys[half] = (bias * mark).astype(B16)

    loads[0].wait()
    for step in range(1, items):
        came = (z + items - step) % items
        x_copies[step - 1].wait_recv()
        remote(
            xall.at[0, came],
            xall.at[1, came],
            0,
            span,
            group_recv.at[0],
            core_peer,
        )
    for step in range(1, items):
        there = (z + step) % items
        remote(
            cotangent.at[there],
            gall.at[z],
            0,
            span,
            group_recv.at[1],
            at(y, x, there, core),
        )

    loads[2].wait()
    inputs = xall[0].reshape(own, width).astype(F32)
    normed, norm_inverse = norm_rows(inputs)
    normed_own[...] = normed
    entry[:own, :] = (normed * (1.0 + scale_att) + shift_att).astype(B16)
    q_all[...] = (dot(entry[:own, :], w_qkv[:, :width], MM).astype(B16) * inv_root).astype(B16)
    kv_all[:own, :] = dot(entry[:own, :], w_qkv[:, width:], MM).astype(B16)
    wait_rows(group_recv.at[0], own)
    other_normed, _ = norm_rows(xall[1].reshape(own, width).astype(F32))
    entry[own:, :] = (other_normed * (1.0 + scale_att) + shift_att).astype(B16)
    kv_all[own:, :] = dot(entry[own:, :], w_qkv[:, width:], MM).astype(B16)

    def head_scores(head):
        pair, half = divmod(head, 2)
        lanes = slice(pair * 128, (pair + 1) * 128)
        return dot(
            kv_all[:, lanes] * halves[half] + bias_keys[half],
            q_all[:, lanes] * halves[half] + marks[half],
            NT,
        )

    scores, parts = head_scores(0), []
    for head in range(HEADS):
        pair, half = divmod(head, 2)
        following = head_scores(head + 1) if head + 1 < HEADS else None
        exp_scores = jnp.exp(scores - jnp.max(scores, axis=0, keepdims=True))
        inverse = 1.0 / jnp.sum(exp_scores, axis=0, keepdims=True)
        inverses[head : head + 1, :] = inverse
        weights = exp_scores.astype(B16)
        probs[head] = weights
        out = dot(kv_all[:, width + pair * 128 : width + (pair + 1) * 128], weights, TN)
        parts.append(out[half * HEAD_DIM : (half + 1) * HEAD_DIM] * inverse)
        if half == 1:
            mixed[:, pair * 128 : (pair + 1) * 128] = (
                jnp.concatenate(parts, axis=0).T.astype(B16)
            )
            parts = []
        scores = following

    loads[3].wait()
    branch = dot(mixed[...], w_proj[...], MM)
    middle = inputs + gate_att * branch
    branch_ref[...] = branch
    second_normed, second_inverse = norm_rows(middle)
    second_ref[...] = second_normed
    second = (second_normed * (1.0 + scale_mlp) + shift_mlp).astype(B16)
    loads[4].wait()
    loads[5].wait()
    mlp_out = jnp.zeros((own, width), F32)
    for block in range(blocks):
        columns = slice(block * width, (block + 1) * width)
        hidden = dot(second, w_fc1[:, columns], MM)
        cumulative = 0.5 * (1.0 + lax.erf(hidden * (0.5**0.5)))
        act = (hidden * cumulative).astype(B16)
        active[block] = act.T
        gelu_slope[block] = cumulative + hidden * (
            jnp.exp(-0.5 * hidden * hidden) * (1.0 / math.sqrt(2.0 * math.pi))
        )
        mlp_out = mlp_out + dot(act, w_fc2[columns, :], MM)

    entry_t[...] = entry[...].T
    second_t[...] = second.T
    mixed_t[...] = mixed[...].T
    keys_t[...] = kv_all[:, :width].T

    def give_back(out, which):
        for step in range(1, items):
            there = (z + step) % items
            remote(
                send_out.at[which, there],
                out.at[z],
                0,
                span,
                group_recv.at[2 + which],
                at(y, x, there, core),
            )
        out[z] = send_out[which, z]

    def rows_of(start, count):
        return pl.ds(pl.multiple_of(start, 16), count)

    first_slot = [sum(copies_in(what[3]) for what in STREAMS[:k]) for k in range(len(STREAMS))]
    core_copies = {}
    core_done = set()

    def core_start(wave, first, count):
        rows = pl.ds(first, count)
        core_copies[wave, first] = remote(
            core_out.at[wave, rows],
            core_in.at[wave, rows],
            1 + wave,
            count,
            c_recv.at[len(core_copies)],
            core_peer,
        )

    groups = {
        "X": (y * 2 + x, ((y * 2 + 1 - x, x_peer), (2 - y * 2 + x, y_peer), (3 - y * 2 - x, xy_peer))),
        "W": (
            z,
            tuple(
                ((z + step) % items, at(y, x, (z + step) % items, core)) for step in range(1, items)
            ),
        ),
    }

    def stream(index, wave, base, count, dims):
        keys = [first for kept_wave, first in core_copies if kept_wave == wave]
        for key in [first for first in keys if first < base + count]:
            if (wave, key) in core_done:
                continue
            core_done.add((wave, key))
            core_copies[wave, key].wait_recv()
        slot = first_slot[index]
        kept, size, place = base, count, base
        terms = [(core_in, base)]
        back = []

        def summed(offset, rows):
            values = hold[wave, rows_of(kept + offset, rows), :]
            for array, at_row in terms:
                values = values + array[wave, rows_of(at_row + offset, rows), :].astype(F32)
            return values

        def send(area, device):
            return remote(
                stage.at[wave, area],
                stage_in.at[wave, area],
                4 + index,
                area.size,
                s_recv.at[slot],
                device,
            )

        result = None
        steps = dims.rstrip("*")
        for number, dim in enumerate(steps):
            last = number == len(steps) - 1
            if dim in groups:
                side, others = groups[dim]
                size //= 4
                for other_number, (other, device) in reversed(list(enumerate(others))):
                    area = pl.ds(place + other_number * size, size)
                    stage[wave, area, :] = summed(other * size, size).astype(B16)
                    send(area, device)
                kept = kept + side * size
                back.append((dim, kept, size))
                terms = [(array, at_row + side * size) for array, at_row in terms]
                terms += [(stage_in, place + other_number * size) for other_number in range(3)]
                place = place + 3 * size
            elif not last:
                size //= 2
                away, keep = (1 - sides[dim]) * size, sides[dim] * size
                area = pl.ds(place, size)
                stage[wave, area, :] = summed(away, size).astype(B16)
                send(area, peers[dim])
                kept = kept + keep
                back.append((dim, kept, size))
                terms = [(array, at_row + keep) for array, at_row in terms] + [(stage_in, place)]
                place = place + size
            else:
                area = pl.ds(place, size)
                stage[wave, area, :] = summed(0, size).astype(B16)
                send(area, peers[dim])
                result = area
            yield
            wait_rows(s_recv.at[slot], 3 * size if dim in groups else size)
            slot += 1
        if result is None:
            values = summed(0, size)
        else:
            values = stage[wave, result, :].astype(F32) + stage_in[wave, result, :].astype(F32)
        total[wave, rows_of(core * half_rows + kept, size), :] = values.astype(B16)

        back.reverse()
        while back:
            dim, start, size = back.pop(0)
            if dims.endswith("*") and dim in "pq" and back and back[0][0] in "pq":
                back.pop(0)
                dim = "X"
            area = total.at[wave, rows_of(core * half_rows + start, size)]
            devices = [device for _, device in reversed(groups[dim][1])] if dim in groups else [peers[dim]]
            for device in devices:
                remote(area, area, 4 + index, size, s_recv.at[slot], device)
            yield
            wait_rows(s_recv.at[slot], len(devices) * size)
            slot += 1
        area = total.at[wave, rows_of(core * half_rows + base, count)]
        copy = remote(area, area, 4 + index, count, s_recv.at[slot], core_peer)
        yield
        copy.wait_recv()

    def compute():
        per_core = blocks // 2
        block_result = middle + gate_mlp * mlp_out
        send_out[0] = block_result.astype(B16).reshape(items, span, width)
        loads[6].wait()
        wait_rows(group_recv.at[1], own - span)
        gradient = gall[...].reshape(own, width).astype(F32)
        mlp_grad = (gate_mlp * gradient).astype(B16)
        for index in range(per_core):
            block = (1 - core) * per_core + index
            rows = slice(index * width, (index + 1) * width)
            core_out[0, rows, :] = dot(active[block], mlp_grad, MM).astype(B16)
        core_start(0, 0, half_rows)
        yield
        for index in range(per_core):
            block = core * per_core + index
            rows = slice(index * width, (index + 1) * width)
            hold[0, rows, :] = dot(active[block], mlp_grad, MM)
        yield
        second_grad = jnp.zeros((own, width), F32)
        for block in range(blocks):
            columns = slice(block * width, (block + 1) * width)
            active_grad = dot(mlp_grad, w_fc2[columns, :], NT)
            hid = (active_grad * gelu_slope[block]).astype(B16)
            hidden_grad[block] = hid
            second_grad = second_grad + dot(hid, w_fc1[:, columns], NT)
            yield
        for index in range(per_core):
            block = (1 - core) * per_core + index
            rows = slice(index * width, (index + 1) * width)
            core_out[1, rows, :] = dot(second_t[...], hidden_grad[block], MM).astype(B16)
        core_start(1, 0, half_rows)
        yield
        for index in range(per_core):
            block = core * per_core + index
            rows = slice(index * width, (index + 1) * width)
            hold[1, rows, :] = dot(second_t[...], hidden_grad[block], MM)
        yield
        second_normed = second_ref[...]
        middle_grad = gradient + norm_back(
            second_normed, second_inverse, second_grad * (1.0 + scale_mlp)
        )
        branch_grad = (gate_att * middle_grad).astype(B16)
        mixed_grad[...] = dot(branch_grad, w_proj[...], NT).astype(B16)
        qkvp[3] = dot(mixed_t[...], branch_grad, MM)
        yield
        mod_own[5:6, :] = col_sum(gradient * mlp_out)
        mod_own[4:5, :] = col_sum(second_grad * second_normed)
        mod_own[3:4, :] = col_sum(second_grad)
        mod_own[2:3, :] = col_sum(middle_grad * branch_ref[...])
        yield

        dq, dkv = q_all, kv_all
        inverse_columns = inverses[...].T
        for pair in range(head_pairs):
            lanes = slice(pair * 128, (pair + 1) * 128)
            v_lanes = slice(width + pair * 128, width + (pair + 1) * 128)
            values, queries = kv_all[:, v_lanes], q_all[:, lanes]
            out_grad = mixed_grad[:, lanes].astype(F32)
            parts = []
            key_grad = jnp.zeros((2 * own, 128), F32)
            value_grad = jnp.zeros((2 * own, 128), F32)
            for half in range(2):
                head = pair * 2 + half
                masked_grad = (
                    out_grad * inverse_columns[:, head : head + 1] * halves[half].astype(F32)
                ).astype(B16)
                weights = probs[head]
                wide_weights = weights.astype(F32)
                weight_grad = dot(values, masked_grad, NT)
                row_sum = col_sum(wide_weights * weight_grad) * inverses[head : head + 1, :]
                score_grad = (wide_weights * (weight_grad - row_sum)).astype(B16)
                value_grad = value_grad + dot(weights, masked_grad, MM)
                key_grad = key_grad + dot(score_grad, queries * halves[half], MM)
                query_grad = dot(keys_t[lanes, :], score_grad, MM)
                parts.append(query_grad[half * HEAD_DIM : (half + 1) * HEAD_DIM])
                if half == 0:
                    yield
            query_grad = jnp.concatenate(parts, axis=0).T * inv_root
            dq[:, lanes] = query_grad.astype(B16)
            dkv[:, lanes] = key_grad.astype(B16)
            dkv[:, v_lanes] = value_grad.astype(B16)
            qkvp[pair, :, :128] = dot(entry_t[:, :own], dq[:, lanes], MM)
            pair_grads = jnp.concatenate([key_grad, value_grad], axis=1).astype(B16)
            qkvp[pair, :, 128:] = dot(entry_t[...], pair_grads, MM)
            if pair == 0:
                core_out[2, :width, :] = qkvp[3 * (1 - core)].astype(B16)
                core_start(2, 0, width)
                hold[2, :width, :] = qkvp[3 * core]
            elif pair == 2:
                core_out[2, width:, :] = qkvp[2 - core].astype(B16)
                core_start(2, width, width)
                hold[2, width:, :] = qkvp[1 + core]
            yield

        entry_send[...] = dot(dkv[own:, :], w_qkv[:, width:], NT)
        entry_copy = remote(entry_send, entry_recv, 0, 2 * own, group_recv.at[4], core_peer)
        entry_grad = dot(dkv[:own, :], w_qkv[:, width:], NT) + dot(dq[...], w_qkv[:, :width], NT)
        yield
        entry_copy.wait_recv()
        entry_grad = entry_grad + entry_recv[...]
        normed = normed_own[...]
        mod_own[1:2, :] = col_sum(entry_grad * normed)
        mod_own[0:1, :] = col_sum(entry_grad)
        mod_copy = remote(mod_own, mod_in, 0, 16, group_recv.at[5], core_peer)
        input_grad = middle_grad + norm_back(
            normed, norm_inverse, entry_grad * (1.0 + scale_att)
        )
        send_out[1] = input_grad.astype(B16).reshape(items, span, width)
        yield
        mod_copy.wait_recv()
        first_row = batch * items
        weight = jnp.where(lax.broadcasted_iota(jnp.int32, mod_own.shape, 0) == 6, 0.5, 1.0)
        mod_all[first_row + z] = (mod_own[...] + mod_in[...]) * weight
        for step in range(1, items):
            place = mod_all.at[first_row + z]
            there = at(y, x, (z + step) % items, core)
            remote(place, place, 0, 16, group_recv.at[6], there)
        yield
        wait_rows(group_recv.at[6], 16 * (items - 1))
        for device in (x_peer, y_peer, xy_peer):
            place = mod_all.at[pl.ds(first_row, items)]
            remote(place, place, 0, 16 * items, group_recv.at[7], device)
        yield
        wait_rows(group_recv.at[7], 3 * 16 * items)
        yield
        give_back(out_block, 0)
        give_back(out_input, 1)

    steps = compute()
    streams = [stream(index, *what) for index, what in enumerate(STREAMS)]
    for step in ORDER:
        next(steps if step < 0 else streams[step], None)
    for rest in [steps] + streams:
        for _ in rest:
            raise AssertionError

    for which in range(2):
        wait_rows(group_recv.at[2 + which], own - span)
    for index, rows in sent_rows.items():
        wait_rows(send_sem.at[index], rows)


def widen_kernel(
    block_16,
    input_16,
    total,
    mod,
    block_out,
    input_out,
    ada_out,
    bias_out,
    qkv_out,
    proj_out,
    fc1_out,
    fc2_out,
    block_32,
    input_32,
    ada_32,
    bias_32,
    qkv_32,
    proj_32,
    fc1_32,
    fc2_32,
    by_piece,
    sem,
):
    count, _, width = mod.shape
    blocks = fc2_32.shape[0] // width
    stores = []

    def store(src, dst):
        copy = pltpu.make_async_copy(src, dst, sem.at[len(stores)])
        copy.start()
        stores.append(copy)

    def part(index):
        return pl.ds(index * width, width)

    for block in range(blocks):
        fc2_32[part(block), :] = total[0, part(block), :].astype(F32)
        store(fc2_32.at[part(block), :], fc2_out.at[part(block), :])
    for piece in range(7):
        for item in range(count):
            by_piece[piece, item : item + 1, :] = mod[item, piece : piece + 1, :]
    conditions = jnp.concatenate([by_piece[6].astype(B16)] * 3, axis=0)
    for piece in range(6):
        columns = slice(piece * width, (piece + 1) * width)
        rows = by_piece[piece]
        bias_32[columns] = jnp.sum(rows, axis=0)
        high = rows.astype(B16)
        rest = rows - high.astype(F32)
        middle = rest.astype(B16)
        low = (rest - middle.astype(F32)).astype(B16)
        parts = jnp.concatenate([high, middle, low], axis=0)
        ada_32[:, columns] = dot(conditions, parts, TN)
        store(ada_32.at[:, part(piece)], ada_out.at[:, part(piece)])
    store(bias_32, bias_out)
    for block in range(blocks):
        columns = slice(block * width, (block + 1) * width)
        fc1_32[:, columns] = total[1, part(block), :].astype(F32)
        store(fc1_32.at[:, part(block)], fc1_out.at[:, part(block)])
    proj_32[...] = total[2, part(2), :].astype(F32)
    store(proj_32, proj_out)
    for pair, block in enumerate((0, 1, 3)):
        for piece in range(3):
            start = piece * width + pair * 128
            qkv_32[:, start : start + 128] = total[
                2, part(block), piece * 128 : (piece + 1) * 128
            ].astype(F32)
    store(qkv_32, qkv_out)
    block_32[...] = block_16[...].astype(F32)
    store(block_32, block_out)
    input_32[...] = input_16[...].astype(F32)
    store(input_32, input_out)
    for copy in stores:
        copy.wait()


def widen(out_block, out_input, total, mod):
    waves, hidden, width = total.shape
    shapes = (
        out_block.shape,
        out_input.shape,
        (width, 6 * width),
        (6 * width,),
        (width, 3 * width),
        (width, width),
        (width, hidden),
        (hidden, width),
    )
    return pl.pallas_call(
        widen_kernel,
        out_shape=tuple(jax.ShapeDtypeStruct(shape, F32) for shape in shapes),
        in_specs=[pl.BlockSpec(memory_space=pltpu.VMEM)] * 4,
        out_specs=(pl.BlockSpec(memory_space=pl.ANY),) * 8,
        scratch_shapes=[pltpu.VMEM(shape, F32) for shape in shapes]
        + [
            pltpu.VMEM((7, mod.shape[0], width), F32),
            pltpu.SemaphoreType.DMA((11 + 2 * (hidden // width),)),
        ],
        name="widen",
        compiler_params=pltpu.CompilerParams(vmem_limit_bytes=30 * 2**20),
    )(out_block, out_input, total, mod)


def fused(block_in, lead_embed, lengths, w_ada, b_ada, w_qkv, w_proj, w_fc1, w_fc2, cotangent):
    items, span, width = block_in.shape
    hidden = w_fc1.shape[1]
    groups = lax.axis_size("batch")
    own = items * span
    blocks = hidden // width
    half = hidden // 2
    waves = 3
    hbm = pl.BlockSpec(memory_space=pl.ANY)
    dma = pltpu.SemaphoreType.DMA
    scratch = [
        pltpu.SMEM(lengths.shape, jnp.int32),
        pltpu.VMEM(lead_embed.shape, B16),
        pltpu.VMEM(b_ada.shape, B16),
        pltpu.VMEM(w_ada.shape, B16),
        pltpu.VMEM(w_qkv.shape, B16),
        pltpu.VMEM(w_proj.shape, B16),
        pltpu.VMEM(w_fc1.shape, B16),
        pltpu.VMEM(w_fc2.shape, B16),
        pltpu.VMEM((2, items, span, width), B16),
        pltpu.VMEM((items, span, width), B16),
        pltpu.VMEM((1, 6 * width), F32),
        pltpu.VMEM((2 * own, width), B16),
        pltpu.VMEM((own, width), F32),
        pltpu.VMEM((own, width), B16),
        pltpu.VMEM((2 * own, 2 * width), B16),
        pltpu.VMEM((2, 2 * own, 128), B16),
        pltpu.VMEM((HEADS, 2 * own, own), B16),
        pltpu.VMEM((8, own), F32),
        pltpu.VMEM((own, width), B16),
        pltpu.VMEM((own, width), F32),
        pltpu.VMEM((own, width), F32),
        pltpu.VMEM((blocks, width, own), B16),
        pltpu.VMEM((blocks, own, width), F32),
        pltpu.VMEM((blocks, own, width), B16),
        pltpu.VMEM((own, width), B16),
        pltpu.VMEM((width, 2 * own), B16),
        pltpu.VMEM((width, own), B16),
        pltpu.VMEM((width, own), B16),
        pltpu.VMEM((width, 2 * own), B16),
        pltpu.VMEM((2, items, span, width), B16),
        pltpu.VMEM((own, width), F32),
        pltpu.VMEM((own, width), F32),
        pltpu.VMEM((blocks, width, width), F32),
        pltpu.VMEM((waves, half, width), B16),
        pltpu.VMEM((waves, half, width), B16),
        pltpu.VMEM((waves, half, width), F32),
        pltpu.VMEM((waves, half, width), B16),
        pltpu.VMEM((waves, half, width), B16),
        pltpu.VMEM((8, width), F32),
        pltpu.VMEM((8, width), F32),
        dma((10,)),
        dma((4 + len(STREAMS),)),
        dma((items - 1,)),
        dma((8,)),
        dma((4,)),
        dma((sum(copies_in(what[3]) for what in STREAMS),)),
    ]
    results = pl.pallas_call(
        fused_kernel,
        out_shape=(
            pltpu.VMEM(block_in.shape, B16),
            pltpu.VMEM(block_in.shape, B16),
            pltpu.VMEM((waves, hidden, width), B16),
            pltpu.VMEM((groups * items, 8, width), F32),
        ),
        in_specs=[hbm] * 10,
        out_specs=(pl.BlockSpec(memory_space=pltpu.VMEM),) * 4,
        scratch_shapes=scratch,
        name="fused_block",
        compiler_params=pltpu.CompilerParams(
            collective_id=0, has_side_effects=True, vmem_limit_bytes=58 * 2**20
        ),
    )(
        lengths,
        block_in,
        cotangent,
        lead_embed,
        b_ada,
        w_ada,
        w_qkv,
        w_proj,
        w_fc1,
        w_fc2,
    )
    return widen(*results)


def choose(*arrays):
    items, span, width = arrays[0].shape
    fits = (
        lax.axis_size("batch") == 4
        and items == 4
        and lax.axis_size("wide") == 2 * items
        and span == 64
        and width == HEADS * HEAD_DIM == 384
        and arrays[7].shape[1] == 4 * width
    )
    return (fused if fits else on_device)(*arrays)


def solution(mesh):
    return jax.shard_map(
        choose,
        mesh=mesh,
        in_specs=(
            P("batch", "wide", None),
            P("batch", None),
            P("batch"),
            P(),
            P(),
            P(),
            P(),
            P(),
            P(),
            P("batch", "wide", None),
        ),
        out_specs=(
            P("batch", "wide", None),
            P("batch", "wide", None),
            P(),
            P(),
            P(),
            P(),
            P(),
            P(),
        ),
        check_vma=False,
    )
```
